128 devices in a mesh: tm: 8 (over x, z_hi), clip: 16 (over z_lo, y, core).
Axes of the slice: x: 4, y: 4, z: 4 (z_hi: 2, z_lo: 2; z = z_hi * 2 + z_lo), core: 2. Of those that a mesh axis runs over, the one named last changes fastest.
Arguments:
- frame_tokens: bfloat16 [64, 8, 256, 512], P('clip', 'tm'), may hold values from -6 to 6
- actions: int32 [64, 8], P('clip', 'tm'), may hold values from 0 to 7
- frame_counts: int32 [64], P('clip'), may hold values from 2 to 8, as said below
- action_table: bfloat16 [8, 512], replicated, may hold values from -6 to 6
- ln_gain: float32 [3, 512], replicated, may hold values from 0.5 to 1.5
- ln_bias: float32 [3, 512], replicated, may hold values from -1.2 to 1.2
- w_sqkv: bfloat16 [512, 1536], replicated, may hold values from -0.25 to 0.25
- w_so: bfloat16 [512, 512], replicated, may hold values from -2 to 2
- w_tqkv: bfloat16 [512, 1536], replicated, may hold values from -0.25 to 0.25
- w_to: bfloat16 [512, 512], replicated, may hold values from -0.375 to 0.375
- w_up: bfloat16 [512, 2048], replicated, may hold values from -0.25 to 0.25
- b_up: float32 [2048], replicated, may hold values from -3 to 3
- w_down: bfloat16 [2048, 512], replicated, may hold values from -0.125 to 0.125
- cotangent: bfloat16 [64, 8, 256, 512], P('clip', 'tm'), may hold values from -6 to 6
Outputs:
- block_out: bfloat16 [64, 8, 256, 512], P('clip', 'tm')
- grad_input: float32 [64, 8, 256, 512], P('clip', 'tm')
- grad_table: float32 [8, 512], replicated
- grad_gain: float32 [3, 512], replicated
- grad_bias: float32 [3, 512], replicated
- grad_sqkv: float32 [512, 1536], replicated
- grad_so: float32 [512, 512], replicated
- grad_tqkv: float32 [512, 1536], replicated
- grad_to: float32 [512, 512], replicated
- grad_up: float32 [512, 2048], replicated
- up_bias_gradient: float32 [2048], replicated
- grad_down: float32 [2048, 512], replicated
The draws below stay inside these ranges and needn't reach their ends.
Inputs may be any that keep to these rules, and one draw needn't show every extreme that they name: `frame_counts`: frames present in a clip come first in it; in each aligned block of 4 clips one clip holds all 8 frames.
All inputs are finite; a program needn't handle non-finite values.
Results may differ from the reference program's by a relative error of at most 0.014.
Values may be sent and summed in bfloat16 or wider, within the bound.
No kernel may reach another device: no remote copies, remote signals or barrier semaphores. Data moves between devices by JAX's collectives and lax.ppermute only.
A program may use at most 256 MiB of HBM per device.

```python
import math
import jax
import jax.numpy as jnp
from jax import lax

D = 512
HEADS = 8
FF = 2048
ACTIONS = 8
PATCH = 256
CLIPS_DEV = 4
FRAMES = 8
CLIPS = 64


def draw_frame_counts(key, part):
    base_counts = jax.random.randint(key, (CLIPS,), 2, FRAMES + 1)
    groups = CLIPS // CLIPS_DEV
    chosen = jax.random.randint(jax.random.fold_in(key, 7), (groups,), 0, CLIPS_DEV)
    positions = jnp.arange(CLIPS, dtype=jnp.int32)
    is_full = positions % CLIPS_DEV == jnp.repeat(chosen, CLIPS_DEV)
    return jnp.where(is_full, FRAMES, base_counts).astype(jnp.int32)


def set_ends(array, rng, least, largest):
    place = [jax.random.randint(jax.random.fold_in(rng, axis), (), 0, length) for axis, length in enumerate(array.shape)]
    main_axis = array.shape.index(max(array.shape))
    neighbour = place[:main_axis] + [(place[main_axis] + 1) % array.shape[main_axis]] + place[main_axis + 1:]
    return array.at[tuple(place)].set(least).at[tuple(neighbour)].set(largest)


def block_scale(rng, shape, split, least, high):
    def one(axis_at, parts):
        heights = jax.random.uniform(jax.random.fold_in(jax.random.fold_in(rng, 6), axis_at), (parts,), jnp.float32, least / len(split), high / len(split))
        return jnp.repeat(jnp.exp(heights), shape[axis_at] // parts).reshape((-1,) + (1,) * (len(shape) - axis_at - 1))

    factor_of = one(*split[0])
    for cut in split[1:]:
        factor_of = factor_of * one(*cut)
    return factor_of


def normal_values(own_key, dims, deviation, limit, pieces=(), kind=jnp.bfloat16):
    drawn = jax.random.normal(own_key, dims, jnp.float32) * deviation
    if len(pieces) > 0:
        drawn = block_scale(own_key, dims, pieces, -0.22, 0.18) * drawn
    return jnp.clip(drawn, min=-limit, max=limit).astype(kind)


def setup_inputs(seed: int = 0) -> dict:
    splits = jax.random.split(jax.random.key(seed), 15)
    frame_tokens = normal_values(splits[0], (CLIPS, FRAMES, PATCH, D), 1.0, 6.0, ((0, 16), (1, 8)))
    actions = set_ends(jax.random.randint(splits[1], (CLIPS, FRAMES), 0, ACTIONS), jax.random.fold_in(splits[1], 1), 0, ACTIONS - 1).astype(jnp.int32)
    frame_counts = draw_frame_counts(jax.random.fold_in(splits[14], 71), 0)
    action_table = normal_values(splits[3], (ACTIONS, D), 1.0, 6.0)
    ln_gain = jnp.clip(1.0 + 0.1 * jax.random.normal(splits[4], (3, D), jnp.float32), 0.5, 1.5)
    ln_bias = normal_values(splits[5], (3, D), 0.2, 1.2, (), jnp.float32)
    w_sqkv = normal_values(splits[6], (D, 3 * D), D ** -0.5, 0.25)
    w_so = normal_values(splits[7], (D, D), (4 * D // PATCH) ** -0.5, 2.0)
    w_tqkv = normal_values(splits[8], (D, 3 * D), D ** -0.5, 0.25)
    w_to = normal_values(splits[9], (D, D), (D // 2) ** -0.5, 0.375)
    w_up = normal_values(splits[10], (D, FF), D ** -0.5, 0.25)
    b_up = normal_values(splits[11], (FF,), 0.5, 3.0, (), jnp.float32)
    w_down = normal_values(splits[12], (FF, D), FF ** -0.5, 0.125)
    cotangent = normal_values(splits[13], (CLIPS, FRAMES, PATCH, D), 1.0, 6.0, ((0, 16), (1, 8)))
    return {"frame_tokens": frame_tokens, "actions": actions, "frame_counts": frame_counts, "action_table": action_table, "ln_gain": ln_gain, "ln_bias": ln_bias, "w_sqkv": w_sqkv, "w_so": w_so, "w_tqkv": w_tqkv, "w_to": w_to, "w_up": w_up, "b_up": b_up, "w_down": w_down, "cotangent": cotangent}


highest = lax.Precision.HIGHEST
eps_norm = 1e-05
big_negative = -1e+30

@jax.custom_vjp
def low(v):
    return lax.optimization_barrier(v.astype(jnp.bfloat16)).astype(jnp.float32)

@jax.custom_vjp
def low_back(v):
    return v

def low_keep(v):
    return (low(v), None)

def low_pass(kept, grad):
    return (grad,)

def back_keep(v):
    return (v, None)

def back_low(kept, grad):
    return (low(grad),)
low.defvjp(low_keep, low_pass)
low_back.defvjp(back_keep, back_low)

def layer_norm(values, gain_row, shift_row):
    center = values - lax.optimization_barrier(jnp.mean(values, axis=-1, keepdims=True))
    spread = lax.optimization_barrier(jnp.mean(center * center, axis=-1, keepdims=True))
    return center * lax.rsqrt(spread + eps_norm) * gain_row + shift_row

def project(values, weight):
    return jnp.einsum('fpd,de->fpe', values, weight, precision=highest)

def clip_block(params, clip_tokens, clip_actions, clip_count):
    emb_table, gain_rows, shift_rows, w_sqkv, w_so, w_tqkv, w_to, w_up, b_up, w_down = params
    head_dim = D // HEADS
    score_scale = 1.0 / math.sqrt(head_dim)
    onehot = (clip_actions[:, None] == jnp.arange(ACTIONS, dtype=jnp.int32)[None, :]).astype(jnp.float32)
    first_state = clip_tokens + jnp.dot(onehot, emb_table, precision=highest)[:, None, :]
    act_one = low(layer_norm(first_state, gain_rows[0], shift_rows[0]))
    s_qkv = low_back(low(project(act_one, w_sqkv))).reshape(FRAMES, PATCH, 3, HEADS, head_dim)
    s_query, s_key, s_value = (s_qkv[:, :, 0], s_qkv[:, :, 1], s_qkv[:, :, 2])
    s_scores = low_back(jnp.einsum('fphd,fqhd->fhpq', s_query, s_key, precision=highest) * score_scale)
    s_probs = low(jax.nn.softmax(s_scores, axis=-1))
    s_out = low_back(low(jnp.einsum('fhpq,fqhd->fphd', s_probs, s_value, precision=highest).reshape(FRAMES, PATCH, D)))
    mid_state = first_state + low_back(project(s_out, w_so))
    act_two = low(layer_norm(mid_state, gain_rows[1], shift_rows[1]))
    t_qkv = low_back(low(project(act_two, w_tqkv))).reshape(FRAMES, PATCH, 3, HEADS, head_dim)
    t_query, t_key, t_value = (t_qkv[:, :, 0], t_qkv[:, :, 1], t_qkv[:, :, 2])
    t_scores = low_back(jnp.einsum('fphd,ephd->phfe', t_query, t_key, precision=highest) * score_scale)
    frame_ids = jnp.arange(FRAMES, dtype=jnp.int32)
    allowed = (frame_ids[None, :] < clip_count) & (frame_ids[None, :] <= frame_ids[:, None])
    t_scores = jnp.where(allowed[None, None], t_scores, big_negative)
    t_probs = low(jax.nn.softmax(t_scores, axis=-1))
    t_out = low_back(low(jnp.einsum('phfe,ephd->fphd', t_probs, t_value, precision=highest).reshape(FRAMES, PATCH, D)))
    late_state = mid_state + low_back(project(t_out, w_to))
    act_three = low(layer_norm(late_state, gain_rows[2], shift_rows[2]))
    pre_act = low_back(project(act_three, w_up) + b_up)
    hidden = low(jax.nn.gelu(pre_act))
    return late_state + low_back(project(hidden, w_down))

def reference(frame_tokens, actions, frame_counts, action_table, ln_gain, ln_bias, w_sqkv, w_so, w_tqkv, w_to, w_up, b_up, w_down, cotangent):
    params = (action_table.astype(jnp.float32), ln_gain.astype(jnp.float32), ln_bias.astype(jnp.float32), w_sqkv.astype(jnp.float32), w_so.astype(jnp.float32), w_tqkv.astype(jnp.float32), w_to.astype(jnp.float32), w_up.astype(jnp.float32), b_up.astype(jnp.float32), w_down.astype(jnp.float32))
    tokens_float = frame_tokens.astype(jnp.float32)
    block_function = jax.checkpoint(clip_block)

    def forward(inputs, weights):

        def step(carry, item):
            return (carry, block_function(weights, item[0], item[1], item[2]))
        _, outputs = lax.scan(step, jnp.zeros((), jnp.float32), (inputs, actions, frame_counts))
        return outputs
    result, pull = jax.vjp(forward, tokens_float, params)
    frame_ids = jnp.arange(FRAMES, dtype=jnp.int32)
    frame_mask = (frame_ids[None, :] < frame_counts[:, None]).astype(jnp.float32)
    grad_input, grads = pull(cotangent.astype(jnp.float32) * frame_mask[:, :, None, None])
    return (result.astype(jnp.bfloat16), grad_input, grads[0], grads[1], grads[2], grads[3], grads[4], grads[5], grads[6], grads[7], grads[8], grads[9])
```

```python
import math

import jax
import jax.numpy as jnp
from jax import lax
from jax.sharding import Mesh, PartitionSpec as P

HEADS = 8
EPS = 1e-05
NEG = -1e30
BF = jnp.bfloat16
F32 = jnp.float32
FRAME_AXES = ("x", "zh")
CHIP_AXES = ("x", "zh", "zl", "y")


def layer_norm(values, gain_row, shift_row):
    center = values - jnp.mean(values, axis=-1, keepdims=True)
    spread = jnp.mean(center * center, axis=-1, keepdims=True)
    return center * lax.rsqrt(spread + EPS) * gain_row + shift_row


def norm_back(values, gain_row, shift_row, upstream):
    _, pull = jax.vjp(layer_norm, values, gain_row, shift_row)
    return pull(upstream)


def mul(a, b):
    return jnp.dot(a, b, preferred_element_type=F32)


def mul_t(a, b):
    return lax.dot_general(a, b, (((a.ndim - 1,), (1,)), ((), ())), preferred_element_type=F32)


def wgrad(a, b):
    a = a.reshape(-1, a.shape[-1])
    b = b.reshape(-1, b.shape[-1])
    return lax.dot_general(a, b, (((0,), (0,)), ((), ())), preferred_element_type=F32)


def to_positions(v):
    clips, patch, width = v.shape
    n = lax.axis_size(FRAME_AXES)
    v = v.reshape(clips, n, patch // n, width).transpose(1, 0, 2, 3)
    return lax.all_to_all(v, FRAME_AXES, 0, 0)


def to_frames(v):
    n, clips, part, width = v.shape
    v = lax.all_to_all(v, FRAME_AXES, 0, 0)
    return v.transpose(1, 0, 2, 3).reshape(clips, n * part, width)


def swap_cores(v):
    return lax.ppermute(v, "c", [(0, 1), (1, 0)])


def reduce_rows(v):
    rows, width = v.shape
    core = lax.axis_index("c")
    chips = lax.axis_size(CHIP_AXES)
    halves = v.reshape(2, rows // 2, width)
    mine = lax.dynamic_index_in_dim(halves, core, 0, keepdims=False)
    other = lax.dynamic_index_in_dim(halves, 1 - core, 0, keepdims=False)
    got = swap_cores(other.astype(BF))
    half = (mine.astype(F32) + got.astype(F32)).astype(BF)
    parts = lax.all_to_all(half.reshape(chips, -1, width), CHIP_AXES, 0, 0)
    part = jnp.sum(parts.astype(F32), axis=0).astype(BF)
    whole = lax.all_to_all(jnp.broadcast_to(part[None], (chips, *part.shape)), CHIP_AXES, 0, 0)
    whole = whole.reshape(rows // 2, width)
    peer = swap_cores(whole)
    first = jnp.where(core == 0, whole, peer)
    second = jnp.where(core == 0, peer, whole)
    return jnp.concatenate([first, second], axis=0)


def shards(
    frame_tokens, actions, frame_counts, action_table, ln_gain, ln_bias, w_sqkv, w_so, w_tqkv, w_to,
    w_up, b_up, w_down, cotangent,
):
    clips, _, patch, width = frame_tokens.shape
    heads = HEADS
    dim = width // heads
    scale = 1.0 / math.sqrt(dim)
    cot = to_positions(cotangent[:, 0])
    frames, _, part, _ = cot.shape
    onehot = (actions[:, 0, None] == jnp.arange(action_table.shape[0], dtype=jnp.int32)).astype(F32)
    embedded = jnp.dot(onehot, action_table.astype(F32), precision=lax.Precision.HIGHEST)
    first_state = frame_tokens[:, 0].astype(F32) + embedded[:, None, :]
    act_one = layer_norm(first_state, ln_gain[0], ln_bias[0]).astype(BF)
    s_qkv = mul(act_one, w_sqkv).astype(BF).reshape(clips, patch, 3, heads, dim)
    s_query, s_key, s_value = s_qkv[:, :, 0], s_qkv[:, :, 1], s_qkv[:, :, 2]
    s_scores = jnp.einsum("nphd,nqhd->nhpq", s_query, s_key, preferred_element_type=F32) * scale
    s_probs = jax.nn.softmax(s_scores, axis=-1)
    s_low = s_probs.astype(BF)
    s_out = jnp.einsum("nhpq,nqhd->nphd", s_low, s_value, preferred_element_type=F32).astype(BF)
    s_out = s_out.reshape(clips, patch, width)
    mid_here = (first_state + mul(s_out, w_so)).astype(BF)

    mid_state = to_positions(mid_here).astype(F32)
    frame_ids = jnp.arange(frames, dtype=jnp.int32)
    mask = (frame_ids[:, None] < frame_counts[None, :]).astype(F32)[:, :, None, None]
    allowed = (frame_ids[None, None, :] < frame_counts[:, None, None]) & (
        frame_ids[None, None, :] <= frame_ids[None, :, None]
    )
    act_two = layer_norm(mid_state, ln_gain[1], ln_bias[1]).astype(BF)
    t_qkv = mul(act_two, w_tqkv).astype(BF).reshape(frames, clips, part, 3, heads, dim)
    t_query, t_key, t_value = t_qkv[..., 0, :, :], t_qkv[..., 1, :, :], t_qkv[..., 2, :, :]
    t_scores = jnp.einsum("fcphd,ecphd->cphfe", t_query, t_key, preferred_element_type=F32) * scale
    t_probs = jax.nn.softmax(jnp.where(allowed[:, None, None], t_scores, NEG), axis=-1)
    t_low = t_probs.astype(BF)
    t_out = jnp.einsum("cphfe,ecphd->fcphd", t_low, t_value, preferred_element_type=F32).astype(BF)
    t_out = t_out.reshape(frames, clips, part, width)
    late_state = mid_state + mul(t_out, w_to)
    act_three = layer_norm(late_state, ln_gain[2], ln_bias[2]).astype(BF)
    pre_act = mul(act_three, w_up) + b_up
    hidden, gelu_pull = jax.vjp(jax.nn.gelu, pre_act)
    hidden = hidden.astype(BF)
    block_out = to_frames((late_state + mul(hidden, w_down)).astype(BF))
    d_out = cot.astype(F32) * mask
    d_down = d_out.astype(BF)
    grad_down = wgrad(hidden, d_down)
    d_pre = gelu_pull(mul_t(d_down, w_down))[0].astype(BF)
    grad_up = wgrad(act_three, d_pre)
    up_bias = jnp.sum(d_pre.astype(F32), axis=(0, 1, 2))
    d_norm3, gain_three, bias_three = norm_back(late_state, ln_gain[2], ln_bias[2], mul_t(d_pre, w_up))
    d_late = d_out + d_norm3
    chunks = w_up.shape[1] // width
    ffn = reduce_rows(
        jnp.concatenate(
            [
                grad_up.astype(BF).reshape(width, chunks, width).transpose(1, 0, 2).reshape(-1, width),
                grad_down.astype(BF),
            ],
            axis=0,
        )
    )
    d_tproj = d_late.astype(BF)
    grad_to = wgrad(t_out, d_tproj)
    d_tout = mul_t(d_tproj, w_to).astype(BF).reshape(frames, clips, part, heads, dim)
    d_tprob = jnp.einsum("fcphd,ecphd->cphfe", d_tout, t_value, preferred_element_type=F32)
    t_delta = jnp.sum(t_probs * d_tprob, axis=-1, keepdims=True)
    d_tscore = (t_probs * (d_tprob - t_delta)).astype(BF)
    d_tq = jnp.einsum("cphfe,ecphd->fcphd", d_tscore, t_key, preferred_element_type=F32) * scale
    d_tk = jnp.einsum("cphfe,fcphd->ecphd", d_tscore, t_query, preferred_element_type=F32) * scale
    d_tv = jnp.einsum("cphfe,fcphd->ecphd", t_low, d_tout, preferred_element_type=F32)
    d_tqkv = jnp.concatenate(
        [v.reshape(frames, clips, part, width) for v in (d_tq, d_tk, d_tv)], axis=-1
    ).astype(BF)
    grad_tqkv = wgrad(act_two, d_tqkv)
    d_norm2, gain_two, bias_two = norm_back(mid_state, ln_gain[1], ln_bias[1], mul_t(d_tqkv, w_tqkv))
    d_mid = to_frames((d_late + d_norm2).astype(BF))

    grad_so = wgrad(s_out, d_mid)
    d_sout = mul_t(d_mid, w_so).astype(BF).reshape(clips, patch, heads, dim)
    d_sprob = jnp.einsum("nphd,nqhd->nhpq", d_sout, s_value, preferred_element_type=F32)
    s_delta = jnp.sum(s_probs * d_sprob, axis=-1, keepdims=True)
    d_sscore = (s_probs * (d_sprob - s_delta)).astype(BF)
    d_sq = jnp.einsum("nhpq,nqhd->nphd", d_sscore, s_key, preferred_element_type=F32) * scale
    d_sk = jnp.einsum("nhpq,nphd->nqhd", d_sscore, s_query, preferred_element_type=F32) * scale
    d_sv = jnp.einsum("nhpq,nphd->nqhd", s_low, d_sout, preferred_element_type=F32)
    d_sqkv = jnp.concatenate([v.reshape(clips, patch, width) for v in (d_sq, d_sk, d_sv)], axis=-1)
    d_sqkv = d_sqkv.astype(BF)
    grad_sqkv = wgrad(act_one, d_sqkv)
    d_norm1, gain_one, bias_one = norm_back(first_state, ln_gain[0], ln_bias[0], mul_t(d_sqkv, w_sqkv))
    grad_input = d_mid.astype(F32) + d_norm1
    frame_sums = jnp.sum(grad_input, axis=1)
    grad_table = jnp.einsum("ca,cd->ad", onehot, frame_sums, precision=lax.Precision.HIGHEST)

    def blocks(v):
        return v.reshape(width, -1, width).transpose(1, 0, 2).reshape(-1, width)

    small = jnp.concatenate(
        [
            grad_table,
            jnp.stack([gain_one, gain_two, gain_three, bias_one, bias_two, bias_three]),
            up_bias.reshape(-1, width),
        ],
        axis=0,
    )
    devices = lax.axis_size(CHIP_AXES) * lax.axis_size("c")
    per_device = small.size // devices
    main = jnp.concatenate([blocks(grad_tqkv), grad_to, blocks(grad_sqkv), grad_so], axis=0)
    rows = main.shape[0] // devices
    extra = jnp.pad(small.reshape(devices, 1, per_device), ((0, 0), (0, rows - 1), (0, 128 - per_device)))
    main = jnp.concatenate([main.reshape(devices, rows, width), extra], axis=-1)
    rest = reduce_rows(main.reshape(devices * rows, width + 128)).astype(F32)
    small = rest.reshape(devices, rows, width + 128)[:, 0, width : width + per_device].reshape(-1, width)
    main = rest[:, :width]

    def unblock(v):
        return v.reshape(-1, width, width).transpose(1, 0, 2).reshape(width, -1)

    table_rows = action_table.shape[0]
    up_rows = w_up.shape[1]
    ffn = ffn.astype(F32)
    return (
        block_out[:, None],
        grad_input[:, None],
        small[:table_rows],
        small[table_rows : table_rows + 3],
        small[table_rows + 3 : table_rows + 6],
        unblock(main[2048:3584]),
        main[3584:4096],
        unblock(main[:1536]),
        main[1536:2048],
        unblock(ffn[:up_rows]),
        small[table_rows + 6 :].reshape(-1),
        ffn[up_rows:],
    )


def solution(mesh):
    fine = Mesh(mesh.devices.reshape(4, 2, 2, 4, 2), ("x", "zh", "zl", "y", "c"))
    clip = ("zl", "y", "c")
    tokens = P(clip, FRAME_AXES, None, None)
    in_specs = (tokens, P(clip, FRAME_AXES), P(clip)) + (P(),) * 10 + (tokens,)
    out_specs = (tokens, tokens) + (P(),) * 10
    return jax.shard_map(shards, mesh=fine, in_specs=in_specs, out_specs=out_specs, check_vma=False)
```

```python
import functools
import math

import jax
import jax.numpy as jnp
from jax import lax
from jax.experimental import pallas as pl
from jax.experimental.pallas import tpu as pltpu
from jax.sharding import Mesh, PartitionSpec as P

HEADS = 8
EPS = 1e-05
NEG = -1e30
BF = jnp.bfloat16
F32 = jnp.float32
FRAME_AXES = ("x", "zh")
CHIP_AXES = ("x", "zh", "zl", "y")
MIB = 1 << 20
SMEM = pltpu.SMEM


def dot(a, b):
    return jnp.dot(a, b, preferred_element_type=F32)


def dot_nt(a, b):
    return lax.dot_general(a, b, (((1,), (1,)), ((), ())), preferred_element_type=F32)


def dot_tn(a, b):
    return lax.dot_general(a, b, (((0,), (0,)), ((), ())), preferred_element_type=F32)


def norm_parts(v):
    center = v - jnp.mean(v, axis=-1, keepdims=True)
    rstd = lax.rsqrt(jnp.mean(center * center, axis=-1, keepdims=True) + EPS)
    return center * rstd, rstd


def norm_back(unit, rstd, gain, up):
    d_unit = up * gain
    mean_a = jnp.mean(d_unit, axis=-1, keepdims=True)
    mean_b = jnp.mean(d_unit * unit, axis=-1, keepdims=True)
    return rstd * (d_unit - mean_a - unit * mean_b)


def fold_rows(v):
    return jnp.sum(v.reshape(-1, 8, v.shape[-1]), axis=0)


def head_masks(scale):
    lane = lax.broadcasted_iota(jnp.int32, (1, 128), 1)
    first = jnp.where(lane < 64, scale, 0.0).astype(BF)
    second = jnp.where(lane < 64, 0.0, scale).astype(BF)
    return first, second


def split_heads(v, masks):
    return jnp.concatenate([v * masks[0], v * masks[1]], axis=0)


def softmax(s):
    e = jnp.exp(s - jnp.max(s, axis=-1, keepdims=True))
    return e * (1.0 / jnp.sum(e, axis=-1, keepdims=True))


def pick_heads(v):
    half = v.shape[0] // 2
    lane = lax.broadcasted_iota(jnp.int32, (half, 128), 1)
    return jnp.where(lane < 64, v[:half], v[half:])


def embed(tok_ref, table_ref, action):
    table = table_ref[...].astype(F32)
    rows = lax.broadcasted_iota(jnp.int32, table.shape, 0)
    row = jnp.sum(jnp.where(rows == action, table, 0.0), axis=0, keepdims=True)
    return tok_ref[0].astype(F32) + row


def spatial_forward(offset, actions_ref, tok_ref, cot_ref, table_ref, gain_ref, bias_ref, wqkv_ref, wo_ref,
                    both_ref, qkv_ref, low_ref, out_ref, act_ref):
    x = embed(tok_ref, table_ref, actions_ref[offset + pl.program_id(0)])
    unit, _ = norm_parts(x)
    act = (unit * gain_ref[0:1] + bias_ref[0:1]).astype(BF)
    act_ref[0] = act
    width = x.shape[1]
    for part in range(3):
        cols = slice(part * width, (part + 1) * width)
        qkv_ref[0, :, cols] = dot(act, wqkv_ref[:, cols]).astype(BF)
    scaled = head_masks(1.0 / math.sqrt(width // HEADS))
    plain = head_masks(1.0)
    n = x.shape[0]
    for pair in range(HEADS // 2):
        at = slice(pair * 128, pair * 128 + 128)
        query = qkv_ref[0, :, pair * 128 : pair * 128 + 128]
        key = qkv_ref[0, :, width + pair * 128 : width + pair * 128 + 128]
        value = qkv_ref[0, :, 2 * width + pair * 128 : 2 * width + pair * 128 + 128]
        s = dot_nt(query, split_heads(key, scaled))
        low_ref[0, pair, :, :n] = softmax(s[:, :n]).astype(BF)
        low_ref[0, pair, :, n:] = softmax(s[:, n:]).astype(BF)
        out_ref[0, :, at] = dot(low_ref[0, pair], split_heads(value, plain)).astype(BF)
    mid = (x + dot(out_ref[0], wo_ref[...])).astype(BF)
    frames, clips, part, _ = both_ref.shape
    step = pl.program_id(0)
    both_ref[:, step] = mid.reshape(frames, part, width)
    both_ref[:, clips // 2 + step] = cot_ref[0].reshape(frames, part, width)


def resident(shape):
    return pl.BlockSpec(shape, lambda *_: (0,) * len(shape), pipeline_mode=pl.Buffered(1))


def params(mib=56):
    return pltpu.CompilerParams(vmem_limit_bytes=mib * MIB)


def cost(flops, nbytes):
    return pl.CostEstimate(flops=int(flops), bytes_accessed=int(nbytes), transcendentals=0)


def run_spatial_forward(frames, offset, clips, actions, tok, cot, table, gain, bias, w_qkv, w_o):
    _, patch, width = tok.shape
    part = patch // frames
    row = lambda c: (c, 0, 0)
    return pl.pallas_call(
        functools.partial(spatial_forward, offset),
        grid=(clips,),
        in_specs=[
            pl.BlockSpec(memory_space=SMEM),
            pl.BlockSpec((1, patch, width), lambda c: (c + offset, 0, 0)),
            pl.BlockSpec((1, patch, width), lambda c: (c + offset, 0, 0)),
            resident(table.shape), resident(gain.shape), resident(bias.shape),
            resident(w_qkv.shape), resident(w_o.shape),
        ],
        out_specs=[
            resident((frames, 2 * clips, part, width)),
            pl.BlockSpec((1, patch, 3 * width), row),
            pl.BlockSpec((1, HEADS // 2, patch, 2 * patch), lambda c: (c, 0, 0, 0)),
            pl.BlockSpec((1, patch, width), row),
            pl.BlockSpec((1, patch, width), row),
        ],
        out_shape=[
            jax.ShapeDtypeStruct((frames, 2 * clips, part, width), BF),
            jax.ShapeDtypeStruct((clips, patch, 3 * width), BF),
            jax.ShapeDtypeStruct((clips, HEADS // 2, patch, 2 * patch), BF),
            jax.ShapeDtypeStruct((clips, patch, width), BF),
            jax.ShapeDtypeStruct((clips, patch, width), BF),
        ],
        compiler_params=params(),
        cost_estimate=cost(clips * patch * width * width * 10, 4 * clips * MIB),
        name="spatial_forward",
    )(actions, tok, cot, table, gain, bias, w_qkv, w_o)


def rows_of(ref, clip, half, part):
    v = ref[:, clip, half * part : (half + 1) * part, :]
    return v.reshape(-1, v.shape[-1])


def load_rows(ref, clips, part):
    return jnp.concatenate(
        [rows_of(ref, c, h, part) for c in range(clips) for h in range(2)], axis=0
    )


def store_rows(ref, v, first, clips, part):
    frames = ref.shape[0]
    block = frames * part
    for c in range(clips):
        for h in range(2):
            at = (2 * c + h) * block
            ref[:, first + c, h * part : (h + 1) * part, :] = v[at : at + block].reshape(frames, part, v.shape[-1])


def temporal(offset, filled, counts_ref, mid_ref, cot_ref, gain_ref, bias_ref, bup_ref, wqkv_ref, wo_ref, wup_ref,
             wdown_ref, *rest):
    rest = rest[8:] if filled else rest
    (both_ref, act2_ref, dqkv_ref, tout_ref, dproj_ref, act3_ref, dpre_ref, hid_ref, ddown_ref,
     small_ref, upbias_ref, qkv_s, low_s, dtout_s) = rest
    step = pl.program_id(0)
    frames, clips, both, width = mid_ref.shape
    part = both // 2
    block = frames * part
    x = load_rows(mid_ref, clips, part).astype(F32)
    rows = x.shape[0]
    unit2, rstd2 = norm_parts(x)
    act2 = (unit2 * gain_ref[1:2] + bias_ref[1:2]).astype(BF)
    act2_ref[...] = act2
    for i in range(3):
        cols = slice(i * width, (i + 1) * width)
        qkv_s[:, cols] = dot(act2, wqkv_ref[:, cols]).astype(BF)
    scaled = head_masks(1.0 / math.sqrt(width // HEADS))
    plain = head_masks(1.0)
    r = lax.broadcasted_iota(jnp.int32, (block, block), 0)
    s = lax.broadcasted_iota(jnp.int32, (block, block), 1)
    base = (r % part == s % part) & (s // part <= r // part)
    row_mask = []
    for c in range(clips):
        count = counts_ref[offset + step * clips + c]
        allowed = base & (s // part < count)
        row_mask.append(count)
        for h in range(2):
            b = 2 * c + h
            at = slice(b * block, (b + 1) * block)
            for pair in range(HEADS // 2):
                lo = pair * 128
                query = qkv_s[at, lo : lo + 128]
                key = qkv_s[at, width + lo : width + lo + 128]
                value = qkv_s[at, 2 * width + lo : 2 * width + lo + 128]
                scores = dot_nt(query, split_heads(key, scaled))
                for k in range(2):
                    sc = jnp.where(allowed, scores[:, k * block : (k + 1) * block], NEG)
                    low_s[b, pair, :, k * block : (k + 1) * block] = softmax(sc).astype(BF)
                tout_ref[at, lo : lo + 128] = dot(low_s[b, pair], split_heads(value, plain)).astype(BF)
    late = x + dot(tout_ref[...], wo_ref[...])
    unit3, rstd3 = norm_parts(late)
    act3 = (unit3 * gain_ref[2:3] + bias_ref[2:3]).astype(BF)
    act3_ref[...] = act3
    frame_of = lax.broadcasted_iota(jnp.int32, (block, width), 0) // part
    d_out = load_rows(cot_ref, clips, part)
    d_out = jnp.concatenate(
        [
            jnp.where(frame_of < row_mask[b // 2], d_out[b * block : (b + 1) * block].astype(F32), 0.0)
            for b in range(2 * clips)
        ],
        axis=0,
    )
    d_down = d_out.astype(BF)
    ddown_ref[...] = d_down
    out = late
    d_act3 = None

    @pl.when(step == 0)
    def _():
        small_ref[...] = jnp.zeros_like(small_ref)
        upbias_ref[...] = jnp.zeros_like(upbias_ref)

    k0 = math.sqrt(2.0 / math.pi)
    k1 = 0.044715
    for j in range(wup_ref.shape[1] // width):
        cols = slice(j * width, (j + 1) * width)
        u = dot(act3, wup_ref[:, cols]) + bup_ref[0:1, cols]
        sq = u * u
        t = jnp.tanh(k0 * u * (1.0 + k1 * sq))
        half_t = 0.5 + 0.5 * t
        hid = (u * half_t).astype(BF)
        slope = half_t + 0.5 * u * (1.0 - t * t) * (k0 + (3.0 * k0 * k1) * sq)
        hid_ref[:, cols] = hid
        out = out + dot(hid, wdown_ref[cols, :])
        d_pre32 = dot_nt(d_down, wdown_ref[cols, :]) * slope
        d_pre = d_pre32.astype(BF)
        dpre_ref[:, cols] = d_pre
        upbias_ref[:, cols] += fold_rows(d_pre.astype(F32))
        more = dot_nt(d_pre, wup_ref[:, cols])
        d_act3 = more if d_act3 is None else d_act3 + more
    store_rows(both_ref, out.astype(BF), both_ref.shape[1] // 2 + step * clips, clips, part)
    small_ref[0] += fold_rows(d_act3 * unit3)
    small_ref[1] += fold_rows(d_act3)
    d_late = d_out + norm_back(unit3, rstd3, gain_ref[2:3], d_act3)
    d_proj = d_late.astype(BF)
    dproj_ref[...] = d_proj
    dtout_s[...] = dot_nt(d_proj, wo_ref[...]).astype(BF)
    for b in range(2 * clips):
        at = slice(b * block, (b + 1) * block)
        for pair in range(HEADS // 2):
            lo = pair * 128
            query = qkv_s[at, lo : lo + 128]
            key = qkv_s[at, width + lo : width + lo + 128]
            value = qkv_s[at, 2 * width + lo : 2 * width + lo + 128]
            d_o = dtout_s[at, lo : lo + 128]
            d_p = dot_nt(d_o, split_heads(value, plain))
            low = low_s[b, pair]
            ds = []
            for k in range(2):
                cols = slice(k * block, (k + 1) * block)
                p = low[:, cols].astype(F32)
                pd = p * d_p[:, cols]
                ds.append((pd - p * jnp.sum(pd, axis=-1, keepdims=True)).astype(BF))
            d_s = jnp.concatenate(ds, axis=1)
            dqkv_ref[at, lo : lo + 128] = dot(d_s, split_heads(key, scaled)).astype(BF)
            d_k = pick_heads(dot_tn(d_s, query)) * (1.0 / math.sqrt(width // HEADS))
            dqkv_ref[at, width + lo : width + lo + 128] = d_k.astype(BF)
            d_v = pick_heads(dot_tn(low, d_o))
            dqkv_ref[at, 2 * width + lo : 2 * width + lo + 128] = d_v.astype(BF)
    d_act2 = dot_nt(dqkv_ref[...], wqkv_ref[...])
    small_ref[2] += fold_rows(d_act2 * unit2)
    small_ref[3] += fold_rows(d_act2)
    d_mid = d_late + norm_back(unit2, rstd2, gain_ref[1:2], d_act2)
    store_rows(both_ref, d_mid.astype(BF), step * clips, clips, part)


def run_temporal(offset, total_clips, counts, both_in, gain, bias, b_up, w_qkv, w_o, w_up, w_down, group, filled):
    frames, clips, both, width = both_in.shape
    clips //= 2
    hidden = w_up.shape[1]
    rows = group * frames * both
    total = total_clips * frames * both
    tokens = lambda off: pl.BlockSpec((frames, group, both, width), lambda c: (0, c + off // group, 0, 0))
    flat = lambda w: pl.BlockSpec((rows, w), lambda c: (c + offset // group, 0))
    widths = (width, 3 * width, width, width, width, hidden, hidden, width)
    out_both = (frames, 2 * clips, both, width)
    inputs = (counts, both_in, both_in, gain, bias, b_up, w_qkv, w_o, w_up, w_down)
    return pl.pallas_call(
        functools.partial(temporal, offset, bool(filled)),
        grid=(clips // group,),
        in_specs=[pl.BlockSpec(memory_space=SMEM), tokens(0), tokens(clips)]
        + [resident(a.shape) for a in (gain, bias, b_up, w_qkv, w_o, w_up, w_down)]
        + [pl.BlockSpec(memory_space=pl.ANY)] * len(filled),
        out_specs=[resident(out_both)]
        + [flat(w) for w in widths]
        + [resident((4, 8, width)), resident((8, hidden))],
        out_shape=[jax.ShapeDtypeStruct(out_both, BF)]
        + [jax.ShapeDtypeStruct((total, w), BF) for w in widths]
        + [jax.ShapeDtypeStruct((4, 8, width), F32), jax.ShapeDtypeStruct((8, hidden), F32)],
        scratch_shapes=[
            pltpu.VMEM((rows, 3 * width), BF),
            pltpu.VMEM((2 * group, HEADS // 2, rows // (2 * group), rows // group), BF),
            pltpu.VMEM((rows, width), BF),
        ],
        input_output_aliases={len(inputs) + i: 1 + i for i in range(len(filled))},
        compiler_params=params(),
        cost_estimate=cost(clips * frames * both * width * width * 40, 8 * clips * MIB),
        name="temporal",
    )(*inputs, *filled)


def spatial_backward(offset, actions_ref, tok_ref, dmid_ref, qkv_ref, low_ref, table_ref, gain_ref, wqkv_ref, wo_ref,
                     *rest):
    dqkv_ref, gin_ref, small_ref, gtable_ref = rest[-4:]
    step = pl.program_id(0)
    action = actions_ref[offset + step]
    x = embed(tok_ref, table_ref, action)
    n, width = x.shape
    d_mid = dmid_ref[:, 0].reshape(n, width)
    d_out = dot_nt(d_mid, wo_ref[...]).astype(BF)
    scaled = head_masks(1.0 / math.sqrt(width // HEADS))
    plain = head_masks(1.0)
    for pair in range(HEADS // 2):
        lo = pair * 128
        query = qkv_ref[0, :, lo : lo + 128]
        key = qkv_ref[0, :, width + lo : width + lo + 128]
        value = qkv_ref[0, :, 2 * width + lo : 2 * width + lo + 128]
        d_o = d_out[:, lo : lo + 128]
        d_p = dot_nt(d_o, split_heads(value, plain))
        low = low_ref[0, pair]
        ds = []
        for k in range(2):
            cols = slice(k * n, (k + 1) * n)
            p = low[:, cols].astype(F32)
            pd = p * d_p[:, cols]
            ds.append((pd - p * jnp.sum(pd, axis=-1, keepdims=True)).astype(BF))
        d_s = jnp.concatenate(ds, axis=1)
        dqkv_ref[0, :, lo : lo + 128] = dot(d_s, split_heads(key, scaled)).astype(BF)
        d_k = pick_heads(dot_tn(d_s, query)) * (1.0 / math.sqrt(width // HEADS))
        dqkv_ref[0, :, width + lo : width + lo + 128] = d_k.astype(BF)
        dqkv_ref[0, :, 2 * width + lo : 2 * width + lo + 128] = pick_heads(dot_tn(low, d_o)).astype(BF)
    d_act = dot_nt(dqkv_ref[0], wqkv_ref[...])
    unit, rstd = norm_parts(x)

    @pl.when(step == 0)
    def _():
        small_ref[...] = jnp.zeros_like(small_ref)
        gtable_ref[...] = jnp.zeros_like(gtable_ref)

    small_ref[0] += fold_rows(d_act * unit)
    small_ref[1] += fold_rows(d_act)
    g = d_mid.astype(F32) + norm_back(unit, rstd, gain_ref[0:1], d_act)
    gin_ref[0] = g
    total = jnp.sum(g, axis=0, keepdims=True)
    rows = lax.broadcasted_iota(jnp.int32, gtable_ref.shape, 0)
    gtable_ref[...] += jnp.where(rows == action, total, 0.0)


def run_spatial_backward(offset, actions, tok, both, qkv, low, table, gain, w_qkv, w_o, filled):
    total, patch, width = tok.shape
    clips = qkv.shape[0]
    frames, _, part, _ = both.shape
    row = lambda c: (c, 0, 0)
    later = lambda c: (c + offset, 0, 0)
    inputs = (actions, tok, both, qkv, low, table, gain, w_qkv, w_o)
    return pl.pallas_call(
        functools.partial(spatial_backward, offset),
        grid=(clips,),
        in_specs=[
            pl.BlockSpec(memory_space=SMEM),
            pl.BlockSpec((1, patch, width), later),
            pl.BlockSpec((frames, 1, part, width), lambda c: (0, c, 0, 0)),
            pl.BlockSpec((1, patch, 3 * width), row),
            pl.BlockSpec((1, HEADS // 2, patch, 2 * patch), lambda c: (c, 0, 0, 0)),
            resident(table.shape), resident(gain.shape), resident(w_qkv.shape), resident(w_o.shape),
        ]
        + [pl.BlockSpec(memory_space=pl.ANY)] * len(filled),
        out_specs=[
            pl.BlockSpec((1, patch, 3 * width), later),
            pl.BlockSpec((1, patch, width), later),
            resident((2, 8, width)),
            resident(table.shape),
        ],
        out_shape=[
            jax.ShapeDtypeStruct((total, patch, 3 * width), BF),
            jax.ShapeDtypeStruct((total, patch, width), F32),
            jax.ShapeDtypeStruct((2, 8, width), F32),
            jax.ShapeDtypeStruct(table.shape, F32),
        ],
        input_output_aliases={len(inputs) + i: i for i in range(len(filled))},
        compiler_params=params(),
        cost_estimate=cost(clips * patch * width * width * 14, 6 * clips * MIB),
        name="spatial_backward",
    )(*inputs, *filled)


def choose(core, first, second, keep_ref, send_ref, at):
    for k in range(first.shape[1] // 128):
        cols = slice(k * 128, (k + 1) * 128)
        keep_ref[at, k] = jnp.where(core == 0, first[:, cols], second[:, cols]).astype(BF)
        send_ref[at, k] = jnp.where(core == 0, second[:, cols], first[:, cols]).astype(BF)


def ffn_grads(core_ref, a_ref, b_ref, c_ref, d_ref, keep_ref, send_ref):
    choose(
        core_ref[0], dot_tn(a_ref[...], b_ref[...]), dot_tn(c_ref[...], d_ref[...]), keep_ref, send_ref, 0
    )


def run_ffn_grads(core, act3, d_pre, hid, d_down):
    total, width = act3.shape
    count = d_pre.shape[1] // width
    wide = pl.BlockSpec((total, width), lambda j: (0, j))
    out = pl.BlockSpec((1, width // 128, width, 128), lambda j: (j, 0, 0, 0))
    return pl.pallas_call(
        ffn_grads,
        grid=(count,),
        in_specs=[pl.BlockSpec(memory_space=SMEM), resident(act3.shape), wide, wide, resident(d_down.shape)],
        out_specs=[out, out],
        out_shape=[jax.ShapeDtypeStruct((count, width // 128, width, 128), BF)] * 2,
        compiler_params=params(),
        cost_estimate=cost(4 * total * width * width * count, 16 * MIB),
        name="ffn_grads",
    )(core, act3, d_pre, hid, d_down)


def temporal_grads(core_ref, act_ref, dqkv_ref, out_ref, dproj_ref, keep_ref, send_ref):
    width = act_ref.shape[1]
    part = lambda j: dot_tn(act_ref[...], dqkv_ref[:, j * width : (j + 1) * width])
    choose(core_ref[0], part(0), part(2), keep_ref, send_ref, 0)
    choose(core_ref[0], part(1), dot_tn(out_ref[...], dproj_ref[...]), keep_ref, send_ref, 1)


def run_temporal_grads(core, act, d_qkv, out, d_proj):
    total, width = act.shape
    shape = (4, width // 128, width, 128)
    spec = pl.BlockSpec((2, *shape[1:]), lambda i: (0, 0, 0, 0))
    arrays = (act, d_qkv, out, d_proj)
    return pl.pallas_call(
        temporal_grads,
        grid=(1,),
        in_specs=[pl.BlockSpec(memory_space=SMEM)] + [resident(a.shape) for a in arrays],
        out_specs=[spec, spec],
        out_shape=[jax.ShapeDtypeStruct(shape, BF)] * 2,
        compiler_params=params(),
        cost_estimate=cost(8 * total * width * width, 8 * MIB),
        name="temporal_grads",
    )(core, *arrays)


def spatial_grads(core_ref, act0_ref, act1_ref, dqkv_ref, out0_ref, out1_ref, both0_ref, both1_ref, *rest):
    keep_ref, send_ref = rest[-2:]
    frames, _, part, width = both0_ref.shape
    flat = lambda ref: ref[...].reshape(-1, width)
    act = jnp.concatenate([flat(act0_ref), flat(act1_ref)], axis=0)
    out = jnp.concatenate([flat(out0_ref), flat(out1_ref)], axis=0)
    half = out0_ref.shape[0]
    d_mid = jnp.concatenate(
        [ref[:, c].reshape(frames * part, width) for ref in (both0_ref, both1_ref) for c in range(half)], axis=0
    )
    total = act.shape[0]
    grad = lambda j: dot_tn(act, dqkv_ref[:, :, j * width : (j + 1) * width].reshape(total, width))
    choose(core_ref[0], grad(0), grad(2), keep_ref, send_ref, 0)
    choose(core_ref[0], grad(1), dot_tn(out, d_mid), keep_ref, send_ref, 1)


def run_spatial_grads(core, *arrays):
    keep = arrays[-1]
    width = keep.shape[2]
    spec = pl.BlockSpec((2, *keep.shape[1:]), lambda i: (1, 0, 0, 0))
    n = len(arrays)
    return pl.pallas_call(
        spatial_grads,
        grid=(1,),
        in_specs=[pl.BlockSpec(memory_space=SMEM)]
        + [resident(a.shape) for a in arrays[:-2]]
        + [pl.BlockSpec(memory_space=pl.ANY)] * 2,
        out_specs=[spec, spec],
        out_shape=[jax.ShapeDtypeStruct(keep.shape, BF)] * 2,
        input_output_aliases={n - 1: 0, n: 1},
        compiler_params=params(),
        cost_estimate=cost(8 * 1024 * width * width, 8 * MIB),
        name="spatial_grads",
    )(core, *arrays)


def unpack(core_ref, mine_ref, peer_ref, up_ref, down_ref, tqkv_ref, to_ref, sqkv_ref, so_ref):
    step = pl.program_id(0)
    core = core_ref[0]
    width = up_ref.shape[0]
    mine = mine_ref[...].reshape(-1, 128).astype(F32)
    peer = peer_ref[...].reshape(-1, 128).astype(F32)
    first = jnp.where(core == 0, mine, peer)
    second = jnp.where(core == 0, peer, mine)

    def put(ref, v, at):
        for k in range(width // 128):
            ref[:, at + k * 128 : at + (k + 1) * 128] = v[k * width : (k + 1) * width]

    @pl.when(step < 4)
    def _():
        put(up_ref, first, 0)
        put(down_ref, second, 0)

    for i, (qkv_ref, o_ref) in enumerate(((tqkv_ref, to_ref), (sqkv_ref, so_ref))):
        @pl.when(step == 4 + 2 * i)
        def _():
            put(qkv_ref, first, 0)
            put(qkv_ref, second, 2 * width)

        @pl.when(step == 5 + 2 * i)
        def _():
            put(qkv_ref, first, width)
            put(o_ref, second, 0)


def run_unpack(core, mine, peer, width):
    chips, _, lanes = mine.shape
    group = chips // 4
    block = pl.BlockSpec((group, 128, lanes), lambda j: (j % 4, j // 4, 0))
    up = lambda j: (0, jnp.minimum(j, 3))
    down = lambda j: (jnp.minimum(j, 3), 0)
    return pl.pallas_call(
        unpack,
        grid=(8,),
        in_specs=[pl.BlockSpec(memory_space=SMEM), block, block],
        out_specs=[
            pl.BlockSpec((width, width), up),
            pl.BlockSpec((width, width), down),
            resident((width, 3 * width)), resident((width, width)),
            resident((width, 3 * width)), resident((width, width)),
        ],
        out_shape=[
            jax.ShapeDtypeStruct((width, 4 * width), F32),
            jax.ShapeDtypeStruct((4 * width, width), F32),
            jax.ShapeDtypeStruct((width, 3 * width), F32), jax.ShapeDtypeStruct((width, width), F32),
            jax.ShapeDtypeStruct((width, 3 * width), F32), jax.ShapeDtypeStruct((width, width), F32),
        ],
        compiler_params=params(),
        cost_estimate=cost(MIB, 24 * MIB),
        name="unpack",
    )(core, mine, peer)


def swap_cores(v):
    return lax.ppermute(v, "c", [(0, 1), (1, 0)])


def after(v, *done):
    return lax.optimization_barrier((v, *done))[0]


def over_frames(v):
    return lax.all_to_all(v, FRAME_AXES, 0, 0)


def over_chips(v):
    return lax.all_to_all(v, CHIP_AXES, 0, 0)


def add_parts(parts):
    return jnp.sum(parts.astype(F32), axis=0).astype(BF)


def add_core(keep, send):
    return (keep.astype(F32) + swap_cores(send).astype(F32)).astype(BF)


def shards(
    frame_tokens, actions, frame_counts, action_table, ln_gain, ln_bias, w_sqkv, w_so, w_tqkv, w_to,
    w_up, b_up, w_down, cotangent,
):
    clips, _, patch, width = frame_tokens.shape
    frames = lax.axis_size(FRAME_AXES)
    chips = lax.axis_size(CHIP_AXES)
    core = lax.axis_index("c").astype(jnp.int32).reshape(1)
    tok = frame_tokens[:, 0]
    acts = actions[:, 0]
    half = clips // 2
    forward = [
        run_spatial_forward(
            frames, i * half, half, acts, tok, cotangent[:, 0], action_table, ln_gain, ln_bias, w_sqkv, w_so
        )
        for i in range(2)
    ]
    there0 = over_frames(forward[0][0])
    there1 = over_frames(after(forward[1][0], there0))
    back = (ln_gain, ln_bias, b_up[None], w_tqkv, w_to, w_up, w_down)
    first = run_temporal(0, clips, frame_counts, there0, *back, 1, ())
    second = run_temporal(half, clips, frame_counts, there1, *back, 1, first[1:9])
    both0 = over_frames(after(first[0], there1))
    both1 = over_frames(after(second[0], both0))
    act_two, d_tqkv, t_out, d_tproj, act_three, d_pre, hidden, d_down, small_b, up_bias = second[1:]
    small_b = small_b + first[9]
    up_bias = up_bias + first[10]
    lines = lambda v: v.reshape(chips, -1, 128)
    keep, send = run_ffn_grads(core, after(act_three, both0), d_pre, hidden, d_down)
    ffn = add_core(keep, send)
    keep, send = run_temporal_grads(core, act_two, d_tqkv, t_out, d_tproj)
    ffn_part = add_parts(over_chips(after(lines(ffn), both1)))

    low = (action_table, ln_gain, w_sqkv, w_so)
    c0 = run_spatial_backward(0, acts, tok, both0, forward[0][1], forward[0][2], *low, ())
    c1 = run_spatial_backward(half, acts, tok, both1, forward[1][1], forward[1][2], *low, c0[:2])
    d_sqkv, grad_input = c1[:2]
    small_c = c0[2] + c1[2]
    keep, send = run_spatial_grads(
        core, forward[0][4], forward[1][4], d_sqkv, forward[0][3], forward[1][3], both0, both1, keep, send
    )
    fold = lambda v: jnp.sum(v, axis=1)
    small_b = fold(small_b)
    small_c = fold(small_c)
    small = jnp.concatenate(
        [
            c0[3] + c1[3],
            jnp.stack([small_c[0], small_b[2], small_b[0], small_c[1], small_b[3], small_b[1]]),
            jnp.sum(up_bias, axis=0).reshape(-1, width),
        ],
        axis=0,
    )
    each = small.size // (2 * chips)
    extra = jnp.pad(small.reshape(chips, 2, each), ((0, 0), (0, 14), (0, 128 - each))).astype(BF)
    late = jnp.concatenate([lines(add_core(keep, send)), extra], axis=1)
    late_part = add_parts(over_chips(after(late, ffn_part)))
    part = jnp.concatenate([ffn_part, late_part], axis=0)
    mine = over_chips(jnp.broadcast_to(part[None], (chips, *part.shape)))
    peer = swap_cores(mine)
    grad_up, grad_down, grad_tqkv, grad_to, grad_sqkv, grad_so = run_unpack(core, mine, peer, width)
    cut = lambda v: v[:, -16:-14, :each].astype(F32)
    small = (cut(mine) + cut(peer)).reshape(-1, width)
    table_rows = action_table.shape[0]
    block_out = jnp.concatenate([both0[:, half:], both1[:, half:]], axis=1)
    block_out = block_out.transpose(1, 0, 2, 3).reshape(clips, 1, patch, width)
    return (
        block_out,
        grad_input[:, None],
        small[:table_rows],
        small[table_rows : table_rows + 3],
        small[table_rows + 3 : table_rows + 6],
        grad_sqkv,
        grad_so,
        grad_tqkv,
        grad_to,
        grad_up,
        small[table_rows + 6 :].reshape(-1),
        grad_down,
    )


def solution(mesh):
    fine = Mesh(mesh.devices.reshape(4, 2, 2, 4, 2), ("x", "zh", "zl", "y", "c"))
    clip = ("zl", "y", "c")
    tokens = P(clip, FRAME_AXES, None, None)
    in_specs = (tokens, P(clip, FRAME_AXES), P(clip)) + (P(),) * 10 + (tokens,)
    out_specs = (tokens, tokens) + (P(),) * 10
    return jax.shard_map(shards, mesh=fine, in_specs=in_specs, out_specs=out_specs, check_vma=False)
```

```python
import functools
import math

import jax
import jax.numpy as jnp
from jax import lax
from jax.experimental import pallas as pl
from jax.experimental.pallas import tpu as pltpu
from jax.sharding import Mesh, PartitionSpec as P

HEADS = 8
EPS = 1e-05
NEG = -1e30
BF = jnp.bfloat16
F32 = jnp.float32
F16 = jnp.float16
FRAME_AXES = ("x", "zh")
CHIP_AXES = ("x", "zh", "zl", "y")
MIB = 1 << 20
SMEM = pltpu.SMEM


def dot(a, b):
    return jnp.dot(a, b, preferred_element_type=F32)


def dot_nt(a, b):
    return lax.dot_general(a, b, (((1,), (1,)), ((), ())), preferred_element_type=F32)


def dot_tn(a, b):
    return lax.dot_general(a, b, (((0,), (0,)), ((), ())), preferred_element_type=F32)


def norm_parts(v):
    center = v - jnp.mean(v, axis=-1, keepdims=True)
    rstd = lax.rsqrt(jnp.mean(center * center, axis=-1, keepdims=True) + EPS)
    return center * rstd, rstd


def norm_back(unit, rstd, gain, up):
    d_unit = up * gain
    mean_a = jnp.mean(d_unit, axis=-1, keepdims=True)
    mean_b = jnp.mean(d_unit * unit, axis=-1, keepdims=True)
    return rstd * (d_unit - mean_a - unit * mean_b)


def fold_rows(v):
    return jnp.sum(v.reshape(-1, 8, v.shape[-1]), axis=0)


def head_masks(scale):
    lane = lax.broadcasted_iota(jnp.int32, (1, 128), 1)
    first = jnp.where(lane < 64, scale, 0.0).astype(BF)
    second = jnp.where(lane < 64, 0.0, scale).astype(BF)
    return first, second


def split_heads(v, masks):
    return jnp.concatenate([v * masks[0], v * masks[1]], axis=0)


def softmax(s):
    e = jnp.exp(s - jnp.max(s, axis=-1, keepdims=True))
    return e * (1.0 / jnp.sum(e, axis=-1, keepdims=True))


def pick_heads(v):
    half = v.shape[0] // 2
    lane = lax.broadcasted_iota(jnp.int32, (half, 128), 1)
    return jnp.where(lane < 64, v[:half], v[half:])


def embed(tok_ref, table_ref, action):
    table = table_ref[...].astype(F32)
    rows = lax.broadcasted_iota(jnp.int32, table.shape, 0)
    row = jnp.sum(jnp.where(rows == action, table, 0.0), axis=0, keepdims=True)
    return tok_ref[0].astype(F32) + row


def spatial_forward(offset, actions_ref, tok_ref, cot_ref, table_ref, gain_ref, bias_ref, wqkv_ref, wo_ref,
                    both_ref, qkv_ref, low_ref, out_ref, act_ref):
    x = embed(tok_ref, table_ref, actions_ref[offset + pl.program_id(0)])
    unit, _ = norm_parts(x)
    act = (unit * gain_ref[0:1] + bias_ref[0:1]).astype(BF)
    act_ref[0] = act
    width = x.shape[1]
    for part in range(3):
        cols = slice(part * width, (part + 1) * width)
        qkv_ref[0, :, cols] = dot(act, wqkv_ref[:, cols]).astype(BF)
    scaled = head_masks(1.0 / math.sqrt(width // HEADS))
    plain = head_masks(1.0)
    n = x.shape[0]
    for pair in range(HEADS // 2):
        at = slice(pair * 128, pair * 128 + 128)
        query = qkv_ref[0, :, pair * 128 : pair * 128 + 128]
        key = qkv_ref[0, :, width + pair * 128 : width + pair * 128 + 128]
        value = qkv_ref[0, :, 2 * width + pair * 128 : 2 * width + pair * 128 + 128]
        s = dot_nt(query, split_heads(key, scaled))
        low_ref[0, pair, :, :n] = softmax(s[:, :n]).astype(BF)
        low_ref[0, pair, :, n:] = softmax(s[:, n:]).astype(BF)
        out_ref[0, :, at] = dot(low_ref[0, pair], split_heads(value, plain)).astype(BF)
    mid = (x + dot(out_ref[0], wo_ref[...])).astype(BF)
    frames, clips, part, _ = both_ref.shape
    step = pl.program_id(0)
    both_ref[:, step] = mid.reshape(frames, part, width)
    both_ref[:, clips // 2 + step] = cot_ref[0].reshape(frames, part, width)


def resident(shape):
    return pl.BlockSpec(shape, lambda *_: (0,) * len(shape), pipeline_mode=pl.Buffered(1))


def params(mib=56):
    return pltpu.CompilerParams(vmem_limit_bytes=mib * MIB)


def cost(flops, nbytes):
    return pl.CostEstimate(flops=int(flops), bytes_accessed=int(nbytes), transcendentals=0)


def run_spatial_forward(frames, offset, clips, actions, tok, cot, table, gain, bias, w_qkv, w_o):
    _, patch, width = tok.shape
    part = patch // frames
    row = lambda c: (c, 0, 0)
    return pl.pallas_call(
        functools.partial(spatial_forward, offset),
        grid=(clips,),
        in_specs=[
            pl.BlockSpec(memory_space=SMEM),
            pl.BlockSpec((1, patch, width), lambda c: (c + offset, 0, 0)),
            pl.BlockSpec((1, patch, width), lambda c: (c + offset, 0, 0)),
            resident(table.shape), resident(gain.shape), resident(bias.shape),
            resident(w_qkv.shape), resident(w_o.shape),
        ],
        out_specs=[
            resident((frames, 2 * clips, part, width)),
            pl.BlockSpec((1, patch, 3 * width), row),
            pl.BlockSpec((1, HEADS // 2, patch, 2 * patch), lambda c: (c, 0, 0, 0)),
            pl.BlockSpec((1, patch, width), row),
            pl.BlockSpec((1, patch, width), row),
        ],
        out_shape=[
            jax.ShapeDtypeStruct((frames, 2 * clips, part, width), BF),
            jax.ShapeDtypeStruct((clips, patch, 3 * width), BF),
            jax.ShapeDtypeStruct((clips, HEADS // 2, patch, 2 * patch), BF),
            jax.ShapeDtypeStruct((clips, patch, width), BF),
            jax.ShapeDtypeStruct((clips, patch, width), BF),
        ],
        compiler_params=params(),
        cost_estimate=cost(clips * patch * width * width * 10, 4 * clips * MIB),
        name="spatial_forward",
    )(actions, tok, cot, table, gain, bias, w_qkv, w_o)


def rows_of(ref, clip, half, part):
    v = ref[:, clip, half * part : (half + 1) * part, :]
    return v.reshape(-1, v.shape[-1])


def load_rows(ref, clips, part):
    return jnp.concatenate(
        [rows_of(ref, c, h, part) for c in range(clips) for h in range(2)], axis=0
    )


def store_rows(ref, v, first, clips, part):
    frames = ref.shape[0]
    block = frames * part
    for c in range(clips):
        for h in range(2):
            at = (2 * c + h) * block
            ref[:, first + c, h * part : (h + 1) * part, :] = v[at : at + block].reshape(frames, part, v.shape[-1])


def temporal(offset, filled, counts_ref, mid_ref, cot_ref, gain_ref, bias_ref, bup_ref, wqkv_ref, wo_ref, wup_ref,
             wdown_ref, *rest):
    rest = rest[8:] if filled else rest
    (both_ref, act2_ref, dqkv_ref, tout_ref, dproj_ref, act3_ref, dpre_ref, hid_ref, ddown_ref,
     small_ref, upbias_ref, qkv_s, low_s, dtout_s) = rest
    step = pl.program_id(0)
    frames, clips, both, width = mid_ref.shape
    part = both // 2
    block = frames * part
    x = load_rows(mid_ref, clips, part).astype(F32)
    rows = x.shape[0]
    unit2, rstd2 = norm_parts(x)
    act2 = (unit2 * gain_ref[1:2] + bias_ref[1:2]).astype(BF)
    act2_ref[...] = act2
    for i in range(3):
        cols = slice(i * width, (i + 1) * width)
        qkv_s[:, cols] = dot(act2, wqkv_ref[:, cols]).astype(BF)
    scaled = head_masks(1.0 / math.sqrt(width // HEADS))
    plain = head_masks(1.0)
    r = lax.broadcasted_iota(jnp.int32, (block, block), 0)
    s = lax.broadcasted_iota(jnp.int32, (block, block), 1)
    base = (r % part == s % part) & (s // part <= r // part)
    row_mask = []
    for c in range(clips):
        count = counts_ref[offset + step * clips + c]
        allowed = base & (s // part < count)
        row_mask.append(count)
        for h in range(2):
            b = 2 * c + h
            at = slice(b * block, (b + 1) * block)
            for pair in range(HEADS // 2):
                lo = pair * 128
                query = qkv_s[at, lo : lo + 128]
                key = qkv_s[at, width + lo : width + lo + 128]
                value = qkv_s[at, 2 * width + lo : 2 * width + lo + 128]
                scores = dot_nt(query, split_heads(key, scaled))
                for k in range(2):
                    sc = jnp.where(allowed, scores[:, k * block : (k + 1) * block], NEG)
                    low_s[b, pair, :, k * block : (k + 1) * block] = softmax(sc).astype(BF)
                tout_ref[at, lo : lo + 128] = dot(low_s[b, pair], split_heads(value, plain)).astype(BF)
    late = x + dot(tout_ref[...], wo_ref[...])
    unit3, rstd3 = norm_parts(late)
    act3 = (unit3 * gain_ref[2:3] + bias_ref[2:3]).astype(BF)
    act3_ref[...] = act3
    frame_of = lax.broadcasted_iota(jnp.int32, (block, width), 0) // part
    d_out = load_rows(cot_ref, clips, part)
    d_out = jnp.concatenate(
        [
            jnp.where(frame_of < row_mask[b // 2], d_out[b * block : (b + 1) * block].astype(F32), 0.0)
            for b in range(2 * clips)
        ],
        axis=0,
    )
    d_down = d_out.astype(BF)
    ddown_ref[...] = d_down
    out = late
    d_act3 = None

    @pl.when(step == 0)
    def _():
        small_ref[...] = jnp.zeros_like(small_ref)
        upbias_ref[...] = jnp.zeros_like(upbias_ref)

    k0 = math.sqrt(2.0 / math.pi)
    k1 = 0.044715
    for j in range(wup_ref.shape[1] // width):
        cols = slice(j * width, (j + 1) * width)
        u = dot(act3, wup_ref[:, cols]) + bup_ref[0:1, cols]
        sq = u * u
        t = jnp.tanh(k0 * u * (1.0 + k1 * sq))
        half_t = 0.5 + 0.5 * t
        hid = (u * half_t).astype(BF)
        slope = half_t + 0.5 * u * (1.0 - t * t) * (k0 + (3.0 * k0 * k1) * sq)
        hid_ref[:, cols] = hid
        out = out + dot(hid, wdown_ref[cols, :])
        d_pre32 = dot_nt(d_down, wdown_ref[cols, :]) * slope
        d_pre = d_pre32.astype(BF)
        dpre_ref[:, cols] = d_pre
        upbias_ref[:, cols] += fold_rows(d_pre.astype(F32))
        more = dot_nt(d_pre, wup_ref[:, cols])
        d_act3 = more if d_act3 is None else d_act3 + more
    store_rows(both_ref, out.astype(BF), both_ref.shape[1] // 2 + step * clips, clips, part)
    small_ref[0] += fold_rows(d_act3 * unit3)
    small_ref[1] += fold_rows(d_act3)
    d_late = d_out + norm_back(unit3, rstd3, gain_ref[2:3], d_act3)
    d_proj = d_late.astype(BF)
    dproj_ref[...] = d_proj
    dtout_s[...] = dot_nt(d_proj, wo_ref[...]).astype(BF)
    for b in range(2 * clips):
        at = slice(b * block, (b + 1) * block)
        for pair in range(HEADS // 2):
            lo = pair * 128
            query = qkv_s[at, lo : lo + 128]
            key = qkv_s[at, width + lo : width + lo + 128]
            value = qkv_s[at, 2 * width + lo : 2 * width + lo + 128]
            d_o = dtout_s[at, lo : lo + 128]
            d_p = dot_nt(d_o, split_heads(value, plain))
            low = low_s[b, pair]
            ds = []
            for k in range(2):
                cols = slice(k * block, (k + 1) * block)
                p = low[:, cols].astype(F32)
                pd = p * d_p[:, cols]
                ds.append((pd - p * jnp.sum(pd, axis=-1, keepdims=True)).astype(BF))
            d_s = jnp.concatenate(ds, axis=1)
            dqkv_ref[at, lo : lo + 128] = dot(d_s, split_heads(key, scaled)).astype(BF)
            d_k = pick_heads(dot_tn(d_s, query)) * (1.0 / math.sqrt(width // HEADS))
            dqkv_ref[at, width + lo : width + lo + 128] = d_k.astype(BF)
            d_v = pick_heads(dot_tn(low, d_o))
            dqkv_ref[at, 2 * width + lo : 2 * width + lo + 128] = d_v.astype(BF)
    d_act2 = dot_nt(dqkv_ref[...], wqkv_ref[...])
    small_ref[2] += fold_rows(d_act2 * unit2)
    small_ref[3] += fold_rows(d_act2)
    d_mid = d_late + norm_back(unit2, rstd2, gain_ref[1:2], d_act2)
    store_rows(both_ref, d_mid.astype(BF), step * clips, clips, part)


def run_temporal(offset, total_clips, counts, both_in, gain, bias, b_up, w_qkv, w_o, w_up, w_down, group, filled):
    frames, clips, both, width = both_in.shape
    clips //= 2
    hidden = w_up.shape[1]
    rows = group * frames * both
    total = total_clips * frames * both
    tokens = lambda off: pl.BlockSpec((frames, group, both, width), lambda c: (0, c + off // group, 0, 0))
    flat = lambda w: pl.BlockSpec((rows, w), lambda c: (c + offset // group, 0))
    widths = (width, 3 * width, width, width, width, hidden, hidden, width)
    out_both = (frames, 2 * clips, both, width)
    inputs = (counts, both_in, both_in, gain, bias, b_up, w_qkv, w_o, w_up, w_down)
    return pl.pallas_call(
        functools.partial(temporal, offset, bool(filled)),
        grid=(clips // group,),
        in_specs=[pl.BlockSpec(memory_space=SMEM), tokens(0), tokens(clips)]
        + [resident(a.shape) for a in (gain, bias, b_up, w_qkv, w_o, w_up, w_down)]
        + [pl.BlockSpec(memory_space=pl.ANY)] * len(filled),
        out_specs=[resident(out_both)]
        + [flat(w) for w in widths]
        + [resident((4, 8, width)), resident((8, hidden))],
        out_shape=[jax.ShapeDtypeStruct(out_both, BF)]
        + [jax.ShapeDtypeStruct((total, w), BF) for w in widths]
        + [jax.ShapeDtypeStruct((4, 8, width), F32), jax.ShapeDtypeStruct((8, hidden), F32)],
        scratch_shapes=[
            pltpu.VMEM((rows, 3 * width), BF),
            pltpu.VMEM((2 * group, HEADS // 2, rows // (2 * group), rows // group), BF),
            pltpu.VMEM((rows, width), BF),
        ],
        input_output_aliases={len(inputs) + i: 1 + i for i in range(len(filled))},
        compiler_params=params(),
        cost_estimate=cost(clips * frames * both * width * width * 40, 8 * clips * MIB),
        name="temporal",
    )(*inputs, *filled)


def spatial_backward(offset, actions_ref, tok_ref, dmid_ref, done_ref, qkv_ref, low_ref, table_ref, gain_ref, wqkv_ref, wo_ref,
                     *rest):
    dqkv_ref, gin_ref, block_ref, small_ref, gtable_ref = rest[-5:]
    step = pl.program_id(0)
    action = actions_ref[offset + step]
    x = embed(tok_ref, table_ref, action)
    n, width = x.shape
    d_mid = dmid_ref[:, 0].reshape(n, width)
    block_ref[0] = done_ref[:, 0].reshape(n, width)
    d_out = dot_nt(d_mid, wo_ref[...]).astype(BF)
    scaled = head_masks(1.0 / math.sqrt(width // HEADS))
    plain = head_masks(1.0)
    for pair in range(HEADS // 2):
        lo = pair * 128
        query = qkv_ref[0, :, lo : lo + 128]
        key = qkv_ref[0, :, width + lo : width + lo + 128]
        value = qkv_ref[0, :, 2 * width + lo : 2 * width + lo + 128]
        d_o = d_out[:, lo : lo + 128]
        d_p = dot_nt(d_o, split_heads(value, plain))
        low = low_ref[0, pair]
        ds = []
        for k in range(2):
            cols = slice(k * n, (k + 1) * n)
            p = low[:, cols].astype(F32)
            pd = p * d_p[:, cols]
            ds.append((pd - p * jnp.sum(pd, axis=-1, keepdims=True)).astype(BF))
        d_s = jnp.concatenate(ds, axis=1)
        dqkv_ref[0, :, lo : lo + 128] = dot(d_s, split_heads(key, scaled)).astype(BF)
        d_k = pick_heads(dot_tn(d_s, query)) * (1.0 / math.sqrt(width // HEADS))
        dqkv_ref[0, :, width + lo : width + lo + 128] = d_k.astype(BF)
        dqkv_ref[0, :, 2 * width + lo : 2 * width + lo + 128] = pick_heads(dot_tn(low, d_o)).astype(BF)
    d_act = dot_nt(dqkv_ref[0], wqkv_ref[...])
    unit, rstd = norm_parts(x)

    @pl.when(step == 0)
    def _():
        small_ref[...] = jnp.zeros_like(small_ref)
        gtable_ref[...] = jnp.zeros_like(gtable_ref)

    small_ref[0] += fold_rows(d_act * unit)
    small_ref[1] += fold_rows(d_act)
    g = d_mid.astype(F32) + norm_back(unit, rstd, gain_ref[0:1], d_act)
    gin_ref[0] = g
    total = jnp.sum(g, axis=0, keepdims=True)
    rows = lax.broadcasted_iota(jnp.int32, gtable_ref.shape, 0)
    gtable_ref[...] += jnp.where(rows == action, total, 0.0)


def run_spatial_backward(offset, actions, tok, both, qkv, low, table, gain, w_qkv, w_o, filled):
    total, patch, width = tok.shape
    clips = qkv.shape[0]
    frames, _, part, _ = both.shape
    row = lambda c: (c, 0, 0)
    later = lambda c: (c + offset, 0, 0)
    inputs = (actions, tok, both, both, qkv, low, table, gain, w_qkv, w_o)
    return pl.pallas_call(
        functools.partial(spatial_backward, offset),
        grid=(clips,),
        in_specs=[
            pl.BlockSpec(memory_space=SMEM),
            pl.BlockSpec((1, patch, width), later),
            pl.BlockSpec((frames, 1, part, width), lambda c: (0, c, 0, 0)),
            pl.BlockSpec((frames, 1, part, width), lambda c: (0, c + clips, 0, 0)),
            pl.BlockSpec((1, patch, 3 * width), row),
            pl.BlockSpec((1, HEADS // 2, patch, 2 * patch), lambda c: (c, 0, 0, 0)),
            resident(table.shape), resident(gain.shape), resident(w_qkv.shape), resident(w_o.shape),
        ]
        + [pl.BlockSpec(memory_space=pl.ANY)] * len(filled),
        out_specs=[
            pl.BlockSpec((1, patch, 3 * width), later),
            pl.BlockSpec((1, patch, width), later),
            pl.BlockSpec((1, patch, width), later),
            resident((2, 8, width)),
            resident(table.shape),
        ],
        out_shape=[
            jax.ShapeDtypeStruct((total, patch, 3 * width), BF),
            jax.ShapeDtypeStruct((total, patch, width), F32),
            jax.ShapeDtypeStruct((total, patch, width), BF),
            jax.ShapeDtypeStruct((2, 8, width), F32),
            jax.ShapeDtypeStruct(table.shape, F32),
        ],
        input_output_aliases={len(inputs) + i: i for i in range(len(filled))},
        compiler_params=params(),
        cost_estimate=cost(clips * patch * width * width * 14, 6 * clips * MIB),
        name="spatial_backward",
    )(*inputs, *filled)


def choose(core, first, second, keep_ref, send_ref, at):
    for k in range(first.shape[1] // 128):
        cols = slice(k * 128, (k + 1) * 128)
        keep_ref[at, k] = jnp.where(core == 0, first[:, cols], second[:, cols]).astype(BF)
        send_ref[at, k] = jnp.where(core == 0, second[:, cols], first[:, cols]).astype(BF)


def ffn_grads(core_ref, a_ref, b_ref, c_ref, d_ref, keep_ref, send_ref):
    choose(
        core_ref[0], dot_tn(a_ref[...], b_ref[...]), dot_tn(c_ref[...], d_ref[...]), keep_ref, send_ref, 0
    )


def run_ffn_grads(core, act3, d_pre, hid, d_down):
    total, width = act3.shape
    count = d_pre.shape[1] // width
    wide = pl.BlockSpec((total, width), lambda j: (0, j))
    out = pl.BlockSpec((1, width // 128, width, 128), lambda j: (j, 0, 0, 0))
    return pl.pallas_call(
        ffn_grads,
        grid=(count,),
        in_specs=[pl.BlockSpec(memory_space=SMEM), resident(act3.shape), wide, wide, resident(d_down.shape)],
        out_specs=[out, out],
        out_shape=[jax.ShapeDtypeStruct((count, width // 128, width, 128), BF)] * 2,
        compiler_params=params(),
        cost_estimate=cost(4 * total * width * width * count, 16 * MIB),
        name="ffn_grads",
    )(core, act3, d_pre, hid, d_down)


def columns(v):
    return jnp.stack([v[:, k * 128 : (k + 1) * 128] for k in range(v.shape[1] // 128)])


def temporal_grads(act_ref, dqkv_ref, out_ref, dproj_ref, grad_ref):
    width = act_ref.shape[1]
    for j in range(3):
        grad_ref[j] = columns(dot_tn(act_ref[...], dqkv_ref[:, j * width : (j + 1) * width]).astype(BF))
    grad_ref[3] = columns(dot_tn(out_ref[...], dproj_ref[...]).astype(BF))


def run_temporal_grads(act, d_qkv, out, d_proj):
    total, width = act.shape
    return pl.pallas_call(
        temporal_grads,
        out_shape=jax.ShapeDtypeStruct((4, width // 128, width, 128), BF),
        compiler_params=params(),
        cost_estimate=cost(8 * total * width * width, 8 * MIB),
        name="temporal_grads",
    )(act, d_qkv, out, d_proj)


def spatial_grads(core_ref, act0_ref, act1_ref, dqkv_ref, out0_ref, out1_ref, both0_ref, both1_ref, other_ref,
                  sb0_ref, sb1_ref, ub0_ref, ub1_ref, sc0_ref, sc1_ref, gt0_ref, gt1_ref,
                  keep_ref, send_ref, extra_ref):
    core = core_ref[0]
    frames, _, part, width = both0_ref.shape
    flat = lambda ref: ref[...].reshape(-1, width)
    act = jnp.concatenate([flat(act0_ref), flat(act1_ref)], axis=0)
    total = act.shape[0]
    half = out0_ref.shape[0]
    for j in range(4):
        if j < 3:
            grad = dot_tn(act, dqkv_ref[:, :, j * width : (j + 1) * width].reshape(total, width))
        else:
            out = jnp.concatenate([flat(out0_ref), flat(out1_ref)], axis=0)
            d_mid = jnp.concatenate(
                [ref[:, c].reshape(frames * part, width) for ref in (both0_ref, both1_ref) for c in range(half)],
                axis=0,
            )
            grad = dot_tn(out, d_mid)
        grad = columns(grad.astype(BF))
        keep_ref[j] = jnp.where(core == 0, other_ref[j], grad)
        send_ref[j] = jnp.where(core == 0, grad, other_ref[j])
    fold = lambda v: jnp.sum(v, axis=-2, keepdims=True)
    sb = fold(sb0_ref[...] + sb1_ref[...])
    sc = fold(sc0_ref[...] + sc1_ref[...])
    ub = fold(ub0_ref[...] + ub1_ref[...])
    table = gt0_ref[...] + gt1_ref[...]
    norms = jnp.concatenate([sc[0], sb[2], sb[0], sc[1], sb[3], sb[1], jnp.zeros((2, width), F32)], axis=0)
    cut = lambda v: [v[:, k * 128 : (k + 1) * 128] for k in range(v.shape[1] // 128)]
    rows = jnp.concatenate(cut(table) + cut(norms) + cut(ub), axis=0)
    extra_ref[...] = jnp.zeros_like(extra_ref)
    extra_ref[: rows.shape[0]] = rows.astype(BF)


def run_spatial_grads(core, chips, *arrays):
    grad = arrays[7]
    return pl.pallas_call(
        spatial_grads,
        in_specs=[pl.BlockSpec(memory_space=SMEM)] + [pl.BlockSpec(memory_space=pltpu.VMEM)] * len(arrays),
        out_shape=[jax.ShapeDtypeStruct(grad.shape, BF)] * 2 + [jax.ShapeDtypeStruct((chips * 16, 128), BF)],
        compiler_params=params(),
        cost_estimate=cost(8 * 1024 * 512 * 512, 8 * MIB),
        name="spatial_grads",
    )(core, *arrays)


def unpack(main_ref, exp_ref, small_ref, up_ref, down_ref, tqkv_ref, to_ref, sqkv_ref, so_ref,
           table_ref, gain_ref, bias_ref, ub_ref):
    step = pl.program_id(0)
    width = to_ref.shape[0]
    exps = exp_ref[...].astype(F32)
    sides = []
    for c in range(2):
        e = jnp.where(step < 4, exps[:, c, 0:1], exps[:, c, 1:2])
        sides.append((main_ref[:, c].astype(F32) * jnp.exp2(e)).reshape(-1, 128))

    def put(ref, v):
        for k in range(width // 128):
            ref[:, k * 128 : (k + 1) * 128] = v[k * width : (k + 1) * width]

    @pl.when(step == 0)
    def _():
        small = small_ref[...].astype(F32)
        small = small[:, :, :16] * jnp.exp2(small[:, :, 16:])
        rows = (small[:, 0] + small[:, 1]).reshape(-1, 128)
        for k in range(width // 128):
            cols = slice(k * 128, (k + 1) * 128)
            table_ref[:, cols] = rows[8 * k : 8 * k + 8]
            gain_ref[:, cols] = rows[32 + 8 * k : 35 + 8 * k]
            bias_ref[:, cols] = rows[35 + 8 * k : 38 + 8 * k]
        for k in range(ub_ref.shape[1] // 128):
            ub_ref[:, k * 128 : (k + 1) * 128] = rows[64 + k : 65 + k]

    @pl.when(step < 4)
    def _():
        put(up_ref, sides[0])
        put(down_ref, sides[1])

    @pl.when((step >= 4) & (step < 7))
    def _():
        put(tqkv_ref, sides[0])
        put(sqkv_ref, sides[1])

    @pl.when(step == 7)
    def _():
        put(to_ref, sides[0])
        put(so_ref, sides[1])


def run_unpack(whole, width):
    chips, _, _, lanes = whole.shape
    group = chips // 4
    up = lambda j: (0, jnp.minimum(j, 3))
    down = lambda j: (jnp.minimum(j, 3), 0)
    third = lambda j: (0, jnp.clip(j - 4, 0, 2))
    square = (width, width)
    outs = [(width, 4 * width), (4 * width, width)] + [(width, 3 * width), square] * 2
    outs += [(8, width), (3, width), (3, width), (1, 4 * width)]
    return pl.pallas_call(
        unpack,
        grid=(8,),
        in_specs=[
            pl.BlockSpec((group, 2, 128, lanes), lambda j: (j % 4, 0, j // 4, 0)),
            pl.BlockSpec((group, 2, 16, lanes), lambda j: (j % 4, 0, 18, 0)),
            pl.BlockSpec((8, 2, 32, lanes), lambda j: (0, 0, 8, 0), pipeline_mode=pl.Buffered(1)),
        ],
        out_specs=[
            pl.BlockSpec(square, up), pl.BlockSpec(square, down),
            pl.BlockSpec(square, third), resident(square), pl.BlockSpec(square, third), resident(square),
        ]
        + [resident(s) for s in outs[6:]],
        out_shape=[jax.ShapeDtypeStruct(s, F32) for s in outs],
        compiler_params=params(24),
        cost_estimate=cost(MIB, 24 * MIB),
        name="unpack",
    )(whole, whole, whole)


def swap_cores(v):
    return lax.ppermute(v, "c", [(0, 1), (1, 0)])


def after(v, *done):
    return lax.optimization_barrier((v, *done))[0]


def over_frames(v):
    return lax.all_to_all(v, FRAME_AXES, 0, 0)


def over_chips(v):
    return lax.all_to_all(v, CHIP_AXES, 0, 0)


def add_parts(parts):
    return jnp.sum(parts.astype(F32), axis=0)


def add_core(keep, send):
    return (keep.astype(F32) + swap_cores(send).astype(F32)).astype(BF)


def exponent(v, axes):
    most = jnp.max(jnp.abs(v), axis=axes, keepdims=True)
    return jnp.clip(jnp.ceil(jnp.log2(jnp.maximum(most, 1e-37))), -120.0, 120.0)


def scaled(v, axes):
    e = exponent(v, axes)
    return (v * jnp.exp2(-e)).astype(F16), jnp.broadcast_to(e, (e.shape[0], 128)).astype(F16)


def shards(
    frame_tokens, actions, frame_counts, action_table, ln_gain, ln_bias, w_sqkv, w_so, w_tqkv, w_to,
    w_up, b_up, w_down, cotangent,
):
    clips, _, patch, width = frame_tokens.shape
    frames = lax.axis_size(FRAME_AXES)
    chips = lax.axis_size(CHIP_AXES)
    core = lax.axis_index("c").astype(jnp.int32).reshape(1)
    tok = frame_tokens[:, 0]
    acts = actions[:, 0]
    half = clips // 2
    forward = [
        run_spatial_forward(
            frames, i * half, half, acts, tok, cotangent[:, 0], action_table, ln_gain, ln_bias, w_sqkv, w_so
        )
        for i in range(2)
    ]
    there0 = over_frames(forward[0][0])
    there1 = over_frames(after(forward[1][0], there0))
    back = (ln_gain, ln_bias, b_up[None], w_tqkv, w_to, w_up, w_down)
    first = run_temporal(0, clips, frame_counts, there0, *back, 1, ())
    second = run_temporal(half, clips, frame_counts, there1, *back, 1, first[1:9])
    both0 = over_frames(after(first[0], there1))
    both1 = over_frames(after(second[0], both0))
    act_two, d_tqkv, t_out, d_tproj, act_three, d_pre, hidden, d_down = second[1:9]
    lines = lambda v: v.reshape(chips, -1, 128)
    keep, send = run_ffn_grads(core, after(act_three, both0), d_pre, hidden, d_down)
    ffn = add_core(keep, after(send, both1))
    temporal_part = run_temporal_grads(act_two, d_tqkv, t_out, d_tproj)
    ffn_part = add_parts(over_chips(lines(ffn)))

    low = (action_table, ln_gain, w_sqkv, w_so)
    c0 = run_spatial_backward(0, acts, tok, both0, forward[0][1], forward[0][2], *low, ())
    c1 = run_spatial_backward(half, acts, tok, both1, forward[1][1], forward[1][2], *low, c0[:3])
    d_sqkv, grad_input, block_out = c1[:3]
    keep, send, extra = run_spatial_grads(
        core, chips, forward[0][4], forward[1][4], d_sqkv, forward[0][3], forward[1][3], both0, both1, temporal_part,
        first[9], second[9], first[10], second[10], c0[3], c1[3], c0[4], c1[4],
    )
    ffn_rows, ffn_exp = scaled(ffn_part, (0, 1))
    late = jnp.concatenate([lines(add_core(keep, after(send, ffn_rows))), lines(extra)], axis=1)
    late_part = add_parts(over_chips(late))
    each = ffn_part.shape[0]
    late_rows, late_exp = scaled(late_part[:each], (0, 1))
    small_rows, small_exp = scaled(late_part[each:], (1,))
    fill = jnp.zeros((14, 128), F16)
    mine = jnp.concatenate([ffn_rows, late_rows, small_rows, small_exp, ffn_exp, late_exp, fill], axis=0)
    whole = lax.all_gather(mine, (*CHIP_AXES, "c"), axis=0, tiled=True).reshape(chips, 2, -1, 128)
    (grad_up, grad_down, grad_tqkv, grad_to, grad_sqkv, grad_so, grad_table, grad_gain, grad_bias, up_bias) = (
        run_unpack(whole.astype(BF), width)
    )
    return (
        block_out[:, None],
        grad_input[:, None],
        grad_table,
        grad_gain,
        grad_bias,
        grad_sqkv,
        grad_so,
        grad_tqkv,
        grad_to,
        grad_up,
        up_bias.reshape(-1),
        grad_down,
    )


def solution(mesh):
    fine = Mesh(mesh.devices.reshape(4, 2, 2, 4, 2), ("x", "zh", "zl", "y", "c"))
    clip = ("zl", "y", "c")
    tokens = P(clip, FRAME_AXES, None, None)
    in_specs = (tokens, P(clip, FRAME_AXES), P(clip)) + (P(),) * 10 + (tokens,)
    out_specs = (tokens, tokens) + (P(),) * 10
    return jax.shard_map(shards, mesh=fine, in_specs=in_specs, out_specs=out_specs, check_vma=False)
```

```python
import functools
import math

import jax
import jax.numpy as jnp
from jax import lax
from jax.experimental import pallas as pl
from jax.experimental.pallas import tpu as pltpu
from jax.sharding import Mesh, PartitionSpec as P

HEADS = 8
EPS = 1e-05
NEG = -1e30
BF = jnp.bfloat16
F32 = jnp.float32
F16 = jnp.float16
FRAME_AXES = ("x", "zh")
CHIP_AXES = ("x", "zh", "zl", "y")
MIB = 1 << 20
SMEM = pltpu.SMEM


def dot(a, b):
    return jnp.dot(a, b, preferred_element_type=F32)


def dot_nt(a, b):
    return lax.dot_general(a, b, (((1,), (1,)), ((), ())), preferred_element_type=F32)


def dot_tn(a, b):
    return lax.dot_general(a, b, (((0,), (0,)), ((), ())), preferred_element_type=F32)


def norm_parts(v):
    center = v - jnp.mean(v, axis=-1, keepdims=True)
    rstd = lax.rsqrt(jnp.mean(center * center, axis=-1, keepdims=True) + EPS)
    return center * rstd, rstd


def norm_back(unit, rstd, gain, up):
    d_unit = up * gain
    mean_a = jnp.mean(d_unit, axis=-1, keepdims=True)
    mean_b = jnp.mean(d_unit * unit, axis=-1, keepdims=True)
    return rstd * (d_unit - mean_a - unit * mean_b)


def fold_rows(v):
    return jnp.sum(v.reshape(-1, 8, v.shape[-1]), axis=0)


def head_masks(scale):
    lane = lax.broadcasted_iota(jnp.int32, (1, 128), 1)
    first = jnp.where(lane < 64, scale, 0.0).astype(BF)
    second = jnp.where(lane < 64, 0.0, scale).astype(BF)
    return first, second


def split_heads(v, masks):
    return jnp.concatenate([v * masks[0], v * masks[1]], axis=0)


def softmax(s):
    e = jnp.exp(s - jnp.max(s, axis=-1, keepdims=True))
    return e * (1.0 / jnp.sum(e, axis=-1, keepdims=True))


def pick_heads(v):
    half = v.shape[0] // 2
    lane = lax.broadcasted_iota(jnp.int32, (half, 128), 1)
    return jnp.where(lane < 64, v[:half], v[half:])


def small_tn(a, b):
    z = dot(a.T, b)
    n = z.shape[1] // 2
    return jnp.concatenate([z[:64, :n], z[64:, n:]], axis=0).T


def embed(tok_ref, table_ref, action):
    table = table_ref[...].astype(F32)
    rows = lax.broadcasted_iota(jnp.int32, table.shape, 0)
    row = jnp.sum(jnp.where(rows == action, table, 0.0), axis=0, keepdims=True)
    return tok_ref[0].astype(F32) + row


def spatial_forward(offset, actions_ref, tok_ref, cot_ref, table_ref, gain_ref, bias_ref, wqkv_ref, wo_ref,
                    both_ref, qkv_ref, low_ref, out_ref, act_ref):
    x = embed(tok_ref, table_ref, actions_ref[offset + pl.program_id(0)])
    unit, _ = norm_parts(x)
    act = (unit * gain_ref[0:1] + bias_ref[0:1]).astype(BF)
    act_ref[0] = act
    width = x.shape[1]
    qkv_ref[0] = dot(act, wqkv_ref[...]).astype(BF)
    scaled = head_masks(1.0 / math.sqrt(width // HEADS))
    plain = head_masks(1.0)
    n = x.shape[0]
    for pair in range(HEADS // 2):
        at = slice(pair * 128, pair * 128 + 128)
        query = qkv_ref[0, :, pair * 128 : pair * 128 + 128]
        key = qkv_ref[0, :, width + pair * 128 : width + pair * 128 + 128]
        value = qkv_ref[0, :, 2 * width + pair * 128 : 2 * width + pair * 128 + 128]
        s = dot_nt(query, split_heads(key, scaled))
        low_ref[0, pair, :, :n] = softmax(s[:, :n]).astype(BF)
        low_ref[0, pair, :, n:] = softmax(s[:, n:]).astype(BF)
        out_ref[0, :, at] = dot(low_ref[0, pair], split_heads(value, plain)).astype(BF)
    mid = (x + dot(out_ref[0], wo_ref[...])).astype(BF)
    frames, clips, part, _ = both_ref.shape
    step = pl.program_id(0)
    both_ref[:, step] = mid.reshape(frames, part, width)
    both_ref[:, clips // 2 + step] = cot_ref[0].reshape(frames, part, width)


def resident(shape):
    return pl.BlockSpec(shape, lambda *_: (0,) * len(shape), pipeline_mode=pl.Buffered(1))


def params(mib=56):
    return pltpu.CompilerParams(vmem_limit_bytes=mib * MIB)


def cost(flops, nbytes):
    return pl.CostEstimate(flops=int(flops), bytes_accessed=int(nbytes), transcendentals=0)


def run_spatial_forward(frames, offset, clips, actions, tok, cot, table, gain, bias, w_qkv, w_o):
    _, patch, width = tok.shape
    part = patch // frames
    row = lambda c: (c, 0, 0)
    return pl.pallas_call(
        functools.partial(spatial_forward, offset),
        grid=(clips,),
        in_specs=[
            pl.BlockSpec(memory_space=SMEM),
            pl.BlockSpec((1, patch, width), lambda c: (c + offset, 0, 0)),
            pl.BlockSpec((1, patch, width), lambda c: (c + offset, 0, 0)),
            resident(table.shape), resident(gain.shape), resident(bias.shape),
            resident(w_qkv.shape), resident(w_o.shape),
        ],
        out_specs=[
            resident((frames, 2 * clips, part, width)),
            pl.BlockSpec((1, patch, 3 * width), row),
            pl.BlockSpec((1, HEADS // 2, patch, 2 * patch), lambda c: (c, 0, 0, 0)),
            pl.BlockSpec((1, patch, width), row),
            pl.BlockSpec((1, patch, width), row),
        ],
        out_shape=[
            jax.ShapeDtypeStruct((frames, 2 * clips, part, width), BF),
            jax.ShapeDtypeStruct((clips, patch, 3 * width), BF),
            jax.ShapeDtypeStruct((clips, HEADS // 2, patch, 2 * patch), BF),
            jax.ShapeDtypeStruct((clips, patch, width), BF),
            jax.ShapeDtypeStruct((clips, patch, width), BF),
        ],
        compiler_params=params(56),
        cost_estimate=cost(clips * patch * width * width * 10, 4 * clips * MIB),
        name="spatial_forward",
    )(actions, tok, cot, table, gain, bias, w_qkv, w_o)


def rows_of(ref, clip, half, part):
    v = ref[:, clip, half * part : (half + 1) * part, :]
    return v.reshape(-1, v.shape[-1])


def load_rows(ref, clips, part):
    return jnp.concatenate(
        [rows_of(ref, c, h, part) for c in range(clips) for h in range(2)], axis=0
    )


def store_rows(ref, v, first, clips, part):
    frames = ref.shape[0]
    block = frames * part
    for c in range(clips):
        for h in range(2):
            at = (2 * c + h) * block
            ref[:, first + c, h * part : (h + 1) * part, :] = v[at : at + block].reshape(frames, part, v.shape[-1])


def temporal(offset, filled, counts_ref, gain_ref, bias_ref, bup_ref, in_hbm, wqkv_hbm, wo_hbm, wup_hbm, wdown_hbm,
             *rest):
    rest = rest[8:] if filled else rest
    both_hbm, *flat_hbm = rest[:9]
    (small_ref, upbias_ref, mid_ref, cot_ref, wqkv_ref, wo_ref, wup_ref, wdown_ref, both_ref, act2_ref, dqkv_ref,
     tout_ref, dproj_ref, act3_ref, dpre_ref, hid_ref, ddown_ref, qkv_s, low_s, dtout_s, in_sems, out_sems) = rest[9:]
    act2_hbm, dqkv_hbm, tout_hbm, dproj_hbm, act3_hbm, dpre_hbm, hid_hbm, ddown_hbm = flat_hbm
    frames, clips, both, width = mid_ref.shape
    pairs = [
        (in_hbm.at[:, :clips], mid_ref), (wqkv_hbm, wqkv_ref), (wo_hbm, wo_ref), (in_hbm.at[:, clips:], cot_ref),
        (wup_hbm, wup_ref), (wdown_hbm, wdown_ref),
    ]
    loads = [pltpu.make_async_copy(*p, in_sems.at[i]) for i, p in enumerate(pairs)]
    for load in loads:
        load.start()
    stores = []
    mine = pl.ds(offset * frames * both, clips * frames * both)

    def store(source, target):
        c = pltpu.make_async_copy(source, target, out_sems.at[len(stores)])
        c.start()
        stores.append(c)

    loads[0].wait()
    part = both // 2
    block = frames * part
    x = load_rows(mid_ref, clips, part).astype(F32)
    rows = x.shape[0]
    unit2, rstd2 = norm_parts(x)
    act2 = (unit2 * gain_ref[1:2] + bias_ref[1:2]).astype(BF)
    act2_ref[...] = act2
    store(act2_ref, act2_hbm.at[mine])
    loads[1].wait()
    qkv_s[...] = dot(act2, wqkv_ref[...]).astype(BF)
    scaled = head_masks(1.0 / math.sqrt(width // HEADS))
    plain = head_masks(1.0)
    r = lax.broadcasted_iota(jnp.int32, (block, block), 0)
    s = lax.broadcasted_iota(jnp.int32, (block, block), 1)
    base = (r % part == s % part) & (s // part <= r // part)
    row_mask = []
    for c in range(clips):
        count = counts_ref[offset + c]
        allowed = base & (s // part < count)
        row_mask.append(count)
        for h in range(2):
            b = 2 * c + h
            at = slice(b * block, (b + 1) * block)
            for pair in range(HEADS // 2):
                lo = pair * 128
                query = qkv_s[at, lo : lo + 128]
                key = qkv_s[at, width + lo : width + lo + 128]
                value = qkv_s[at, 2 * width + lo : 2 * width + lo + 128]
                scores = dot_nt(query, split_heads(key, scaled))
                for k in range(2):
                    sc = jnp.where(allowed, scores[:, k * block : (k + 1) * block], NEG)
                    low_s[b, pair, :, k * block : (k + 1) * block] = softmax(sc).astype(BF)
                tout_ref[at, lo : lo + 128] = dot(low_s[b, pair], split_heads(value, plain)).astype(BF)
    store(tout_ref, tout_hbm.at[mine])
    loads[2].wait()
    late = x + dot(tout_ref[...], wo_ref[...])
    unit3, rstd3 = norm_parts(late)
    act3 = (unit3 * gain_ref[2:3] + bias_ref[2:3]).astype(BF)
    act3_ref[...] = act3
    store(act3_ref, act3_hbm.at[mine])
    loads[3].wait()
    frame_of = lax.broadcasted_iota(jnp.int32, (block, width), 0) // part
    d_out = load_rows(cot_ref, clips, part)
    d_out = jnp.concatenate(
        [
            jnp.where(frame_of < row_mask[b // 2], d_out[b * block : (b + 1) * block].astype(F32), 0.0)
            for b in range(2 * clips)
        ],
        axis=0,
    )
    d_down = d_out.astype(BF)
    ddown_ref[...] = d_down
    store(ddown_ref, ddown_hbm.at[mine])
    out = late
    d_act3 = None
    loads[4].wait()
    loads[5].wait()
    k0 = math.sqrt(2.0 / math.pi)
    k1 = 0.044715
    for j in range(2):
        cols = slice(j * 2 * width, (j + 1) * 2 * width)
        u = dot(act3, wup_ref[:, cols]) + bup_ref[0:1, cols]
        sq = u * u
        t = jnp.tanh(k0 * u * (1.0 + k1 * sq))
        half_t = 0.5 + 0.5 * t
        hid = (u * half_t).astype(BF)
        slope = half_t + 0.5 * u * (1.0 - t * t) * (k0 + (3.0 * k0 * k1) * sq)
        hid_ref[:, cols] = hid
        store(hid_ref.at[:, cols], hid_hbm.at[mine, cols])
        out = out + dot(hid, wdown_ref[cols, :])
        d_pre32 = dot_nt(d_down, wdown_ref[cols, :]) * slope
        d_pre = d_pre32.astype(BF)
        dpre_ref[:, cols] = d_pre
        store(dpre_ref.at[:, cols], dpre_hbm.at[mine, cols])
        upbias_ref[:, cols] = fold_rows(d_pre.astype(F32))
        more = dot_nt(d_pre, wup_ref[:, cols])
        d_act3 = more if d_act3 is None else d_act3 + more
    store_rows(both_ref, out.astype(BF), clips, clips, part)
    store(both_ref.at[:, clips:], both_hbm.at[:, clips:])
    small_ref[0] = fold_rows(d_act3 * unit3)
    small_ref[1] = fold_rows(d_act3)
    d_late = d_out + norm_back(unit3, rstd3, gain_ref[2:3], d_act3)
    d_proj = d_late.astype(BF)
    dproj_ref[...] = d_proj
    store(dproj_ref, dproj_hbm.at[mine])
    dtout_s[...] = dot_nt(d_proj, wo_ref[...]).astype(BF)
    for b in range(2 * clips):
        at = slice(b * block, (b + 1) * block)
        for pair in range(HEADS // 2):
            lo = pair * 128
            query = qkv_s[at, lo : lo + 128]
            key = qkv_s[at, width + lo : width + lo + 128]
            value = qkv_s[at, 2 * width + lo : 2 * width + lo + 128]
            d_o = dtout_s[at, lo : lo + 128]
            d_p = dot_nt(d_o, split_heads(value, plain))
            low = low_s[b, pair]
            ds = []
            for k in range(2):
                cols = slice(k * block, (k + 1) * block)
                p = low[:, cols].astype(F32)
                pd = p * d_p[:, cols]
                ds.append((pd - p * jnp.sum(pd, axis=-1, keepdims=True)).astype(BF))
            d_s = jnp.concatenate(ds, axis=1)
            dqkv_ref[at, lo : lo + 128] = dot(d_s, split_heads(key, scaled)).astype(BF)
            d_k = pick_heads(dot_tn(d_s, query)) * (1.0 / math.sqrt(width // HEADS))
            dqkv_ref[at, width + lo : width + lo + 128] = d_k.astype(BF)
            d_v = pick_heads(dot_tn(low, d_o))
            dqkv_ref[at, 2 * width + lo : 2 * width + lo + 128] = d_v.astype(BF)
    store(dqkv_ref, dqkv_hbm.at[mine])
    d_act2 = dot_nt(dqkv_ref[...], wqkv_ref[...])
    small_ref[2] = fold_rows(d_act2 * unit2)
    small_ref[3] = fold_rows(d_act2)
    d_mid = d_late + norm_back(unit2, rstd2, gain_ref[1:2], d_act2)
    store_rows(both_ref, d_mid.astype(BF), 0, clips, part)
    store(both_ref.at[:, :clips], both_hbm.at[:, :clips])
    for c in stores:
        c.wait()


def run_temporal(offset, total_clips, counts, both_in, gain, bias, b_up, w_qkv, w_o, w_up, w_down, filled):
    frames, clips, both, width = both_in.shape
    clips //= 2
    hidden = w_up.shape[1]
    rows = clips * frames * both
    total = total_clips * frames * both
    widths = (width, 3 * width, width, width, width, hidden, hidden, width)
    small = (counts, gain, bias, b_up)
    large = (both_in, w_qkv, w_o, w_up, w_down)
    hbm = pl.BlockSpec(memory_space=pl.ANY)
    vmem = pl.BlockSpec(memory_space=pltpu.VMEM)
    half = (frames, clips, both, width)
    return pl.pallas_call(
        functools.partial(temporal, offset, bool(filled)),
        in_specs=[pl.BlockSpec(memory_space=SMEM)] + [vmem] * 3 + [hbm] * (len(large) + len(filled)),
        out_specs=[hbm] * 9 + [vmem] * 2,
        out_shape=[jax.ShapeDtypeStruct(both_in.shape, BF)]
        + [jax.ShapeDtypeStruct((total, w), BF) for w in widths]
        + [jax.ShapeDtypeStruct((4, 8, width), F32), jax.ShapeDtypeStruct((8, hidden), F32)],
        scratch_shapes=[pltpu.VMEM(half, BF)] * 2
        + [pltpu.VMEM(w.shape, BF) for w in large[1:]]
        + [pltpu.VMEM(both_in.shape, BF)]
        + [pltpu.VMEM((rows, w), BF) for w in widths]
        + [
            pltpu.VMEM((rows, 3 * width), BF),
            pltpu.VMEM((2 * clips, HEADS // 2, rows // (2 * clips), rows // clips), BF),
            pltpu.VMEM((rows, width), BF),
            pltpu.SemaphoreType.DMA((6,)),
            pltpu.SemaphoreType.DMA((12,)),
        ],
        input_output_aliases={len(small) + len(large) + i: 1 + i for i in range(len(filled))},
        compiler_params=params(),
        cost_estimate=cost(clips * frames * both * width * width * 40, 8 * clips * MIB),
        name="temporal",
    )(*small, *large, *filled)


def spatial_backward(offset, actions_ref, tok_ref, dmid_ref, done_ref, qkv_ref, low_ref, table_ref, gain_ref, wqkv_ref, wo_ref,
                     *rest):
    dqkv_ref, gin_ref, block_ref, small_ref, gtable_ref = rest[-5:]
    step = pl.program_id(0)
    action = actions_ref[offset + step]
    x = embed(tok_ref, table_ref, action)
    n, width = x.shape
    d_mid = dmid_ref[:, 0].reshape(n, width)
    block_ref[0] = done_ref[:, 0].reshape(n, width)
    d_out = dot_nt(d_mid, wo_ref[...]).astype(BF)
    scaled = head_masks(1.0 / math.sqrt(width // HEADS))
    plain = head_masks(1.0)
    for pair in range(HEADS // 2):
        lo = pair * 128
        query = qkv_ref[0, :, lo : lo + 128]
        key = qkv_ref[0, :, width + lo : width + lo + 128]
        value = qkv_ref[0, :, 2 * width + lo : 2 * width + lo + 128]
        d_o = d_out[:, lo : lo + 128]
        d_p = dot_nt(d_o, split_heads(value, plain))
        low = low_ref[0, pair]
        ds = []
        for k in range(2):
            cols = slice(k * n, (k + 1) * n)
            p = low[:, cols].astype(F32)
            pd = p * d_p[:, cols]
            ds.append((pd - p * jnp.sum(pd, axis=-1, keepdims=True)).astype(BF))
        d_s = jnp.concatenate(ds, axis=1)
        dqkv_ref[0, :, lo : lo + 128] = dot(d_s, split_heads(key, scaled)).astype(BF)
        d_k = small_tn(query, d_s) * (1.0 / math.sqrt(width // HEADS))
        dqkv_ref[0, :, width + lo : width + lo + 128] = d_k.astype(BF)
        dqkv_ref[0, :, 2 * width + lo : 2 * width + lo + 128] = small_tn(d_o, low).astype(BF)
    d_act = dot_nt(dqkv_ref[0], wqkv_ref[...])
    unit, rstd = norm_parts(x)

    @pl.when(step == 0)
    def _():
        small_ref[...] = jnp.zeros_like(small_ref)
        gtable_ref[...] = jnp.zeros_like(gtable_ref)

    small_ref[0] += fold_rows(d_act * unit)
    small_ref[1] += fold_rows(d_act)
    g = d_mid.astype(F32) + norm_back(unit, rstd, gain_ref[0:1], d_act)
    gin_ref[0] = g
    total = jnp.sum(g, axis=0, keepdims=True)
    rows = lax.broadcasted_iota(jnp.int32, gtable_ref.shape, 0)
    gtable_ref[...] += jnp.where(rows == action, total, 0.0)


def run_spatial_backward(offset, actions, tok, both, qkv, low, table, gain, w_qkv, w_o, filled):
    total, patch, width = tok.shape
    clips = qkv.shape[0]
    frames, _, part, _ = both.shape
    row = lambda c: (c, 0, 0)
    later = lambda c: (c + offset, 0, 0)
    inputs = (actions, tok, both, both, qkv, low, table, gain, w_qkv, w_o)
    return pl.pallas_call(
        functools.partial(spatial_backward, offset),
        grid=(clips,),
        in_specs=[
            pl.BlockSpec(memory_space=SMEM),
            pl.BlockSpec((1, patch, width), later),
            pl.BlockSpec((frames, 1, part, width), lambda c: (0, c, 0, 0)),
            pl.BlockSpec((frames, 1, part, width), lambda c: (0, c + clips, 0, 0)),
            pl.BlockSpec((1, patch, 3 * width), row),
            pl.BlockSpec((1, HEADS // 2, patch, 2 * patch), lambda c: (c, 0, 0, 0)),
            resident(table.shape), resident(gain.shape), resident(w_qkv.shape), resident(w_o.shape),
        ]
        + [pl.BlockSpec(memory_space=pl.ANY)] * len(filled),
        out_specs=[
            pl.BlockSpec((1, patch, 3 * width), later),
            pl.BlockSpec((1, patch, width), later),
            pl.BlockSpec((1, patch, width), later),
            resident((2, 8, width)),
            resident(table.shape),
        ],
        out_shape=[
            jax.ShapeDtypeStruct((total, patch, 3 * width), BF),
            jax.ShapeDtypeStruct((total, patch, width), F32),
            jax.ShapeDtypeStruct((total, patch, width), BF),
            jax.ShapeDtypeStruct((2, 8, width), F32),
            jax.ShapeDtypeStruct(table.shape, F32),
        ],
        input_output_aliases={len(inputs) + i: i for i in range(len(filled))},
        compiler_params=params(56),
        cost_estimate=cost(clips * patch * width * width * 14, 6 * clips * MIB),
        name="spatial_backward",
    )(*inputs, *filled)


def choose(core, first, second, keep_ref, send_ref, at):
    for k in range(first.shape[1] // 128):
        cols = slice(k * 128, (k + 1) * 128)
        keep_ref[at, k] = jnp.where(core == 0, first[:, cols], second[:, cols]).astype(BF)
        send_ref[at, k] = jnp.where(core == 0, second[:, cols], first[:, cols]).astype(BF)


def ffn_grads(core_ref, a_ref, b_ref, c_ref, d_ref, keep_ref, send_ref):
    choose(
        core_ref[0], dot_tn(a_ref[...], b_ref[...]), dot_tn(c_ref[...], d_ref[...]), keep_ref, send_ref, 0
    )


def run_ffn_grads(core, act3, d_pre, hid, d_down):
    total, width = act3.shape
    count = d_pre.shape[1] // width
    wide = pl.BlockSpec((total, width), lambda j: (0, j))
    out = pl.BlockSpec((1, width // 128, width, 128), lambda j: (j, 0, 0, 0))
    return pl.pallas_call(
        ffn_grads,
        grid=(count,),
        in_specs=[pl.BlockSpec(memory_space=SMEM), resident(act3.shape), wide, wide, resident(d_down.shape)],
        out_specs=[out, out],
        out_shape=[jax.ShapeDtypeStruct((count, width // 128, width, 128), BF)] * 2,
        compiler_params=params(),
        cost_estimate=cost(4 * total * width * width * count, 16 * MIB),
        name="ffn_grads",
    )(core, act3, d_pre, hid, d_down)


def columns(v):
    return jnp.stack([v[:, k * 128 : (k + 1) * 128] for k in range(v.shape[1] // 128)])


def temporal_grads(act_ref, dqkv_ref, out_ref, dproj_ref, grad_ref):
    width = act_ref.shape[1]
    for j in range(3):
        grad_ref[j] = columns(dot_tn(act_ref[...], dqkv_ref[:, j * width : (j + 1) * width]).astype(BF))
    grad_ref[3] = columns(dot_tn(out_ref[...], dproj_ref[...]).astype(BF))


def run_temporal_grads(act, d_qkv, out, d_proj):
    total, width = act.shape
    return pl.pallas_call(
        temporal_grads,
        out_shape=jax.ShapeDtypeStruct((4, width // 128, width, 128), BF),
        compiler_params=params(),
        cost_estimate=cost(8 * total * width * width, 8 * MIB),
        name="temporal_grads",
    )(act, d_qkv, out, d_proj)


def spatial_grads(core_ref, act0_ref, act1_ref, dqkv_ref, out0_ref, out1_ref, both0_ref, both1_ref, other_ref,
                  sb0_ref, sb1_ref, ub0_ref, ub1_ref, sc0_ref, sc1_ref, gt0_ref, gt1_ref,
                  keep_ref, send_ref, extra_ref):
    core = core_ref[0]
    frames, _, part, width = both0_ref.shape
    flat = lambda ref: ref[...].reshape(-1, width)
    act = jnp.concatenate([flat(act0_ref), flat(act1_ref)], axis=0)
    total = act.shape[0]
    half = out0_ref.shape[0]
    for j in range(4):
        if j < 3:
            grad = dot_tn(act, dqkv_ref[:, :, j * width : (j + 1) * width].reshape(total, width))
        else:
            out = jnp.concatenate([flat(out0_ref), flat(out1_ref)], axis=0)
            d_mid = jnp.concatenate(
                [ref[:, c].reshape(frames * part, width) for ref in (both0_ref, both1_ref) for c in range(half)],
                axis=0,
            )
            grad = dot_tn(out, d_mid)
        grad = columns(grad.astype(BF))
        keep_ref[j] = jnp.where(core == 0, other_ref[j], grad)
        send_ref[j] = jnp.where(core == 0, grad, other_ref[j])
    fold = lambda v: jnp.sum(v, axis=-2, keepdims=True)
    sb = fold(sb0_ref[...] + sb1_ref[...])
    sc = fold(sc0_ref[...] + sc1_ref[...])
    ub = fold(ub0_ref[...] + ub1_ref[...])
    table = gt0_ref[...] + gt1_ref[...]
    norms = jnp.concatenate([sc[0], sb[2], sb[0], sc[1], sb[3], sb[1], jnp.zeros((2, width), F32)], axis=0)
    cut = lambda v: [v[:, k * 128 : (k + 1) * 128] for k in range(v.shape[1] // 128)]
    rows = jnp.concatenate(cut(table) + cut(norms) + cut(ub), axis=0)
    extra_ref[...] = jnp.zeros_like(extra_ref)
    extra_ref[: rows.shape[0]] = rows.astype(BF)


def run_spatial_grads(core, chips, *arrays):
    grad = arrays[7]
    return pl.pallas_call(
        spatial_grads,
        in_specs=[pl.BlockSpec(memory_space=SMEM)] + [pl.BlockSpec(memory_space=pltpu.VMEM)] * len(arrays),
        out_shape=[jax.ShapeDtypeStruct(grad.shape, BF)] * 2 + [jax.ShapeDtypeStruct((chips * 16, 128), BF)],
        compiler_params=params(),
        cost_estimate=cost(8 * 1024 * 512 * 512, 8 * MIB),
        name="spatial_grads",
    )(core, *arrays)


def unpack(main_ref, exp_ref, small_ref, up_ref, down_ref, tqkv_ref, to_ref, sqkv_ref, so_ref,
           table_ref, gain_ref, bias_ref, ub_ref):
    step = pl.program_id(0)
    width = to_ref.shape[0]
    exps = exp_ref[...].astype(F32)
    sides = []
    for c in range(2):
        e = jnp.where(step < 4, exps[:, c, 0:1], exps[:, c, 1:2])
        sides.append((main_ref[:, c].astype(F32) * jnp.exp2(e)).reshape(-1, 128))

    def put(ref, v):
        for k in range(width // 128):
            ref[:, k * 128 : (k + 1) * 128] = v[k * width : (k + 1) * width]

    @pl.when(step == 0)
    def _():
        small = small_ref[...].astype(F32)
        small = small[:, :, :16] * jnp.exp2(small[:, :, 16:])
        rows = (small[:, 0] + small[:, 1]).reshape(-1, 128)
        for k in range(width // 128):
            cols = slice(k * 128, (k + 1) * 128)
            table_ref[:, cols] = rows[8 * k : 8 * k + 8]
            gain_ref[:, cols] = rows[32 + 8 * k : 35 + 8 * k]
            bias_ref[:, cols] = rows[35 + 8 * k : 38 + 8 * k]
        for k in range(ub_ref.shape[1] // 128):
            ub_ref[:, k * 128 : (k + 1) * 128] = rows[64 + k : 65 + k]

    @pl.when(step < 4)
    def _():
        put(up_ref, sides[0])
        put(down_ref, sides[1])

    @pl.when((step >= 4) & (step < 7))
    def _():
        put(tqkv_ref, sides[0])
        put(sqkv_ref, sides[1])

    @pl.when(step == 7)
    def _():
        put(to_ref, sides[0])
        put(so_ref, sides[1])


def run_unpack(whole, width):
    chips, _, _, lanes = whole.shape
    group = chips // 4
    up = lambda j: (0, jnp.minimum(j, 3))
    down = lambda j: (jnp.minimum(j, 3), 0)
    third = lambda j: (0, jnp.clip(j - 4, 0, 2))
    square = (width, width)
    outs = [(width, 4 * width), (4 * width, width)] + [(width, 3 * width), square] * 2
    outs += [(8, width), (3, width), (3, width), (1, 4 * width)]
    return pl.pallas_call(
        unpack,
        grid=(8,),
        in_specs=[
            pl.BlockSpec((group, 2, 128, lanes), lambda j: (j % 4, 0, j // 4, 0)),
            pl.BlockSpec((group, 2, 16, lanes), lambda j: (j % 4, 0, 18, 0)),
            pl.BlockSpec((8, 2, 32, lanes), lambda j: (0, 0, 8, 0), pipeline_mode=pl.Buffered(1)),
        ],
        out_specs=[
            pl.BlockSpec(square, up), pl.BlockSpec(square, down),
            pl.BlockSpec(square, third), resident(square), pl.BlockSpec(square, third), resident(square),
        ]
        + [resident(s) for s in outs[6:]],
        out_shape=[jax.ShapeDtypeStruct(s, F32) for s in outs],
        compiler_params=params(24),
        cost_estimate=cost(MIB, 24 * MIB),
        name="unpack",
    )(whole, whole, whole)


def swap_cores(v):
    return lax.ppermute(v, "c", [(0, 1), (1, 0)])


def after(v, *done):
    return lax.optimization_barrier((v, *done))[0]


def over_frames(v):
    return lax.all_to_all(v, FRAME_AXES, 0, 0)


def over_chips(v):
    return lax.all_to_all(v, CHIP_AXES, 0, 0)


def add_parts(parts):
    return jnp.sum(parts.astype(F32), axis=0)


def add_core(keep, send):
    return (keep.astype(F32) + swap_cores(send).astype(F32)).astype(BF)


def exponent(v, axes):
    most = jnp.max(jnp.abs(v), axis=axes, keepdims=True)
    return jnp.clip(jnp.ceil(jnp.log2(jnp.maximum(most, 1e-37))), -120.0, 120.0)


def scaled(v, axes):
    e = exponent(v, axes)
    return (v * jnp.exp2(-e)).astype(F16), jnp.broadcast_to(e, (e.shape[0], 128)).astype(F16)


def shards(
    frame_tokens, actions, frame_counts, action_table, ln_gain, ln_bias, w_sqkv, w_so, w_tqkv, w_to,
    w_up, b_up, w_down, cotangent,
):
    clips, _, patch, width = frame_tokens.shape
    frames = lax.axis_size(FRAME_AXES)
    chips = lax.axis_size(CHIP_AXES)
    core = lax.axis_index("c").astype(jnp.int32).reshape(1)
    tok = frame_tokens[:, 0]
    acts = actions[:, 0]
    half = clips // 2
    forward = [
        run_spatial_forward(
            frames, i * half, half, acts, tok, cotangent[:, 0], action_table, ln_gain, ln_bias, w_sqkv, w_so
        )
        for i in range(2)
    ]
    there0 = over_frames(forward[0][0])
    there1 = over_frames(after(forward[1][0], there0))
    back = (ln_gain, ln_bias, b_up[None], w_tqkv, w_to, w_up, w_down)
    first = run_temporal(0, clips, frame_counts, there0, *back, ())
    second = run_temporal(half, clips, frame_counts, there1, *back, first[1:9])
    both0 = over_frames(after(first[0], there1))
    both1 = over_frames(after(second[0], both0))
    act_two, d_tqkv, t_out, d_tproj, act_three, d_pre, hidden, d_down = second[1:9]
    lines = lambda v: v.reshape(chips, -1, 128)
    keep, send = run_ffn_grads(core, after(act_three, both0), d_pre, hidden, d_down)
    ffn = add_core(keep, after(send, both1))
    temporal_part = run_temporal_grads(act_two, d_tqkv, t_out, d_tproj)
    ffn_part = add_parts(over_chips(lines(ffn)))

    low = (action_table, ln_gain, w_sqkv, w_so)
    c0 = run_spatial_backward(0, acts, tok, both0, forward[0][1], forward[0][2], *low, ())
    c1 = run_spatial_backward(half, acts, tok, both1, forward[1][1], forward[1][2], *low, c0[:3])
    d_sqkv, grad_input, block_out = c1[:3]
    keep, send, extra = run_spatial_grads(
        core, chips, forward[0][4], forward[1][4], d_sqkv, forward[0][3], forward[1][3], both0, both1, temporal_part,
        first[9], second[9], first[10], second[10], c0[3], c1[3], c0[4], c1[4],
    )
    ffn_rows, ffn_exp = scaled(ffn_part, (0, 1))
    late = jnp.concatenate([lines(add_core(keep, after(send, ffn_rows))), lines(extra)], axis=1)
    late_part = add_parts(over_chips(late))
    each = ffn_part.shape[0]
    late_rows, late_exp = scaled(late_part[:each], (0, 1))
    small_rows, small_exp = scaled(late_part[each:], (1,))
    fill = jnp.zeros((14, 128), F16)
    mine = jnp.concatenate([ffn_rows, late_rows, small_rows, small_exp, ffn_exp, late_exp, fill], axis=0)
    whole = lax.all_gather(mine, (*CHIP_AXES, "c"), axis=0, tiled=True).reshape(chips, 2, -1, 128)
    (grad_up, grad_down, grad_tqkv, grad_to, grad_sqkv, grad_so, grad_table, grad_gain, grad_bias, up_bias) = (
        run_unpack(whole.astype(BF), width)
    )
    return (
        block_out[:, None],
        grad_input[:, None],
        grad_table,
        grad_gain,
        grad_bias,
        grad_sqkv,
        grad_so,
        grad_tqkv,
        grad_to,
        grad_up,
        up_bias.reshape(-1),
        grad_down,
    )


def solution(mesh):
    fine = Mesh(mesh.devices.reshape(4, 2, 2, 4, 2), ("x", "zh", "zl", "y", "c"))
    clip = ("zl", "y", "c")
    tokens = P(clip, FRAME_AXES, None, None)
    in_specs = (tokens, P(clip, FRAME_AXES), P(clip)) + (P(),) * 10 + (tokens,)
    out_specs = (tokens, tokens) + (P(),) * 10
    return jax.shard_map(shards, mesh=fine, in_specs=in_specs, out_specs=out_specs, check_vma=False)
```

```python
import functools
import math

import jax
import jax.numpy as jnp
from jax import lax
from jax.experimental import pallas as pl
from jax.experimental.pallas import tpu as pltpu
from jax.sharding import Mesh, PartitionSpec as P

HEADS = 8
EPS = 1e-05
NEG = -1e30
BF = jnp.bfloat16
F32 = jnp.float32
F16 = jnp.float16
FRAME_AXES = ("x", "zh")
CHIP_AXES = ("x", "zh", "zl", "y")
MIB = 1 << 20
SMEM = pltpu.SMEM


def dot(a, b):
    return jnp.dot(a, b, preferred_element_type=F32)


def dot_nt(a, b):
    return lax.dot_general(a, b, (((1,), (1,)), ((), ())), preferred_element_type=F32)


def dot_tn(a, b):
    return lax.dot_general(a, b, (((0,), (0,)), ((), ())), preferred_element_type=F32)


def norm_parts(v):
    center = v - jnp.mean(v, axis=-1, keepdims=True)
    rstd = lax.rsqrt(jnp.mean(center * center, axis=-1, keepdims=True) + EPS)
    return center * rstd, rstd


def norm_back(unit, rstd, gain, up):
    d_unit = up * gain
    mean_a = jnp.mean(d_unit, axis=-1, keepdims=True)
    mean_b = jnp.mean(d_unit * unit, axis=-1, keepdims=True)
    return rstd * (d_unit - mean_a - unit * mean_b)


def fold_rows(v):
    return jnp.sum(v.reshape(-1, 8, v.shape[-1]), axis=0)


def head_masks(scale):
    lane = lax.broadcasted_iota(jnp.int32, (1, 128), 1)
    first = jnp.where(lane < 64, scale, 0.0).astype(BF)
    second = jnp.where(lane < 64, 0.0, scale).astype(BF)
    return first, second


def split_heads(v, masks):
    return jnp.concatenate([v * masks[0], v * masks[1]], axis=0)


def softmax(s):
    e = jnp.exp(s - jnp.max(s, axis=-1, keepdims=True))
    return e * (1.0 / jnp.sum(e, axis=-1, keepdims=True))


def pick_heads(v):
    half = v.shape[0] // 2
    lane = lax.broadcasted_iota(jnp.int32, (half, 128), 1)
    return jnp.where(lane < 64, v[:half], v[half:])


def small_tn(a, b):
    z = dot(a.T, b)
    n = z.shape[1] // 2
    return jnp.concatenate([z[:64, :n], z[64:, n:]], axis=0).T


def embed(tok_ref, table_ref, action):
    table = table_ref[...].astype(F32)
    rows = lax.broadcasted_iota(jnp.int32, table.shape, 0)
    row = jnp.sum(jnp.where(rows == action, table, 0.0), axis=0, keepdims=True)
    return tok_ref[0].astype(F32) + row


def spatial_forward(offset, actions_ref, table_ref, gain_ref, bias_ref, tok_hbm, cot_hbm, wqkv_hbm, wo_hbm,
                    both_hbm, qkv_hbm, low_hbm, out_hbm, act_hbm,
                    tok_ref, cot_ref, wqkv_ref, wo_ref, both_ref, qkv_ref, low_ref, out_ref, act_ref,
                    in_sems, out_sems):
    clips, n, width = tok_ref.shape
    frames, _, part, _ = both_ref.shape
    mine = pl.ds(offset, clips)
    pairs = [(tok_hbm.at[mine], tok_ref), (wqkv_hbm, wqkv_ref), (cot_hbm.at[mine], cot_ref), (wo_hbm, wo_ref)]
    loads = [pltpu.make_async_copy(*p, in_sems.at[i]) for i, p in enumerate(pairs)]
    for load in loads:
        load.start()
    stores = []

    def store(source, target):
        c = pltpu.make_async_copy(source, target, out_sems.at[len(stores)])
        c.start()
        stores.append(c)

    loads[0].wait()
    x = jnp.concatenate(
        [embed(tok_ref.at[pl.ds(c, 1)], table_ref, actions_ref[offset + c]) for c in range(clips)], axis=0
    )
    unit, _ = norm_parts(x)
    act = (unit * gain_ref[0:1] + bias_ref[0:1]).astype(BF)
    act_ref[...] = act.reshape(act_ref.shape)
    store(act_ref, act_hbm)
    loads[1].wait()
    qkv_ref[...] = dot(act, wqkv_ref[...]).astype(BF).reshape(qkv_ref.shape)
    store(qkv_ref, qkv_hbm)
    loads[2].wait()
    for c in range(clips):
        both_ref[:, clips + c] = cot_ref[c].reshape(frames, part, width)
    store(both_ref.at[:, clips:], both_hbm.at[:, clips:])
    scaled = head_masks(1.0 / math.sqrt(width // HEADS))
    plain = head_masks(1.0)
    for c in range(clips):
        for pair in range(HEADS // 2):
            lo = pair * 128
            query = qkv_ref[c, :, lo : lo + 128]
            key = qkv_ref[c, :, width + lo : width + lo + 128]
            value = qkv_ref[c, :, 2 * width + lo : 2 * width + lo + 128]
            s = dot_nt(query, split_heads(key, scaled))
            low_ref[c, pair, :, :n] = softmax(s[:, :n]).astype(BF)
            low_ref[c, pair, :, n:] = softmax(s[:, n:]).astype(BF)
            out_ref[c, :, lo : lo + 128] = dot(low_ref[c, pair], split_heads(value, plain)).astype(BF)
        store(low_ref.at[c], low_hbm.at[c])
    store(out_ref, out_hbm)
    loads[3].wait()
    mid = (x + dot(out_ref[...].reshape(clips * n, width), wo_ref[...])).astype(BF)
    for c in range(clips):
        both_ref[:, c] = mid[c * n : (c + 1) * n].reshape(frames, part, width)
    store(both_ref.at[:, :clips], both_hbm.at[:, :clips])
    for c in stores:
        c.wait()


def resident(shape):
    return pl.BlockSpec(shape, lambda *_: (0,) * len(shape), pipeline_mode=pl.Buffered(1))


def params(mib=56):
    return pltpu.CompilerParams(vmem_limit_bytes=mib * MIB)


def cost(flops, nbytes):
    return pl.CostEstimate(flops=int(flops), bytes_accessed=int(nbytes), transcendentals=0)


def run_spatial_forward(frames, offset, clips, actions, tok, cot, table, gain, bias, w_qkv, w_o):
    _, patch, width = tok.shape
    part = patch // frames
    hbm = pl.BlockSpec(memory_space=pl.ANY)
    vmem = pl.BlockSpec(memory_space=pltpu.VMEM)
    rows = (clips, patch, width)
    outs = [
        (frames, 2 * clips, part, width), (clips, patch, 3 * width), (clips, HEADS // 2, patch, 2 * patch), rows, rows,
    ]
    return pl.pallas_call(
        functools.partial(spatial_forward, offset),
        in_specs=[pl.BlockSpec(memory_space=SMEM)] + [vmem] * 3 + [hbm] * 4,
        out_specs=[hbm] * 5,
        out_shape=[jax.ShapeDtypeStruct(o, BF) for o in outs],
        scratch_shapes=[pltpu.VMEM(v, BF) for v in (rows, rows, w_qkv.shape, w_o.shape, *outs)]
        + [pltpu.SemaphoreType.DMA((4,)), pltpu.SemaphoreType.DMA((5 + clips,))],
        compiler_params=params(),
        cost_estimate=cost(clips * patch * width * width * 10, 4 * clips * MIB),
        name="spatial_forward",
    )(actions, table, gain, bias, tok, cot, w_qkv, w_o)


def rows_of(ref, clip, half, part):
    v = ref[:, clip, half * part : (half + 1) * part, :]
    return v.reshape(-1, v.shape[-1])


def load_rows(ref, clips, part):
    return jnp.concatenate(
        [rows_of(ref, c, h, part) for c in range(clips) for h in range(2)], axis=0
    )


def store_rows(ref, v, first, clips, part):
    frames = ref.shape[0]
    block = frames * part
    for c in range(clips):
        for h in range(2):
            at = (2 * c + h) * block
            ref[:, first + c, h * part : (h + 1) * part, :] = v[at : at + block].reshape(frames, part, v.shape[-1])


def temporal(offset, filled, counts_ref, gain_ref, bias_ref, bup_ref, in_hbm, wqkv_hbm, wo_hbm, wup_hbm, wdown_hbm,
             *rest):
    rest = rest[8:] if filled else rest
    both_hbm, *flat_hbm = rest[:9]
    (small_ref, upbias_ref, mid_ref, cot_ref, wqkv_ref, wo_ref, wup_ref, wdown_ref, both_ref, act2_ref, dqkv_ref,
     tout_ref, dproj_ref, act3_ref, dpre_ref, hid_ref, ddown_ref, qkv_s, low_s, dtout_s, in_sems, out_sems) = rest[9:]
    act2_hbm, dqkv_hbm, tout_hbm, dproj_hbm, act3_hbm, dpre_hbm, hid_hbm, ddown_hbm = flat_hbm
    frames, clips, both, width = mid_ref.shape
    pairs = [
        (in_hbm.at[:, :clips], mid_ref), (wqkv_hbm, wqkv_ref), (wo_hbm, wo_ref), (in_hbm.at[:, clips:], cot_ref),
        (wup_hbm, wup_ref), (wdown_hbm, wdown_ref),
    ]
    loads = [pltpu.make_async_copy(*p, in_sems.at[i]) for i, p in enumerate(pairs)]
    for load in loads:
        load.start()
    stores = []
    mine = pl.ds(offset * frames * both, clips * frames * both)

    def store(source, target):
        c = pltpu.make_async_copy(source, target, out_sems.at[len(stores)])
        c.start()
        stores.append(c)

    loads[0].wait()
    part = both // 2
    block = frames * part
    x = load_rows(mid_ref, clips, part).astype(F32)
    rows = x.shape[0]
    unit2, rstd2 = norm_parts(x)
    act2 = (unit2 * gain_ref[1:2] + bias_ref[1:2]).astype(BF)
    act2_ref[...] = act2
    store(act2_ref, act2_hbm.at[mine])
    loads[1].wait()
    qkv_s[...] = dot(act2, wqkv_ref[...]).astype(BF)
    scaled = head_masks(1.0 / math.sqrt(width // HEADS))
    plain = head_masks(1.0)
    r = lax.broadcasted_iota(jnp.int32, (block, block), 0)
    s = lax.broadcasted_iota(jnp.int32, (block, block), 1)
    base = (r % part == s % part) & (s // part <= r // part)
    row_mask = []
    for c in range(clips):
        count = counts_ref[offset + c]
        allowed = base & (s // part < count)
        row_mask.append(count)
        for h in range(2):
            b = 2 * c + h
            at = slice(b * block, (b + 1) * block)
            for pair in range(HEADS // 2):
                lo = pair * 128
                query = qkv_s[at, lo : lo + 128]
                key = qkv_s[at, width + lo : width + lo + 128]
                value = qkv_s[at, 2 * width + lo : 2 * width + lo + 128]
                scores = dot_nt(query, split_heads(key, scaled))
                for k in range(2):
                    sc = jnp.where(allowed, scores[:, k * block : (k + 1) * block], NEG)
                    low_s[b, pair, :, k * block : (k + 1) * block] = softmax(sc).astype(BF)
                tout_ref[at, lo : lo + 128] = dot(low_s[b, pair], split_heads(value, plain)).astype(BF)
    store(tout_ref, tout_hbm.at[mine])
    loads[2].wait()
    late = x + dot(tout_ref[...], wo_ref[...])
    unit3, rstd3 = norm_parts(late)
    act3 = (unit3 * gain_ref[2:3] + bias_ref[2:3]).astype(BF)
    act3_ref[...] = act3
    store(act3_ref, act3_hbm.at[mine])
    loads[3].wait()
    frame_of = lax.broadcasted_iota(jnp.int32, (block, width), 0) // part
    d_out = load_rows(cot_ref, clips, part)
    d_out = jnp.concatenate(
        [
            jnp.where(frame_of < row_mask[b // 2], d_out[b * block : (b + 1) * block].astype(F32), 0.0)
            for b in range(2 * clips)
        ],
        axis=0,
    )
    d_down = d_out.astype(BF)
    ddown_ref[...] = d_down
    store(ddown_ref, ddown_hbm.at[mine])
    out = late
    d_act3 = None
    loads[4].wait()
    loads[5].wait()
    k0 = math.sqrt(2.0 / math.pi)
    k1 = 0.044715
    for j in range(2):
        cols = slice(j * 2 * width, (j + 1) * 2 * width)
        u = dot(act3, wup_ref[:, cols]) + bup_ref[0:1, cols]
        sq = u * u
        t = jnp.tanh(k0 * u * (1.0 + k1 * sq))
        half_t = 0.5 + 0.5 * t
        hid = (u * half_t).astype(BF)
        slope = half_t + 0.5 * u * (1.0 - t * t) * (k0 + (3.0 * k0 * k1) * sq)
        hid_ref[:, cols] = hid
        store(hid_ref.at[:, cols], hid_hbm.at[mine, cols])
        out = out + dot(hid, wdown_ref[cols, :])
        d_pre32 = dot_nt(d_down, wdown_ref[cols, :]) * slope
        d_pre = d_pre32.astype(BF)
        dpre_ref[:, cols] = d_pre
        store(dpre_ref.at[:, cols], dpre_hbm.at[mine, cols])
        upbias_ref[:, cols] = fold_rows(d_pre.astype(F32))
        more = dot_nt(d_pre, wup_ref[:, cols])
        d_act3 = more if d_act3 is None else d_act3 + more
    store_rows(both_ref, out.astype(BF), clips, clips, part)
    store(both_ref.at[:, clips:], both_hbm.at[:, clips:])
    small_ref[0] = fold_rows(d_act3 * unit3)
    small_ref[1] = fold_rows(d_act3)
    d_late = d_out + norm_back(unit3, rstd3, gain_ref[2:3], d_act3)
    d_proj = d_late.astype(BF)
    dproj_ref[...] = d_proj
    store(dproj_ref, dproj_hbm.at[mine])
    dtout_s[...] = dot_nt(d_proj, wo_ref[...]).astype(BF)
    for b in range(2 * clips):
        at = slice(b * block, (b + 1) * block)
        for pair in range(HEADS // 2):
            lo = pair * 128
            query = qkv_s[at, lo : lo + 128]
            key = qkv_s[at, width + lo : width + lo + 128]
            value = qkv_s[at, 2 * width + lo : 2 * width + lo + 128]
            d_o = dtout_s[at, lo : lo + 128]
            d_p = dot_nt(d_o, split_heads(value, plain))
            low = low_s[b, pair]
            ds = []
            for k in range(2):
                cols = slice(k * block, (k + 1) * block)
                p = low[:, cols].astype(F32)
                pd = p * d_p[:, cols]
                ds.append((pd - p * jnp.sum(pd, axis=-1, keepdims=True)).astype(BF))
            d_s = jnp.concatenate(ds, axis=1)
            dqkv_ref[at, lo : lo + 128] = dot(d_s, split_heads(key, scaled)).astype(BF)
            d_k = pick_heads(dot_tn(d_s, query)) * (1.0 / math.sqrt(width // HEADS))
            dqkv_ref[at, width + lo : width + lo + 128] = d_k.astype(BF)
            d_v = pick_heads(dot_tn(low, d_o))
            dqkv_ref[at, 2 * width + lo : 2 * width + lo + 128] = d_v.astype(BF)
    store(dqkv_ref, dqkv_hbm.at[mine])
    d_act2 = dot_nt(dqkv_ref[...], wqkv_ref[...])
    small_ref[2] = fold_rows(d_act2 * unit2)
    small_ref[3] = fold_rows(d_act2)
    d_mid = d_late + norm_back(unit2, rstd2, gain_ref[1:2], d_act2)
    store_rows(both_ref, d_mid.astype(BF), 0, clips, part)
    store(both_ref.at[:, :clips], both_hbm.at[:, :clips])
    for c in stores:
        c.wait()


def run_temporal(offset, total_clips, counts, both_in, gain, bias, b_up, w_qkv, w_o, w_up, w_down, filled):
    frames, clips, both, width = both_in.shape
    clips //= 2
    hidden = w_up.shape[1]
    rows = clips * frames * both
    total = total_clips * frames * both
    widths = (width, 3 * width, width, width, width, hidden, hidden, width)
    small = (counts, gain, bias, b_up)
    large = (both_in, w_qkv, w_o, w_up, w_down)
    hbm = pl.BlockSpec(memory_space=pl.ANY)
    vmem = pl.BlockSpec(memory_space=pltpu.VMEM)
    half = (frames, clips, both, width)
    return pl.pallas_call(
        functools.partial(temporal, offset, bool(filled)),
        in_specs=[pl.BlockSpec(memory_space=SMEM)] + [vmem] * 3 + [hbm] * (len(large) + len(filled)),
        out_specs=[hbm] * 9 + [vmem] * 2,
        out_shape=[jax.ShapeDtypeStruct(both_in.shape, BF)]
        + [jax.ShapeDtypeStruct((total, w), BF) for w in widths]
        + [jax.ShapeDtypeStruct((4, 8, width), F32), jax.ShapeDtypeStruct((8, hidden), F32)],
        scratch_shapes=[pltpu.VMEM(half, BF)] * 2
        + [pltpu.VMEM(w.shape, BF) for w in large[1:]]
        + [pltpu.VMEM(both_in.shape, BF)]
        + [pltpu.VMEM((rows, w), BF) for w in widths]
        + [
            pltpu.VMEM((rows, 3 * width), BF),
            pltpu.VMEM((2 * clips, HEADS // 2, rows // (2 * clips), rows // clips), BF),
            pltpu.VMEM((rows, width), BF),
            pltpu.SemaphoreType.DMA((6,)),
            pltpu.SemaphoreType.DMA((12,)),
        ],
        input_output_aliases={len(small) + len(large) + i: 1 + i for i in range(len(filled))},
        compiler_params=params(),
        cost_estimate=cost(clips * frames * both * width * width * 40, 8 * clips * MIB),
        name="temporal",
    )(*small, *large, *filled)


def spatial_backward(dmid_ref, done_ref, qkv_ref, low_ref, wo_ref, *rest):
    dqkv_ref, block_ref = rest[-2:]
    _, n, width = block_ref.shape
    d_mid = dmid_ref[:, 0].reshape(n, width)
    block_ref[0] = done_ref[:, 0].reshape(n, width)
    d_out = dot_nt(d_mid, wo_ref[...]).astype(BF)
    scaled = head_masks(1.0 / math.sqrt(width // HEADS))
    plain = head_masks(1.0)
    for pair in range(HEADS // 2):
        lo = pair * 128
        query = qkv_ref[0, :, lo : lo + 128]
        key = qkv_ref[0, :, width + lo : width + lo + 128]
        value = qkv_ref[0, :, 2 * width + lo : 2 * width + lo + 128]
        d_o = d_out[:, lo : lo + 128]
        d_p = dot_nt(d_o, split_heads(value, plain))
        low = low_ref[0, pair]
        ds = []
        for k in range(2):
            cols = slice(k * n, (k + 1) * n)
            p = low[:, cols].astype(F32)
            pd = p * d_p[:, cols]
            ds.append((pd - p * jnp.sum(pd, axis=-1, keepdims=True)).astype(BF))
        d_s = jnp.concatenate(ds, axis=1)
        dqkv_ref[0, :, lo : lo + 128] = dot(d_s, split_heads(key, scaled)).astype(BF)
        d_k = small_tn(query, d_s) * (1.0 / math.sqrt(width // HEADS))
        dqkv_ref[0, :, width + lo : width + lo + 128] = d_k.astype(BF)
        dqkv_ref[0, :, 2 * width + lo : 2 * width + lo + 128] = small_tn(d_o, low).astype(BF)


def spatial_input(offset, actions_ref, tok_ref, dmid_ref, dqkv_ref, table_ref, gain_ref, wqkv_ref, *rest):
    gin_ref, small_ref, gtable_ref = rest[-3:]
    step = pl.program_id(0)
    action = actions_ref[offset + step]
    x = embed(tok_ref, table_ref, action)
    n, width = x.shape
    d_mid = dmid_ref[:, 0].reshape(n, width)
    d_act = dot_nt(dqkv_ref[0], wqkv_ref[...])
    unit, rstd = norm_parts(x)

    @pl.when(step == 0)
    def _():
        small_ref[...] = jnp.zeros_like(small_ref)
        gtable_ref[...] = jnp.zeros_like(gtable_ref)

    small_ref[0] += fold_rows(d_act * unit)
    small_ref[1] += fold_rows(d_act)
    g = d_mid.astype(F32) + norm_back(unit, rstd, gain_ref[0:1], d_act)
    gin_ref[0] = g
    total = jnp.sum(g, axis=0, keepdims=True)
    rows = lax.broadcasted_iota(jnp.int32, gtable_ref.shape, 0)
    gtable_ref[...] += jnp.where(rows == action, total, 0.0)


def run_spatial_input(offset, actions, tok, both, d_qkv, table, gain, w_qkv, filled):
    total, patch, width = tok.shape
    frames, clips, part, _ = both.shape
    clips //= 2
    later = lambda c: (c + offset, 0, 0)
    inputs = (actions, tok, both, d_qkv, table, gain, w_qkv)
    return pl.pallas_call(
        functools.partial(spatial_input, offset),
        grid=(clips,),
        in_specs=[
            pl.BlockSpec(memory_space=SMEM),
            pl.BlockSpec((1, patch, width), later),
            pl.BlockSpec((frames, 1, part, width), lambda c: (0, c, 0, 0)),
            pl.BlockSpec((1, patch, 3 * width), later),
            resident(table.shape), resident(gain.shape), resident(w_qkv.shape),
        ]
        + [pl.BlockSpec(memory_space=pl.ANY)] * len(filled),
        out_specs=[pl.BlockSpec((1, patch, width), later), resident((2, 8, width)), resident(table.shape)],
        out_shape=[
            jax.ShapeDtypeStruct((total, patch, width), F32),
            jax.ShapeDtypeStruct((2, 8, width), F32),
            jax.ShapeDtypeStruct(table.shape, F32),
        ],
        input_output_aliases={len(inputs) + i: i for i in range(len(filled))},
        compiler_params=params(),
        cost_estimate=cost(clips * patch * width * width * 6, 4 * clips * MIB),
        name="spatial_input",
    )(*inputs, *filled)


def run_spatial_backward(offset, total, both, qkv, low, w_o, filled):
    clips, patch, width = qkv.shape
    width //= 3
    frames, _, part, _ = both.shape
    row = lambda c: (c, 0, 0)
    later = lambda c: (c + offset, 0, 0)
    inputs = (both, both, qkv, low, w_o)
    return pl.pallas_call(
        spatial_backward,
        grid=(clips,),
        in_specs=[
            pl.BlockSpec((frames, 1, part, width), lambda c: (0, c, 0, 0)),
            pl.BlockSpec((frames, 1, part, width), lambda c: (0, c + clips, 0, 0)),
            pl.BlockSpec((1, patch, 3 * width), row),
            pl.BlockSpec((1, HEADS // 2, patch, 2 * patch), lambda c: (c, 0, 0, 0)),
            resident(w_o.shape),
        ]
        + [pl.BlockSpec(memory_space=pl.ANY)] * len(filled),
        out_specs=[pl.BlockSpec((1, patch, 3 * width), later), pl.BlockSpec((1, patch, width), later)],
        out_shape=[
            jax.ShapeDtypeStruct((total, patch, 3 * width), BF),
            jax.ShapeDtypeStruct((total, patch, width), BF),
        ],
        input_output_aliases={len(inputs) + i: i for i in range(len(filled))},
        compiler_params=params(),
        cost_estimate=cost(clips * patch * width * width * 8, 5 * clips * MIB),
        name="spatial_backward",
    )(*inputs, *filled)


def choose(core, first, second, keep_ref, send_ref, at):
    for k in range(first.shape[1] // 128):
        cols = slice(k * 128, (k + 1) * 128)
        keep_ref[at, k] = jnp.where(core == 0, first[:, cols], second[:, cols]).astype(BF)
        send_ref[at, k] = jnp.where(core == 0, second[:, cols], first[:, cols]).astype(BF)


def ffn_grads(core_ref, a_ref, b_ref, c_ref, d_ref, keep_ref, send_ref):
    choose(
        core_ref[0], dot_tn(a_ref[...], b_ref[...]), dot_tn(c_ref[...], d_ref[...]), keep_ref, send_ref, 0
    )


def run_ffn_grads(core, act3, d_pre, hid, d_down):
    total, width = act3.shape
    count = d_pre.shape[1] // width
    wide = pl.BlockSpec((total, width), lambda j: (0, j))
    out = pl.BlockSpec((1, width // 128, width, 128), lambda j: (j, 0, 0, 0))
    return pl.pallas_call(
        ffn_grads,
        grid=(count,),
        in_specs=[pl.BlockSpec(memory_space=SMEM), resident(act3.shape), wide, wide, resident(d_down.shape)],
        out_specs=[out, out],
        out_shape=[jax.ShapeDtypeStruct((count, width // 128, width, 128), BF)] * 2,
        compiler_params=params(),
        cost_estimate=cost(4 * total * width * width * count, 16 * MIB),
        name="ffn_grads",
    )(core, act3, d_pre, hid, d_down)


def columns(v):
    return jnp.stack([v[:, k * 128 : (k + 1) * 128] for k in range(v.shape[1] // 128)])


def temporal_grads(act_ref, dqkv_ref, out_ref, dproj_ref, grad_ref):
    width = act_ref.shape[1]
    for j in range(3):
        grad_ref[j] = columns(dot_tn(act_ref[...], dqkv_ref[:, j * width : (j + 1) * width]).astype(BF))
    grad_ref[3] = columns(dot_tn(out_ref[...], dproj_ref[...]).astype(BF))


def run_temporal_grads(act, d_qkv, out, d_proj):
    total, width = act.shape
    return pl.pallas_call(
        temporal_grads,
        out_shape=jax.ShapeDtypeStruct((4, width // 128, width, 128), BF),
        compiler_params=params(),
        cost_estimate=cost(8 * total * width * width, 8 * MIB),
        name="temporal_grads",
    )(act, d_qkv, out, d_proj)


def spatial_grads(core_ref, act0_ref, act1_ref, dqkv_ref, out0_ref, out1_ref, both0_ref, both1_ref, other_ref,
                  keep_ref, send_ref):
    core = core_ref[0]
    frames, _, part, width = both0_ref.shape
    flat = lambda ref: ref[...].reshape(-1, width)
    act = jnp.concatenate([flat(act0_ref), flat(act1_ref)], axis=0)
    total = act.shape[0]
    half = out0_ref.shape[0]
    for j in range(4):
        if j < 3:
            grad = dot_tn(act, dqkv_ref[:, :, j * width : (j + 1) * width].reshape(total, width))
        else:
            out = jnp.concatenate([flat(out0_ref), flat(out1_ref)], axis=0)
            d_mid = jnp.concatenate(
                [ref[:, c].reshape(frames * part, width) for ref in (both0_ref, both1_ref) for c in range(half)],
                axis=0,
            )
            grad = dot_tn(out, d_mid)
        grad = columns(grad.astype(BF))
        keep_ref[j] = jnp.where(core == 0, other_ref[j], grad)
        send_ref[j] = jnp.where(core == 0, grad, other_ref[j])


def pack_small(sb0_ref, sb1_ref, ub0_ref, ub1_ref, sc0_ref, sc1_ref, gt0_ref, gt1_ref, sums_ref):
    width = gt0_ref.shape[1]
    fold = lambda v: jnp.sum(v, axis=-2, keepdims=True)
    sb = fold(sb0_ref[...] + sb1_ref[...])
    sc = fold(sc0_ref[...] + sc1_ref[...])
    ub = fold(ub0_ref[...] + ub1_ref[...])
    table = gt0_ref[...] + gt1_ref[...]
    norms = jnp.concatenate([sc[0], sb[2], sb[0], sc[1], sb[3], sb[1], jnp.zeros((2, width), F32)], axis=0)
    cut = lambda v: [v[:, k * 128 : (k + 1) * 128] for k in range(v.shape[1] // 128)]
    rows = jnp.concatenate(cut(table) + cut(norms) + cut(ub), axis=0)
    sums_ref[...] = rows


def run_pack_small(*arrays):
    return pl.pallas_call(
        pack_small,
        out_shape=jax.ShapeDtypeStruct((80, 128), F32),
        compiler_params=params(),
        cost_estimate=cost(2**33, 64 * MIB),
        name="pack_small",
    )(*arrays)


def run_spatial_grads(core, *arrays):
    grad = arrays[7]
    return pl.pallas_call(
        spatial_grads,
        in_specs=[pl.BlockSpec(memory_space=SMEM)] + [pl.BlockSpec(memory_space=pltpu.VMEM)] * len(arrays),
        out_shape=[jax.ShapeDtypeStruct(grad.shape, BF)] * 2,
        compiler_params=params(),
        cost_estimate=cost(8 * 1024 * 512 * 512, 8 * MIB),
        name="spatial_grads",
    )(core, *arrays)


def unpack(main_ref, up_ref, down_ref, tqkv_ref, to_ref, sqkv_ref, so_ref,
           table_ref, gain_ref, bias_ref, ub_ref):
    step = pl.program_id(0)
    width = to_ref.shape[0]
    group = main_ref.shape[0] // 4
    chips = pl.ds((step % 4) * group, group)
    exps = main_ref[chips, :, 336:352].astype(F32)
    sides = []
    for c in range(2):
        e = jnp.where(step < 4, exps[:, c, 0:1], exps[:, c, 1:2])
        sides.append((main_ref[chips, c, pl.ds((step // 4) * 128, 128)].astype(F32) * jnp.exp2(e)).reshape(-1, 128))

    def put(ref, v):
        for k in range(width // 128):
            ref[:, k * 128 : (k + 1) * 128] = v[k * width : (k + 1) * width]

    @pl.when(step == 0)
    def _():
        every = main_ref[:, :, 336:352].astype(F32)

        def total(start, stop, row):
            terms = main_ref[:, :, start:stop].astype(F32) * jnp.exp2(every[:, :, row : row + 1])
            return jnp.sum(jnp.sum(terms, axis=1), axis=0)

        rows = jnp.concatenate([total(256, 288, 2), total(288, 320, 3), total(320, 336, 4)], axis=0)
        for k in range(width // 128):
            cols = slice(k * 128, (k + 1) * 128)
            table_ref[:, cols] = rows[8 * k : 8 * k + 8]
            gain_ref[:, cols] = rows[32 + 8 * k : 35 + 8 * k]
            bias_ref[:, cols] = rows[35 + 8 * k : 38 + 8 * k]
        for k in range(ub_ref.shape[1] // 128):
            ub_ref[:, k * 128 : (k + 1) * 128] = rows[64 + k : 65 + k]

    @pl.when(step < 4)
    def _():
        put(up_ref, sides[0])
        put(down_ref, sides[1])

    @pl.when((step >= 4) & (step < 7))
    def _():
        put(tqkv_ref, sides[0])
        put(sqkv_ref, sides[1])

    @pl.when(step == 7)
    def _():
        put(to_ref, sides[0])
        put(so_ref, sides[1])


def run_unpack(whole, width):
    up = lambda j: (0, jnp.minimum(j, 3))
    down = lambda j: (jnp.minimum(j, 3), 0)
    third = lambda j: (0, jnp.clip(j - 4, 0, 2))
    square = (width, width)
    outs = [(width, 4 * width), (4 * width, width)] + [(width, 3 * width), square] * 2
    outs += [(8, width), (3, width), (3, width), (1, 4 * width)]
    return pl.pallas_call(
        unpack,
        grid=(8,),
        in_specs=[
            pl.BlockSpec(memory_space=pltpu.VMEM),
        ],
        out_specs=[
            pl.BlockSpec(square, up), pl.BlockSpec(square, down),
            pl.BlockSpec(square, third), resident(square), pl.BlockSpec(square, third), resident(square),
        ]
        + [resident(s) for s in outs[6:]],
        out_shape=[jax.ShapeDtypeStruct(s, F32) for s in outs],
        compiler_params=params(36),
        cost_estimate=cost(MIB, 24 * MIB),
        name="unpack",
    )(whole)


def swap_cores(v):
    return lax.ppermute(v, "c", [(0, 1), (1, 0)])


def after(v, *done):
    return lax.optimization_barrier((v, *done))[0]


def over_frames(v):
    return lax.all_to_all(v, FRAME_AXES, 0, 0)


def over_chips(v):
    return lax.all_to_all(v, CHIP_AXES, 0, 0)


def add_parts(parts):
    return jnp.sum(parts.astype(F32), axis=0)


def add_core(keep, send, *done):
    got = after(swap_cores(send), *done)
    return (keep.astype(F32) + got.astype(F32)).astype(BF)


def exponent(v, axes):
    most = jnp.max(jnp.abs(v), axis=axes, keepdims=True)
    return jnp.clip(jnp.ceil(jnp.log2(jnp.maximum(most, 1e-37))), -120.0, 120.0)


def scaled(v, axes):
    e = exponent(v, axes)
    return (v * jnp.exp2(-e)).astype(F16), jnp.broadcast_to(e, (e.shape[0], 128)).astype(F16)


def shards(
    frame_tokens, actions, frame_counts, action_table, ln_gain, ln_bias, w_sqkv, w_so, w_tqkv, w_to,
    w_up, b_up, w_down, cotangent,
):
    clips, _, patch, width = frame_tokens.shape
    frames = lax.axis_size(FRAME_AXES)
    chips = lax.axis_size(CHIP_AXES)
    core = lax.axis_index("c").astype(jnp.int32).reshape(1)
    tok = frame_tokens[:, 0]
    acts = actions[:, 0]
    half = clips // 2
    forward = [
        run_spatial_forward(
            frames, i * half, half, acts, tok, cotangent[:, 0], action_table, ln_gain, ln_bias, w_sqkv, w_so
        )
        for i in range(2)
    ]
    there0 = over_frames(forward[0][0])
    there1 = over_frames(after(forward[1][0], there0))
    back = (ln_gain, ln_bias, b_up[None], w_tqkv, w_to, w_up, w_down)
    first = run_temporal(0, clips, frame_counts, there0, *back, ())
    second = run_temporal(half, clips, frame_counts, there1, *back, first[1:9])
    both0 = over_frames(after(first[0], there1))
    both1 = over_frames(after(second[0], both0))
    act_two, d_tqkv, t_out, d_tproj, act_three, d_pre, hidden, d_down = second[1:9]
    lines = lambda v: v.reshape(chips, -1, 128)
    keep, send = run_ffn_grads(core, after(act_three, both0), d_pre, hidden, d_down)
    ffn = add_core(keep, after(send, both1))
    temporal_part = run_temporal_grads(after(act_two, ffn), d_tqkv, t_out, d_tproj)
    ffn_part = add_parts(over_chips(lines(ffn)))

    d_sqkv, block_out = run_spatial_backward(
        half, clips, both1, forward[1][1], forward[1][2], w_so,
        run_spatial_backward(0, clips, both0, forward[0][1], forward[0][2], w_so, ()),
    )
    keep, send = run_spatial_grads(
        core, forward[0][4], forward[1][4], d_sqkv, forward[0][3], forward[1][3], both0, both1, temporal_part
    )
    ffn_rows, ffn_exp = scaled(ffn_part, (0, 1))
    late_rows, late_exp = scaled(add_parts(over_chips(lines(add_core(keep, send, ffn_rows)))), (0, 1))
    low = (action_table, ln_gain, w_sqkv)
    in0 = run_spatial_input(0, acts, tok, both0, d_sqkv, *low, ())
    in1 = run_spatial_input(half, acts, tok, both1, d_sqkv, *low, in0[:1])
    grad_input = in1[0]
    sums = run_pack_small(first[9], second[9], first[10], second[10], in0[1], in1[1], in0[2], in1[2])
    own = [scaled(v, (0, 1)) for v in (sums[:32], sums[32:64], sums[64:])]
    fill = jnp.zeros((11, 128), F16)
    mine = jnp.concatenate(
        [ffn_rows, late_rows, *(v for v, _ in own), ffn_exp, late_exp, *(e for _, e in own), fill], axis=0
    )
    whole = lax.all_gather(mine, (*CHIP_AXES, "c"), axis=0, tiled=True).reshape(chips, 2, -1, 128)
    (grad_up, grad_down, grad_tqkv, grad_to, grad_sqkv, grad_so, grad_table, grad_gain, grad_bias, up_bias) = (
        run_unpack(whole.astype(BF), width)
    )
    return (
        block_out[:, None],
        grad_input[:, None],
        grad_table,
        grad_gain,
        grad_bias,
        grad_sqkv,
        grad_so,
        grad_tqkv,
        grad_to,
        grad_up,
        up_bias.reshape(-1),
        grad_down,
    )


def solution(mesh):
    fine = Mesh(mesh.devices.reshape(4, 2, 2, 4, 2), ("x", "zh", "zl", "y", "c"))
    clip = ("zl", "y", "c")
    tokens = P(clip, FRAME_AXES, None, None)
    in_specs = (tokens, P(clip, FRAME_AXES), P(clip)) + (P(),) * 10 + (tokens,)
    out_specs = (tokens, tokens) + (P(),) * 10
    return jax.shard_map(shards, mesh=fine, in_specs=in_specs, out_specs=out_specs, check_vma=False)
```

```python
import functools
import math

import jax
import jax.numpy as jnp
from jax import lax
from jax.experimental import pallas as pl
from jax.experimental.pallas import tpu as pltpu
from jax.sharding import Mesh, PartitionSpec as P

HEADS = 8
EPS = 1e-05
NEG = -1e30
BF = jnp.bfloat16
F32 = jnp.float32
F16 = jnp.float16
FRAME_AXES = ("x", "zh")
CHIP_AXES = ("x", "zh", "zl", "y")
MIB = 1 << 20
SMEM = pltpu.SMEM


def dot(a, b):
    return jnp.dot(a, b, preferred_element_type=F32)


def dot_nt(a, b):
    return lax.dot_general(a, b, (((1,), (1,)), ((), ())), preferred_element_type=F32)


def dot_tn(a, b):
    return lax.dot_general(a, b, (((0,), (0,)), ((), ())), preferred_element_type=F32)


def norm_parts(v):
    center = v - jnp.mean(v, axis=-1, keepdims=True)
    rstd = lax.rsqrt(jnp.mean(center * center, axis=-1, keepdims=True) + EPS)
    return center * rstd, rstd


def norm_back(unit, rstd, gain, up):
    d_unit = up * gain
    mean_a = jnp.mean(d_unit, axis=-1, keepdims=True)
    mean_b = jnp.mean(d_unit * unit, axis=-1, keepdims=True)
    return rstd * (d_unit - mean_a - unit * mean_b)


def fold_rows(v):
    return jnp.sum(v.reshape(-1, 8, v.shape[-1]), axis=0)


def head_masks(scale):
    lane = lax.broadcasted_iota(jnp.int32, (1, 128), 1)
    first = jnp.where(lane < 64, scale, 0.0).astype(BF)
    second = jnp.where(lane < 64, 0.0, scale).astype(BF)
    return first, second


def split_heads(v, masks):
    return jnp.concatenate([v * masks[0], v * masks[1]], axis=0)


def softmax(s):
    e = jnp.exp(s - jnp.max(s, axis=-1, keepdims=True))
    return e * (1.0 / jnp.sum(e, axis=-1, keepdims=True))


def pick_heads(v):
    half = v.shape[0] // 2
    lane = lax.broadcasted_iota(jnp.int32, (half, 128), 1)
    return jnp.where(lane < 64, v[:half], v[half:])


def small_tn(a, b):
    z = dot(a.T, b)
    n = z.shape[1] // 2
    return jnp.concatenate([z[:64, :n], z[64:, n:]], axis=0).T


def embed(tok_ref, table_ref, action):
    table = table_ref[...].astype(F32)
    rows = lax.broadcasted_iota(jnp.int32, table.shape, 0)
    row = jnp.sum(jnp.where(rows == action, table, 0.0), axis=0, keepdims=True)
    return tok_ref[0].astype(F32) + row


def spatial_forward(offset, actions_ref, table_ref, gain_ref, bias_ref, tok_hbm, cot_hbm, wqkv_hbm, wo_hbm,
                    both_hbm, qkv_hbm, low_hbm, out_hbm, act_hbm,
                    tok_ref, cot_ref, wqkv_ref, wo_ref, both_ref, qkv_ref, low_ref, out_ref, act_ref,
                    in_sems, out_sems):
    clips, n, width = tok_ref.shape
    frames, _, part, _ = both_ref.shape
    mine = pl.ds(offset, clips)
    pairs = [(tok_hbm.at[mine], tok_ref), (wqkv_hbm, wqkv_ref), (cot_hbm.at[mine], cot_ref), (wo_hbm, wo_ref)]
    loads = [pltpu.make_async_copy(*p, in_sems.at[i]) for i, p in enumerate(pairs)]
    for load in loads:
        load.start()
    stores = []

    def store(source, target):
        c = pltpu.make_async_copy(source, target, out_sems.at[len(stores)])
        c.start()
        stores.append(c)

    loads[0].wait()
    x = jnp.concatenate(
        [embed(tok_ref.at[pl.ds(c, 1)], table_ref, actions_ref[offset + c]) for c in range(clips)], axis=0
    )
    unit, _ = norm_parts(x)
    act = (unit * gain_ref[0:1] + bias_ref[0:1]).astype(BF)
    act_ref[...] = act.reshape(act_ref.shape)
    store(act_ref, act_hbm)
    loads[1].wait()
    qkv_ref[...] = dot(act, wqkv_ref[...]).astype(BF).reshape(qkv_ref.shape)
    store(qkv_ref, qkv_hbm)
    loads[2].wait()
    for c in range(clips):
        both_ref[:, clips + c] = cot_ref[c].reshape(frames, part, width)
    store(both_ref.at[:, clips:], both_hbm.at[:, clips:])
    scaled = head_masks(1.0 / math.sqrt(width // HEADS))
    plain = head_masks(1.0)
    for c in range(clips):
        for pair in range(HEADS // 2):
            lo = pair * 128
            query = qkv_ref[c, :, lo : lo + 128]
            key = qkv_ref[c, :, width + lo : width + lo + 128]
            value = qkv_ref[c, :, 2 * width + lo : 2 * width + lo + 128]
            s = dot_nt(query, split_heads(key, scaled))
            low_ref[c, pair, :, :n] = softmax(s[:, :n]).astype(BF)
            low_ref[c, pair, :, n:] = softmax(s[:, n:]).astype(BF)
            out_ref[c, :, lo : lo + 128] = dot(low_ref[c, pair], split_heads(value, plain)).astype(BF)
        store(low_ref.at[c], low_hbm.at[c])
    store(out_ref, out_hbm)
    loads[3].wait()
    mid = (x + dot(out_ref[...].reshape(clips * n, width), wo_ref[...])).astype(BF)
    for c in range(clips):
        both_ref[:, c] = mid[c * n : (c + 1) * n].reshape(frames, part, width)
    store(both_ref.at[:, :clips], both_hbm.at[:, :clips])
    for c in stores:
        c.wait()


def resident(shape):
    return pl.BlockSpec(shape, lambda *_: (0,) * len(shape), pipeline_mode=pl.Buffered(1))


def params(mib=56):
    return pltpu.CompilerParams(vmem_limit_bytes=mib * MIB)


def cost(flops, nbytes):
    return pl.CostEstimate(flops=int(flops), bytes_accessed=int(nbytes), transcendentals=0)


def run_spatial_forward(frames, offset, clips, actions, tok, cot, table, gain, bias, w_qkv, w_o):
    _, patch, width = tok.shape
    part = patch // frames
    hbm = pl.BlockSpec(memory_space=pl.ANY)
    vmem = pl.BlockSpec(memory_space=pltpu.VMEM)
    rows = (clips, patch, width)
    outs = [
        (frames, 2 * clips, part, width), (clips, patch, 3 * width), (clips, HEADS // 2, patch, 2 * patch), rows, rows,
    ]
    return pl.pallas_call(
        functools.partial(spatial_forward, offset),
        in_specs=[pl.BlockSpec(memory_space=SMEM)] + [vmem] * 3 + [hbm] * 4,
        out_specs=[hbm] * 5,
        out_shape=[jax.ShapeDtypeStruct(o, BF) for o in outs],
        scratch_shapes=[pltpu.VMEM(v, BF) for v in (rows, rows, w_qkv.shape, w_o.shape, *outs)]
        + [pltpu.SemaphoreType.DMA((4,)), pltpu.SemaphoreType.DMA((5 + clips,))],
        compiler_params=params(),
        cost_estimate=cost(clips * patch * width * width * 10, 4 * clips * MIB),
        name="spatial_forward",
    )(actions, table, gain, bias, tok, cot, w_qkv, w_o)


def rows_of(ref, clip, half, part):
    v = ref[:, clip, half * part : (half + 1) * part, :]
    return v.reshape(-1, v.shape[-1])


def load_rows(ref, clips, part):
    return jnp.concatenate(
        [rows_of(ref, c, h, part) for c in range(clips) for h in range(2)], axis=0
    )


def store_rows(ref, v, first, clips, part):
    frames = ref.shape[0]
    block = frames * part
    for c in range(clips):
        for h in range(2):
            at = (2 * c + h) * block
            ref[:, first + c, h * part : (h + 1) * part, :] = v[at : at + block].reshape(frames, part, v.shape[-1])


def temporal(offset, filled, counts_ref, gain_ref, bias_ref, bup_ref, in_hbm, wqkv_hbm, wo_hbm, wup_hbm, wdown_hbm,
             *rest):
    rest = rest[8:] if filled else rest
    both_hbm, *flat_hbm = rest[:9]
    (small_ref, upbias_ref, mid_ref, cot_ref, wqkv_ref, wo_ref, wup_ref, wdown_ref, both_ref, act2_ref, dqkv_ref,
     tout_ref, dproj_ref, act3_ref, dpre_ref, hid_ref, ddown_ref, qkv_s, low_s, dtout_s, in_sems, out_sems) = rest[9:]
    act2_hbm, dqkv_hbm, tout_hbm, dproj_hbm, act3_hbm, dpre_hbm, hid_hbm, ddown_hbm = flat_hbm
    frames, clips, both, width = mid_ref.shape
    pairs = [
        (in_hbm.at[:, :clips], mid_ref), (wqkv_hbm, wqkv_ref), (wo_hbm, wo_ref), (in_hbm.at[:, clips:], cot_ref),
        (wup_hbm, wup_ref), (wdown_hbm, wdown_ref),
    ]
    loads = [pltpu.make_async_copy(*p, in_sems.at[i]) for i, p in enumerate(pairs)]
    for load in loads:
        load.start()
    stores = []
    mine = pl.ds(offset * frames * both, clips * frames * both)

    def store(source, target):
        c = pltpu.make_async_copy(source, target, out_sems.at[len(stores)])
        c.start()
        stores.append(c)

    loads[0].wait()
    part = both // 2
    block = frames * part
    x = load_rows(mid_ref, clips, part).astype(F32)
    rows = x.shape[0]
    unit2, rstd2 = norm_parts(x)
    act2 = (unit2 * gain_ref[1:2] + bias_ref[1:2]).astype(BF)
    act2_ref[...] = act2
    store(act2_ref, act2_hbm.at[mine])
    loads[1].wait()
    qkv_s[...] = dot(act2, wqkv_ref[...]).astype(BF)
    scaled = head_masks(1.0 / math.sqrt(width // HEADS))
    plain = head_masks(1.0)
    r = lax.broadcasted_iota(jnp.int32, (block, block), 0)
    s = lax.broadcasted_iota(jnp.int32, (block, block), 1)
    base = (r % part == s % part) & (s // part <= r // part)
    row_mask = []
    for c in range(clips):
        count = counts_ref[offset + c]
        allowed = base & (s // part < count)
        row_mask.append(count)
        for h in range(2):
            b = 2 * c + h
            at = slice(b * block, (b + 1) * block)
            for pair in range(HEADS // 2):
                lo = pair * 128
                query = qkv_s[at, lo : lo + 128]
                key = qkv_s[at, width + lo : width + lo + 128]
                value = qkv_s[at, 2 * width + lo : 2 * width + lo + 128]
                scores = dot_nt(query, split_heads(key, scaled))
                for k in range(2):
                    sc = jnp.where(allowed, scores[:, k * block : (k + 1) * block], NEG)
                    low_s[b, pair, :, k * block : (k + 1) * block] = softmax(sc).astype(BF)
                tout_ref[at, lo : lo + 128] = dot(low_s[b, pair], split_heads(value, plain)).astype(BF)
    store(tout_ref, tout_hbm.at[mine])
    loads[2].wait()
    late = x + dot(tout_ref[...], wo_ref[...])
    unit3, rstd3 = norm_parts(late)
    act3 = (unit3 * gain_ref[2:3] + bias_ref[2:3]).astype(BF)
    act3_ref[...] = act3
    store(act3_ref, act3_hbm.at[mine])
    loads[3].wait()
    frame_of = lax.broadcasted_iota(jnp.int32, (block, width), 0) // part
    d_out = load_rows(cot_ref, clips, part)
    d_out = jnp.concatenate(
        [
            jnp.where(frame_of < row_mask[b // 2], d_out[b * block : (b + 1) * block].astype(F32), 0.0)
            for b in range(2 * clips)
        ],
        axis=0,
    )
    d_down = d_out.astype(BF)
    ddown_ref[...] = d_down
    store(ddown_ref, ddown_hbm.at[mine])
    out = late
    d_act3 = None
    loads[4].wait()
    loads[5].wait()
    k0 = math.sqrt(2.0 / math.pi)
    k1 = 0.044715
    for j in range(2):
        cols = slice(j * 2 * width, (j + 1) * 2 * width)
        u = dot(act3, wup_ref[:, cols]) + bup_ref[0:1, cols]
        sq = u * u
        t = jnp.tanh(k0 * u * (1.0 + k1 * sq))
        half_t = 0.5 + 0.5 * t
        hid = (u * half_t).astype(BF)
        slope = half_t + 0.5 * u * (1.0 - t * t) * (k0 + (3.0 * k0 * k1) * sq)
        hid_ref[:, cols] = hid
        store(hid_ref.at[:, cols], hid_hbm.at[mine, cols])
        out = out + dot(hid, wdown_ref[cols, :])
        d_pre32 = dot_nt(d_down, wdown_ref[cols, :]) * slope
        d_pre = d_pre32.astype(BF)
        dpre_ref[:, cols] = d_pre
        store(dpre_ref.at[:, cols], dpre_hbm.at[mine, cols])
        upbias_ref[:, cols] = fold_rows(d_pre.astype(F32))
        more = dot_nt(d_pre, wup_ref[:, cols])
        d_act3 = more if d_act3 is None else d_act3 + more
    store_rows(both_ref, out.astype(BF), clips, clips, part)
    store(both_ref.at[:, clips:], both_hbm.at[:, clips:])
    small_ref[0] = fold_rows(d_act3 * unit3)
    small_ref[1] = fold_rows(d_act3)
    d_late = d_out + norm_back(unit3, rstd3, gain_ref[2:3], d_act3)
    d_proj = d_late.astype(BF)
    dproj_ref[...] = d_proj
    store(dproj_ref, dproj_hbm.at[mine])
    dtout_s[...] = dot_nt(d_proj, wo_ref[...]).astype(BF)
    for b in range(2 * clips):
        at = slice(b * block, (b + 1) * block)
        for pair in range(HEADS // 2):
            lo = pair * 128
            query = qkv_s[at, lo : lo + 128]
            key = qkv_s[at, width + lo : width + lo + 128]
            value = qkv_s[at, 2 * width + lo : 2 * width + lo + 128]
            d_o = dtout_s[at, lo : lo + 128]
            d_p = dot_nt(d_o, split_heads(value, plain))
            low = low_s[b, pair]
            ds = []
            for k in range(2):
                cols = slice(k * block, (k + 1) * block)
                p = low[:, cols].astype(F32)
                pd = p * d_p[:, cols]
                ds.append((pd - p * jnp.sum(pd, axis=-1, keepdims=True)).astype(BF))
            d_s = jnp.concatenate(ds, axis=1)
            dqkv_ref[at, lo : lo + 128] = dot(d_s, split_heads(key, scaled)).astype(BF)
            d_k = pick_heads(dot_tn(d_s, query)) * (1.0 / math.sqrt(width // HEADS))
            dqkv_ref[at, width + lo : width + lo + 128] = d_k.astype(BF)
            d_v = pick_heads(dot_tn(low, d_o))
            dqkv_ref[at, 2 * width + lo : 2 * width + lo + 128] = d_v.astype(BF)
    store(dqkv_ref, dqkv_hbm.at[mine])
    d_act2 = dot_nt(dqkv_ref[...], wqkv_ref[...])
    small_ref[2] = fold_rows(d_act2 * unit2)
    small_ref[3] = fold_rows(d_act2)
    d_mid = d_late + norm_back(unit2, rstd2, gain_ref[1:2], d_act2)
    store_rows(both_ref, d_mid.astype(BF), 0, clips, part)
    store(both_ref.at[:, :clips], both_hbm.at[:, :clips])
    for c in stores:
        c.wait()


def run_temporal(offset, total_clips, counts, both_in, gain, bias, b_up, w_qkv, w_o, w_up, w_down, filled):
    frames, clips, both, width = both_in.shape
    clips //= 2
    hidden = w_up.shape[1]
    rows = clips * frames * both
    total = total_clips * frames * both
    widths = (width, 3 * width, width, width, width, hidden, hidden, width)
    small = (counts, gain, bias, b_up)
    large = (both_in, w_qkv, w_o, w_up, w_down)
    hbm = pl.BlockSpec(memory_space=pl.ANY)
    vmem = pl.BlockSpec(memory_space=pltpu.VMEM)
    half = (frames, clips, both, width)
    return pl.pallas_call(
        functools.partial(temporal, offset, bool(filled)),
        in_specs=[pl.BlockSpec(memory_space=SMEM)] + [vmem] * 3 + [hbm] * (len(large) + len(filled)),
        out_specs=[hbm] * 9 + [vmem] * 2,
        out_shape=[jax.ShapeDtypeStruct(both_in.shape, BF)]
        + [jax.ShapeDtypeStruct((total, w), BF) for w in widths]
        + [jax.ShapeDtypeStruct((4, 8, width), F32), jax.ShapeDtypeStruct((8, hidden), F32)],
        scratch_shapes=[pltpu.VMEM(half, BF)] * 2
        + [pltpu.VMEM(w.shape, BF) for w in large[1:]]
        + [pltpu.VMEM(both_in.shape, BF)]
        + [pltpu.VMEM((rows, w), BF) for w in widths]
        + [
            pltpu.VMEM((rows, 3 * width), BF),
            pltpu.VMEM((2 * clips, HEADS // 2, rows // (2 * clips), rows // clips), BF),
            pltpu.VMEM((rows, width), BF),
            pltpu.SemaphoreType.DMA((6,)),
            pltpu.SemaphoreType.DMA((12,)),
        ],
        input_output_aliases={len(small) + len(large) + i: 1 + i for i in range(len(filled))},
        compiler_params=params(),
        cost_estimate=cost(clips * frames * both * width * width * 40, 8 * clips * MIB),
        name="temporal",
    )(*small, *large, *filled)


def spatial_backward(dmid_ref, done_ref, qkv_ref, low_ref, wo_ref, *rest):
    dqkv_ref, block_ref = rest[-2:]
    _, n, width = block_ref.shape
    d_mid = dmid_ref[:, 0].reshape(n, width)
    block_ref[0] = done_ref[:, 0].reshape(n, width)
    d_out = dot_nt(d_mid, wo_ref[...]).astype(BF)
    scaled = head_masks(1.0 / math.sqrt(width // HEADS))
    plain = head_masks(1.0)
    for pair in range(HEADS // 2):
        lo = pair * 128
        query = qkv_ref[0, :, lo : lo + 128]
        key = qkv_ref[0, :, width + lo : width + lo + 128]
        value = qkv_ref[0, :, 2 * width + lo : 2 * width + lo + 128]
        d_o = d_out[:, lo : lo + 128]
        d_p = dot_nt(d_o, split_heads(value, plain))
        low = low_ref[0, pair]
        ds = []
        for k in range(2):
            cols = slice(k * n, (k + 1) * n)
            p = low[:, cols].astype(F32)
            pd = p * d_p[:, cols]
            ds.append((pd - p * jnp.sum(pd, axis=-1, keepdims=True)).astype(BF))
        d_s = jnp.concatenate(ds, axis=1)
        dqkv_ref[0, :, lo : lo + 128] = dot(d_s, split_heads(key, scaled)).astype(BF)
        d_k = small_tn(query, d_s) * (1.0 / math.sqrt(width // HEADS))
        dqkv_ref[0, :, width + lo : width + lo + 128] = d_k.astype(BF)
        dqkv_ref[0, :, 2 * width + lo : 2 * width + lo + 128] = small_tn(d_o, low).astype(BF)


def spatial_input(offset, actions_ref, tok_ref, dmid_ref, dqkv_ref, table_ref, gain_ref, wqkv_ref, *rest):
    gin_ref, small_ref, gtable_ref = rest[-3:]
    step = pl.program_id(0)
    action = actions_ref[offset + step]
    x = embed(tok_ref, table_ref, action)
    n, width = x.shape
    d_mid = dmid_ref[:, 0].reshape(n, width)
    d_act = dot_nt(dqkv_ref[0], wqkv_ref[...])
    unit, rstd = norm_parts(x)

    @pl.when(step == 0)
    def _():
        small_ref[...] = jnp.zeros_like(small_ref)
        gtable_ref[...] = jnp.zeros_like(gtable_ref)

    small_ref[0] += fold_rows(d_act * unit)
    small_ref[1] += fold_rows(d_act)
    g = d_mid.astype(F32) + norm_back(unit, rstd, gain_ref[0:1], d_act)
    gin_ref[0] = g
    total = jnp.sum(g, axis=0, keepdims=True)
    rows = lax.broadcasted_iota(jnp.int32, gtable_ref.shape, 0)
    gtable_ref[...] += jnp.where(rows == action, total, 0.0)


def run_spatial_input(offset, actions, tok, both, d_qkv, table, gain, w_qkv, filled):
    total, patch, width = tok.shape
    frames, clips, part, _ = both.shape
    clips //= 2
    later = lambda c: (c + offset, 0, 0)
    inputs = (actions, tok, both, d_qkv, table, gain, w_qkv)
    return pl.pallas_call(
        functools.partial(spatial_input, offset),
        grid=(clips,),
        in_specs=[
            pl.BlockSpec(memory_space=SMEM),
            pl.BlockSpec((1, patch, width), later),
            pl.BlockSpec((frames, 1, part, width), lambda c: (0, c, 0, 0)),
            pl.BlockSpec((1, patch, 3 * width), later),
            resident(table.shape), resident(gain.shape), resident(w_qkv.shape),
        ]
        + [pl.BlockSpec(memory_space=pl.ANY)] * len(filled),
        out_specs=[pl.BlockSpec((1, patch, width), later), resident((2, 8, width)), resident(table.shape)],
        out_shape=[
            jax.ShapeDtypeStruct((total, patch, width), F32),
            jax.ShapeDtypeStruct((2, 8, width), F32),
            jax.ShapeDtypeStruct(table.shape, F32),
        ],
        input_output_aliases={len(inputs) + i: i for i in range(len(filled))},
        compiler_params=params(),
        cost_estimate=cost(clips * patch * width * width * 6, 4 * clips * MIB),
        name="spatial_input",
    )(*inputs, *filled)


def run_spatial_backward(offset, total, both, qkv, low, w_o, filled):
    clips, patch, width = qkv.shape
    width //= 3
    frames, _, part, _ = both.shape
    row = lambda c: (c, 0, 0)
    later = lambda c: (c + offset, 0, 0)
    inputs = (both, both, qkv, low, w_o)
    return pl.pallas_call(
        spatial_backward,
        grid=(clips,),
        in_specs=[
            pl.BlockSpec((frames, 1, part, width), lambda c: (0, c, 0, 0)),
            pl.BlockSpec((frames, 1, part, width), lambda c: (0, c + clips, 0, 0)),
            pl.BlockSpec((1, patch, 3 * width), row),
            pl.BlockSpec((1, HEADS // 2, patch, 2 * patch), lambda c: (c, 0, 0, 0)),
            resident(w_o.shape),
        ]
        + [pl.BlockSpec(memory_space=pl.ANY)] * len(filled),
        out_specs=[pl.BlockSpec((1, patch, 3 * width), later), pl.BlockSpec((1, patch, width), later)],
        out_shape=[
            jax.ShapeDtypeStruct((total, patch, 3 * width), BF),
            jax.ShapeDtypeStruct((total, patch, width), BF),
        ],
        input_output_aliases={len(inputs) + i: i for i in range(len(filled))},
        compiler_params=params(),
        cost_estimate=cost(clips * patch * width * width * 8, 5 * clips * MIB),
        name="spatial_backward",
    )(*inputs, *filled)


def choose(core, first, second, keep_ref, send_ref, at):
    for k in range(first.shape[1] // 128):
        cols = slice(k * 128, (k + 1) * 128)
        keep_ref[at, k] = jnp.where(core == 0, first[:, cols], second[:, cols]).astype(BF)
        send_ref[at, k] = jnp.where(core == 0, second[:, cols], first[:, cols]).astype(BF)


def ffn_grads(core_ref, a_ref, b_ref, c_ref, d_ref, keep_ref, send_ref):
    choose(
        core_ref[0], dot_tn(a_ref[...], b_ref[...]), dot_tn(c_ref[...], d_ref[...]), keep_ref, send_ref, 0
    )


def run_ffn_grads(core, act3, d_pre, hid, d_down):
    total, width = act3.shape
    count = d_pre.shape[1] // width
    wide = pl.BlockSpec((total, width), lambda j: (0, j))
    out = pl.BlockSpec((1, width // 128, width, 128), lambda j: (j, 0, 0, 0))
    return pl.pallas_call(
        ffn_grads,
        grid=(count,),
        in_specs=[pl.BlockSpec(memory_space=SMEM), resident(act3.shape), wide, wide, resident(d_down.shape)],
        out_specs=[out, out],
        out_shape=[jax.ShapeDtypeStruct((count, width // 128, width, 128), BF)] * 2,
        compiler_params=params(),
        cost_estimate=cost(4 * total * width * width * count, 16 * MIB),
        name="ffn_grads",
    )(core, act3, d_pre, hid, d_down)


def columns(v):
    return jnp.stack([v[:, k * 128 : (k + 1) * 128] for k in range(v.shape[1] // 128)])


def temporal_grads(act_ref, dqkv_ref, out_ref, dproj_ref, grad_ref):
    width = act_ref.shape[1]
    for j in range(3):
        grad_ref[j] = columns(dot_tn(act_ref[...], dqkv_ref[:, j * width : (j + 1) * width]).astype(BF))
    grad_ref[3] = columns(dot_tn(out_ref[...], dproj_ref[...]).astype(BF))


def run_temporal_grads(act, d_qkv, out, d_proj):
    total, width = act.shape
    return pl.pallas_call(
        temporal_grads,
        out_shape=jax.ShapeDtypeStruct((4, width // 128, width, 128), BF),
        compiler_params=params(),
        cost_estimate=cost(8 * total * width * width, 8 * MIB),
        name="temporal_grads",
    )(act, d_qkv, out, d_proj)


def spatial_grads(core_ref, act0_ref, act1_ref, dqkv_ref, other_ref, out0_hbm, out1_hbm, both0_hbm, both1_hbm,
                  keep_ref, send_ref, out_s, mid_s, sems):
    step = pl.program_id(0)
    core = core_ref[0]
    half, n, width = act0_ref.shape
    total = 2 * half * n
    pairs = [
        (out0_hbm, out_s.at[0]), (out1_hbm, out_s.at[1]),
        (both0_hbm.at[:, :half], mid_s.at[0]), (both1_hbm.at[:, :half], mid_s.at[1]),
    ]
    loads = [pltpu.make_async_copy(*p, sems.at[i]) for i, p in enumerate(pairs)]

    def emit(grad):
        grad = columns(grad.astype(BF))
        keep_ref[0] = jnp.where(core == 0, other_ref[0], grad)
        send_ref[0] = jnp.where(core == 0, grad, other_ref[0])

    @pl.when(step == 0)
    def _():
        for load in loads:
            load.start()

    @pl.when(step < 3)
    def _():
        act = jnp.concatenate([act0_ref[...].reshape(-1, width), act1_ref[...].reshape(-1, width)], axis=0)
        emit(dot_tn(act, dqkv_ref[...].reshape(total, width)))

    @pl.when(step == 3)
    def _():
        for load in loads:
            load.wait()
        d_mid = jnp.concatenate([mid_s[i, :, c].reshape(n, width) for i in range(2) for c in range(half)], axis=0)
        emit(dot_tn(out_s[...].reshape(total, width), d_mid))


def run_spatial_grads(core, act0, act1, d_qkv, out0, out1, both0, both1, other):
    half, n, width = act0.shape
    frames, _, part, _ = both0.shape
    block = pl.BlockSpec((1, *other.shape[1:]), lambda j: (j, 0, 0, 0))
    return pl.pallas_call(
        spatial_grads,
        grid=(4,),
        in_specs=[
            pl.BlockSpec(memory_space=SMEM), resident(act0.shape), resident(act1.shape),
            pl.BlockSpec((2 * half, n, width), lambda j: (0, 0, jnp.minimum(j, 2))), block,
        ]
        + [pl.BlockSpec(memory_space=pl.ANY)] * 4,
        out_specs=[block, block],
        out_shape=[jax.ShapeDtypeStruct(other.shape, BF)] * 2,
        scratch_shapes=[
            pltpu.VMEM((2, half, n, width), BF), pltpu.VMEM((2, frames, half, part, width), BF),
            pltpu.SemaphoreType.DMA((4,)),
        ],
        compiler_params=params(),
        cost_estimate=cost(8 * 1024 * width * width, 8 * MIB),
        name="spatial_grads",
    )(core, act0, act1, d_qkv, other, out0, out1, both0, both1)


def pack_small(sb0_ref, sb1_ref, ub0_ref, ub1_ref, sc0_ref, sc1_ref, gt0_ref, gt1_ref, sums_ref):
    width = gt0_ref.shape[1]
    fold = lambda v: jnp.sum(v, axis=-2, keepdims=True)
    sb = fold(sb0_ref[...] + sb1_ref[...])
    sc = fold(sc0_ref[...] + sc1_ref[...])
    ub = fold(ub0_ref[...] + ub1_ref[...])
    table = gt0_ref[...] + gt1_ref[...]
    norms = jnp.concatenate([sc[0], sb[2], sb[0], sc[1], sb[3], sb[1], jnp.zeros((2, width), F32)], axis=0)
    cut = lambda v: [v[:, k * 128 : (k + 1) * 128] for k in range(v.shape[1] // 128)]
    rows = jnp.concatenate(cut(table) + cut(norms) + cut(ub), axis=0)
    sums_ref[...] = rows


def run_pack_small(*arrays):
    return pl.pallas_call(
        pack_small,
        out_shape=jax.ShapeDtypeStruct((80, 128), F32),
        compiler_params=params(),
        cost_estimate=cost(2**33, 64 * MIB),
        name="pack_small",
    )(*arrays)


def unpack(main_ref, up_ref, down_ref, tqkv_ref, to_ref, sqkv_ref, so_ref,
           table_ref, gain_ref, bias_ref, ub_ref):
    step = pl.program_id(0)
    width = to_ref.shape[0]
    group = main_ref.shape[0] // 4
    chips = pl.ds((step % 4) * group, group)
    exps = main_ref[chips, :, 336:352].astype(F32)
    sides = []
    for c in range(2):
        e = jnp.where(step < 4, exps[:, c, 0:1], exps[:, c, 1:2])
        sides.append((main_ref[chips, c, pl.ds((step // 4) * 128, 128)].astype(F32) * jnp.exp2(e)).reshape(-1, 128))

    def put(ref, v):
        for k in range(width // 128):
            ref[:, k * 128 : (k + 1) * 128] = v[k * width : (k + 1) * width]

    @pl.when(step == 0)
    def _():
        every = main_ref[:, :, 336:352].astype(F32)

        def total(start, stop, row):
            terms = main_ref[:, :, start:stop].astype(F32) * jnp.exp2(every[:, :, row : row + 1])
            return jnp.sum(jnp.sum(terms, axis=1), axis=0)

        rows = jnp.concatenate([total(256, 288, 2), total(288, 320, 3), total(320, 336, 4)], axis=0)
        for k in range(width // 128):
            cols = slice(k * 128, (k + 1) * 128)
            table_ref[:, cols] = rows[8 * k : 8 * k + 8]
            gain_ref[:, cols] = rows[32 + 8 * k : 35 + 8 * k]
            bias_ref[:, cols] = rows[35 + 8 * k : 38 + 8 * k]
        for k in range(ub_ref.shape[1] // 128):
            ub_ref[:, k * 128 : (k + 1) * 128] = rows[64 + k : 65 + k]

    @pl.when(step < 4)
    def _():
        put(up_ref, sides[0])
        put(down_ref, sides[1])

    @pl.when((step >= 4) & (step < 7))
    def _():
        put(tqkv_ref, sides[0])
        put(sqkv_ref, sides[1])

    @pl.when(step == 7)
    def _():
        put(to_ref, sides[0])
        put(so_ref, sides[1])


def run_unpack(whole, width):
    up = lambda j: (0, jnp.minimum(j, 3))
    down = lambda j: (jnp.minimum(j, 3), 0)
    third = lambda j: (0, jnp.clip(j - 4, 0, 2))
    square = (width, width)
    outs = [(width, 4 * width), (4 * width, width)] + [(width, 3 * width), square] * 2
    outs += [(8, width), (3, width), (3, width), (1, 4 * width)]
    return pl.pallas_call(
        unpack,
        grid=(8,),
        in_specs=[
            pl.BlockSpec(memory_space=pltpu.VMEM),
        ],
        out_specs=[
            pl.BlockSpec(square, up), pl.BlockSpec(square, down),
            pl.BlockSpec(square, third), resident(square), pl.BlockSpec(square, third), resident(square),
        ]
        + [resident(s) for s in outs[6:]],
        out_shape=[jax.ShapeDtypeStruct(s, F32) for s in outs],
        compiler_params=params(36),
        cost_estimate=cost(MIB, 24 * MIB),
        name="unpack",
    )(whole)


def swap_cores(v):
    return lax.ppermute(v, "c", [(0, 1), (1, 0)])


def after(v, *done):
    return lax.optimization_barrier((v, *done))[0]


def over_frames(v):
    return lax.all_to_all(v, FRAME_AXES, 0, 0)


def over_chips(v):
    return lax.all_to_all(v, CHIP_AXES, 0, 0)


def add_parts(parts):
    return jnp.sum(parts.astype(F32), axis=0)


def add_core(keep, send, *done):
    got = after(swap_cores(send), *done)
    return (keep.astype(F32) + got.astype(F32)).astype(BF)


def exponent(v, axes):
    most = jnp.max(jnp.abs(v), axis=axes, keepdims=True)
    return jnp.clip(jnp.ceil(jnp.log2(jnp.maximum(most, 1e-37))), -120.0, 120.0)


def scaled(v, axes):
    e = exponent(v, axes)
    return (v * jnp.exp2(-e)).astype(F16), jnp.broadcast_to(e, (e.shape[0], 128)).astype(F16)


def shards(
    frame_tokens, actions, frame_counts, action_table, ln_gain, ln_bias, w_sqkv, w_so, w_tqkv, w_to,
    w_up, b_up, w_down, cotangent,
):
    clips, _, patch, width = frame_tokens.shape
    frames = lax.axis_size(FRAME_AXES)
    chips = lax.axis_size(CHIP_AXES)
    core = lax.axis_index("c").astype(jnp.int32).reshape(1)
    tok = frame_tokens[:, 0]
    acts = actions[:, 0]
    half = clips // 2
    forward = [
        run_spatial_forward(
            frames, i * half, half, acts, tok, cotangent[:, 0], action_table, ln_gain, ln_bias, w_sqkv, w_so
        )
        for i in range(2)
    ]
    there0 = over_frames(forward[0][0])
    there1 = over_frames(after(forward[1][0], there0))
    back = (ln_gain, ln_bias, b_up[None], w_tqkv, w_to, w_up, w_down)
    first = run_temporal(0, clips, frame_counts, there0, *back, ())
    second = run_temporal(half, clips, frame_counts, there1, *back, first[1:9])
    both0 = over_frames(after(first[0], there1))
    both1 = over_frames(after(second[0], both0))
    act_two, d_tqkv, t_out, d_tproj, act_three, d_pre, hidden, d_down = second[1:9]
    lines = lambda v: v.reshape(chips, -1, 128)
    keep, send = run_ffn_grads(core, after(act_three, both0), d_pre, hidden, d_down)
    ffn = add_core(keep, after(send, both1))
    temporal_part = run_temporal_grads(act_two, d_tqkv, t_out, d_tproj)
    ffn_part = add_parts(over_chips(after(lines(ffn), both1, temporal_part)))

    d_sqkv, block_out = run_spatial_backward(
        half, clips, both1, forward[1][1], forward[1][2], w_so,
        run_spatial_backward(0, clips, both0, forward[0][1], forward[0][2], w_so, ()),
    )
    keep, send = run_spatial_grads(
        core, forward[0][4], forward[1][4], d_sqkv, forward[0][3], forward[1][3], both0, both1, temporal_part
    )
    ffn_rows, ffn_exp = scaled(ffn_part, (0, 1))
    late_rows, late_exp = scaled(add_parts(over_chips(lines(add_core(keep, send, ffn_rows)))), (0, 1))
    low = (action_table, ln_gain, w_sqkv)
    in0 = run_spatial_input(0, acts, tok, both0, d_sqkv, *low, ())
    in1 = run_spatial_input(half, acts, tok, both1, d_sqkv, *low, in0[:1])
    grad_input = in1[0]
    sums = run_pack_small(first[9], second[9], first[10], second[10], in0[1], in1[1], in0[2], in1[2])
    own = [scaled(v, (0, 1)) for v in (sums[:32], sums[32:64], sums[64:])]
    fill = jnp.zeros((11, 128), F16)
    mine = jnp.concatenate(
        [ffn_rows, late_rows, *(v for v, _ in own), ffn_exp, late_exp, *(e for _, e in own), fill], axis=0
    )
    whole = lax.all_gather(mine, (*CHIP_AXES, "c"), axis=0, tiled=True).reshape(chips, 2, -1, 128)
    (grad_up, grad_down, grad_tqkv, grad_to, grad_sqkv, grad_so, grad_table, grad_gain, grad_bias, up_bias) = (
        run_unpack(whole.astype(BF), width)
    )
    return (
        block_out[:, None],
        grad_input[:, None],
        grad_table,
        grad_gain,
        grad_bias,
        grad_sqkv,
        grad_so,
        grad_tqkv,
        grad_to,
        grad_up,
        up_bias.reshape(-1),
        grad_down,
    )


def solution(mesh):
    fine = Mesh(mesh.devices.reshape(4, 2, 2, 4, 2), ("x", "zh", "zl", "y", "c"))
    clip = ("zl", "y", "c")
    tokens = P(clip, FRAME_AXES, None, None)
    in_specs = (tokens, P(clip, FRAME_AXES), P(clip)) + (P(),) * 10 + (tokens,)
    out_specs = (tokens, tokens) + (P(),) * 10
    return jax.shard_map(shards, mesh=fine, in_specs=in_specs, out_specs=out_specs, check_vma=False)
```

```python
import functools
import math

import jax
import jax.numpy as jnp
from jax import lax
from jax.experimental import pallas as pl
from jax.experimental.pallas import tpu as pltpu
from jax.sharding import Mesh, PartitionSpec as P

HEADS = 8
EPS = 1e-05
NEG = -1e30
BF = jnp.bfloat16
F32 = jnp.float32
F16 = jnp.float16
FRAME_AXES = ("x", "zh")
CHIP_AXES = ("x", "zh", "zl", "y")
MIB = 1 << 20
SMEM = pltpu.SMEM


def dot(a, b):
    return jnp.dot(a, b, preferred_element_type=F32)


def dot_nt(a, b):
    return lax.dot_general(a, b, (((1,), (1,)), ((), ())), preferred_element_type=F32)


def dot_tn(a, b):
    return lax.dot_general(a, b, (((0,), (0,)), ((), ())), preferred_element_type=F32)


def norm_parts(v):
    center = v - jnp.mean(v, axis=-1, keepdims=True)
    rstd = lax.rsqrt(jnp.mean(center * center, axis=-1, keepdims=True) + EPS)
    return center * rstd, rstd


def norm_back(unit, rstd, gain, up):
    d_unit = up * gain
    mean_a = jnp.mean(d_unit, axis=-1, keepdims=True)
    mean_b = jnp.mean(d_unit * unit, axis=-1, keepdims=True)
    return rstd * (d_unit - mean_a - unit * mean_b)


def fold_rows(v):
    return jnp.sum(v.reshape(-1, 8, v.shape[-1]), axis=0)


def head_masks(scale):
    lane = lax.broadcasted_iota(jnp.int32, (1, 128), 1)
    first = jnp.where(lane < 64, scale, 0.0).astype(BF)
    second = jnp.where(lane < 64, 0.0, scale).astype(BF)
    return first, second


def split_heads(v, masks):
    return jnp.concatenate([v * masks[0], v * masks[1]], axis=0)


def softmax(s):
    e = jnp.exp(s - jnp.max(s, axis=-1, keepdims=True))
    return e * (1.0 / jnp.sum(e, axis=-1, keepdims=True))


def pick_heads(v):
    half = v.shape[0] // 2
    lane = lax.broadcasted_iota(jnp.int32, (half, 128), 1)
    return jnp.where(lane < 64, v[:half], v[half:])


def small_tn(a, b):
    z = dot(a.T, b)
    n = z.shape[1] // 2
    return jnp.concatenate([z[:64, :n], z[64:, n:]], axis=0).T


def embed(tok_ref, table_ref, action):
    table = table_ref[...].astype(F32)
    rows = lax.broadcasted_iota(jnp.int32, table.shape, 0)
    row = jnp.sum(jnp.where(rows == action, table, 0.0), axis=0, keepdims=True)
    return tok_ref[0].astype(F32) + row


def spatial_forward(offset, actions_ref, table_ref, gain_ref, bias_ref, tok_hbm, cot_hbm, wqkv_hbm, wo_hbm,
                    both_hbm, qkv_hbm, low_hbm, out_hbm, act_hbm,
                    tok_ref, cot_ref, wqkv_ref, wo_ref, both_ref, qkv_ref, low_ref, out_ref, act_ref,
                    in_sems, out_sems):
    clips, n, width = tok_ref.shape
    frames, _, part, _ = both_ref.shape
    mine = pl.ds(offset, clips)
    pairs = [(tok_hbm.at[mine], tok_ref), (wqkv_hbm, wqkv_ref), (cot_hbm.at[mine], cot_ref), (wo_hbm, wo_ref)]
    loads = [pltpu.make_async_copy(*p, in_sems.at[i]) for i, p in enumerate(pairs)]
    for load in loads:
        load.start()
    stores = []

    def store(source, target):
        c = pltpu.make_async_copy(source, target, out_sems.at[len(stores)])
        c.start()
        stores.append(c)

    loads[0].wait()
    x = jnp.concatenate(
        [embed(tok_ref.at[pl.ds(c, 1)], table_ref, actions_ref[offset + c]) for c in range(clips)], axis=0
    )
    unit, _ = norm_parts(x)
    act = (unit * gain_ref[0:1] + bias_ref[0:1]).astype(BF)
    act_ref[...] = act.reshape(act_ref.shape)
    store(act_ref, act_hbm)
    loads[1].wait()
    qkv_ref[...] = dot(act, wqkv_ref[...]).astype(BF).reshape(qkv_ref.shape)
    store(qkv_ref, qkv_hbm)
    loads[2].wait()
    for c in range(clips):
        both_ref[:, clips + c] = cot_ref[c].reshape(frames, part, width)
    store(both_ref.at[:, clips:], both_hbm.at[:, clips:])
    scaled = head_masks(1.0 / math.sqrt(width // HEADS))
    plain = head_masks(1.0)
    for c in range(clips):
        for pair in range(HEADS // 2):
            lo = pair * 128
            query = qkv_ref[c, :, lo : lo + 128]
            key = qkv_ref[c, :, width + lo : width + lo + 128]
            value = qkv_ref[c, :, 2 * width + lo : 2 * width + lo + 128]
            s = dot_nt(query, split_heads(key, scaled))
            low_ref[c, pair, :, :n] = softmax(s[:, :n]).astype(BF)
            low_ref[c, pair, :, n:] = softmax(s[:, n:]).astype(BF)
            out_ref[c, :, lo : lo + 128] = dot(low_ref[c, pair], split_heads(value, plain)).astype(BF)
        store(low_ref.at[c], low_hbm.at[c])
    store(out_ref, out_hbm)
    loads[3].wait()
    mid = (x + dot(out_ref[...].reshape(clips * n, width), wo_ref[...])).astype(BF)
    for c in range(clips):
        both_ref[:, c] = mid[c * n : (c + 1) * n].reshape(frames, part, width)
    store(both_ref.at[:, :clips], both_hbm.at[:, :clips])
    for c in stores:
        c.wait()


def resident(shape):
    return pl.BlockSpec(shape, lambda *_: (0,) * len(shape), pipeline_mode=pl.Buffered(1))


def params(mib=56):
    return pltpu.CompilerParams(vmem_limit_bytes=mib * MIB)


def cost(flops, nbytes):
    return pl.CostEstimate(flops=int(flops), bytes_accessed=int(nbytes), transcendentals=0)


def run_spatial_forward(frames, offset, clips, actions, tok, cot, table, gain, bias, w_qkv, w_o):
    _, patch, width = tok.shape
    part = patch // frames
    hbm = pl.BlockSpec(memory_space=pl.ANY)
    vmem = pl.BlockSpec(memory_space=pltpu.VMEM)
    rows = (clips, patch, width)
    outs = [
        (frames, 2 * clips, part, width), (clips, patch, 3 * width), (clips, HEADS // 2, patch, 2 * patch), rows, rows,
    ]
    return pl.pallas_call(
        functools.partial(spatial_forward, offset),
        in_specs=[pl.BlockSpec(memory_space=SMEM)] + [vmem] * 3 + [hbm] * 4,
        out_specs=[hbm] * 5,
        out_shape=[jax.ShapeDtypeStruct(o, BF) for o in outs],
        scratch_shapes=[pltpu.VMEM(v, BF) for v in (rows, rows, w_qkv.shape, w_o.shape, *outs)]
        + [pltpu.SemaphoreType.DMA((4,)), pltpu.SemaphoreType.DMA((5 + clips,))],
        compiler_params=params(),
        cost_estimate=cost(clips * patch * width * width * 10, 4 * clips * MIB),
        name="spatial_forward",
    )(actions, table, gain, bias, tok, cot, w_qkv, w_o)


def rows_of(ref, clip, half, part):
    v = ref[:, clip, half * part : (half + 1) * part, :]
    return v.reshape(-1, v.shape[-1])


def load_rows(ref, clips, part):
    return jnp.concatenate(
        [rows_of(ref, c, h, part) for c in range(clips) for h in range(2)], axis=0
    )


def store_rows(ref, v, first, clips, part):
    frames = ref.shape[0]
    block = frames * part
    for c in range(clips):
        for h in range(2):
            at = (2 * c + h) * block
            ref[:, first + c, h * part : (h + 1) * part, :] = v[at : at + block].reshape(frames, part, v.shape[-1])


def temporal(offset, filled, counts_ref, gain_ref, bias_ref, bup_ref, in_hbm, wqkv_hbm, wo_hbm, wup_hbm, wdown_hbm,
             *rest):
    rest = rest[8:] if filled else rest
    both_hbm, *flat_hbm = rest[:9]
    (small_ref, upbias_ref, mid_ref, cot_ref, wqkv_ref, wo_ref, wup_ref, wdown_ref, both_ref, act2_ref, dqkv_ref,
     tout_ref, dproj_ref, act3_ref, dpre_ref, hid_ref, ddown_ref, qkv_s, low_s, dtout_s, in_sems, out_sems) = rest[9:]
    act2_hbm, dqkv_hbm, tout_hbm, dproj_hbm, act3_hbm, dpre_hbm, hid_hbm, ddown_hbm = flat_hbm
    frames, clips, both, width = mid_ref.shape
    pairs = [
        (in_hbm.at[:, :clips], mid_ref), (wqkv_hbm, wqkv_ref), (wo_hbm, wo_ref), (in_hbm.at[:, clips:], cot_ref),
        (wup_hbm, wup_ref), (wdown_hbm, wdown_ref),
    ]
    loads = [pltpu.make_async_copy(*p, in_sems.at[i]) for i, p in enumerate(pairs)]
    for load in loads:
        load.start()
    stores = []
    mine = pl.ds(offset * frames * both, clips * frames * both)

    def store(source, target):
        c = pltpu.make_async_copy(source, target, out_sems.at[len(stores)])
        c.start()
        stores.append(c)

    loads[0].wait()
    part = both // 2
    block = frames * part
    x = load_rows(mid_ref, clips, part).astype(F32)
    rows = x.shape[0]
    unit2, rstd2 = norm_parts(x)
    act2 = (unit2 * gain_ref[1:2] + bias_ref[1:2]).astype(BF)
    act2_ref[...] = act2
    store(act2_ref, act2_hbm.at[mine])
    loads[1].wait()
    qkv_s[...] = dot(act2, wqkv_ref[...]).astype(BF)
    scaled = head_masks(1.0 / math.sqrt(width // HEADS))
    plain = head_masks(1.0)
    r = lax.broadcasted_iota(jnp.int32, (block, block), 0)
    s = lax.broadcasted_iota(jnp.int32, (block, block), 1)
    base = (r % part == s % part) & (s // part <= r // part)
    row_mask = []
    for c in range(clips):
        count = counts_ref[offset + c]
        allowed = base & (s // part < count)
        row_mask.append(count)
        for h in range(2):
            b = 2 * c + h
            at = slice(b * block, (b + 1) * block)
            for pair in range(HEADS // 2):
                lo = pair * 128
                query = qkv_s[at, lo : lo + 128]
                key = qkv_s[at, width + lo : width + lo + 128]
                value = qkv_s[at, 2 * width + lo : 2 * width + lo + 128]
                scores = dot_nt(query, split_heads(key, scaled))
                for k in range(2):
                    sc = jnp.where(allowed, scores[:, k * block : (k + 1) * block], NEG)
                    low_s[b, pair, :, k * block : (k + 1) * block] = softmax(sc).astype(BF)
                tout_ref[at, lo : lo + 128] = dot(low_s[b, pair], split_heads(value, plain)).astype(BF)
    store(tout_ref, tout_hbm.at[mine])
    loads[2].wait()
    late = x + dot(tout_ref[...], wo_ref[...])
    unit3, rstd3 = norm_parts(late)
    act3 = (unit3 * gain_ref[2:3] + bias_ref[2:3]).astype(BF)
    act3_ref[...] = act3
    store(act3_ref, act3_hbm.at[mine])
    loads[3].wait()
    frame_of = lax.broadcasted_iota(jnp.int32, (block, width), 0) // part
    d_out = load_rows(cot_ref, clips, part)
    d_out = jnp.concatenate(
        [
            jnp.where(frame_of < row_mask[b // 2], d_out[b * block : (b + 1) * block].astype(F32), 0.0)
            for b in range(2 * clips)
        ],
        axis=0,
    )
    d_down = d_out.astype(BF)
    ddown_ref[...] = d_down
    store(ddown_ref, ddown_hbm.at[mine])
    out = late
    d_act3 = None
    loads[4].wait()
    loads[5].wait()
    k0 = math.sqrt(2.0 / math.pi)
    k1 = 0.044715
    for j in range(2):
        cols = slice(j * 2 * width, (j + 1) * 2 * width)
        u = dot(act3, wup_ref[:, cols]) + bup_ref[0:1, cols]
        sq = u * u
        t = jnp.tanh(k0 * u * (1.0 + k1 * sq))
        half_t = 0.5 + 0.5 * t
        hid = (u * half_t).astype(BF)
        slope = half_t + 0.5 * u * (1.0 - t * t) * (k0 + (3.0 * k0 * k1) * sq)
        hid_ref[:, cols] = hid
        store(hid_ref.at[:, cols], hid_hbm.at[mine, cols])
        out = out + dot(hid, wdown_ref[cols, :])
        d_pre32 = dot_nt(d_down, wdown_ref[cols, :]) * slope
        d_pre = d_pre32.astype(BF)
        dpre_ref[:, cols] = d_pre
        store(dpre_ref.at[:, cols], dpre_hbm.at[mine, cols])
        upbias_ref[:, cols] = fold_rows(d_pre.astype(F32))
        more = dot_nt(d_pre, wup_ref[:, cols])
        d_act3 = more if d_act3 is None else d_act3 + more
    store_rows(both_ref, out.astype(BF), clips, clips, part)
    store(both_ref.at[:, clips:], both_hbm.at[:, clips:])
    small_ref[0] = fold_rows(d_act3 * unit3)
    small_ref[1] = fold_rows(d_act3)
    d_late = d_out + norm_back(unit3, rstd3, gain_ref[2:3], d_act3)
    d_proj = d_late.astype(BF)
    dproj_ref[...] = d_proj
    store(dproj_ref, dproj_hbm.at[mine])
    dtout_s[...] = dot_nt(d_proj, wo_ref[...]).astype(BF)
    for b in range(2 * clips):
        at = slice(b * block, (b + 1) * block)
        for pair in range(HEADS // 2):
            lo = pair * 128
            query = qkv_s[at, lo : lo + 128]
            key = qkv_s[at, width + lo : width + lo + 128]
            value = qkv_s[at, 2 * width + lo : 2 * width + lo + 128]
            d_o = dtout_s[at, lo : lo + 128]
            d_p = dot_nt(d_o, split_heads(value, plain))
            low = low_s[b, pair]
            ds = []
            for k in range(2):
                cols = slice(k * block, (k + 1) * block)
                p = low[:, cols].astype(F32)
                pd = p * d_p[:, cols]
                ds.append((pd - p * jnp.sum(pd, axis=-1, keepdims=True)).astype(BF))
            d_s = jnp.concatenate(ds, axis=1)
            dqkv_ref[at, lo : lo + 128] = dot(d_s, split_heads(key, scaled)).astype(BF)
            d_k = small_tn(query, d_s) * (1.0 / math.sqrt(width // HEADS))
            dqkv_ref[at, width + lo : width + lo + 128] = d_k.astype(BF)
            d_v = small_tn(d_o, low)
            dqkv_ref[at, 2 * width + lo : 2 * width + lo + 128] = d_v.astype(BF)
    store(dqkv_ref, dqkv_hbm.at[mine])
    d_act2 = dot_nt(dqkv_ref[...], wqkv_ref[...])
    small_ref[2] = fold_rows(d_act2 * unit2)
    small_ref[3] = fold_rows(d_act2)
    d_mid = d_late + norm_back(unit2, rstd2, gain_ref[1:2], d_act2)
    store_rows(both_ref, d_mid.astype(BF), 0, clips, part)
    store(both_ref.at[:, :clips], both_hbm.at[:, :clips])
    for c in stores:
        c.wait()


def run_temporal(offset, total_clips, counts, both_in, gain, bias, b_up, w_qkv, w_o, w_up, w_down, filled):
    frames, clips, both, width = both_in.shape
    clips //= 2
    hidden = w_up.shape[1]
    rows = clips * frames * both
    total = total_clips * frames * both
    widths = (width, 3 * width, width, width, width, hidden, hidden, width)
    small = (counts, gain, bias, b_up)
    large = (both_in, w_qkv, w_o, w_up, w_down)
    hbm = pl.BlockSpec(memory_space=pl.ANY)
    vmem = pl.BlockSpec(memory_space=pltpu.VMEM)
    half = (frames, clips, both, width)
    return pl.pallas_call(
        functools.partial(temporal, offset, bool(filled)),
        in_specs=[pl.BlockSpec(memory_space=SMEM)] + [vmem] * 3 + [hbm] * (len(large) + len(filled)),
        out_specs=[hbm] * 9 + [vmem] * 2,
        out_shape=[jax.ShapeDtypeStruct(both_in.shape, BF)]
        + [jax.ShapeDtypeStruct((total, w), BF) for w in widths]
        + [jax.ShapeDtypeStruct((4, 8, width), F32), jax.ShapeDtypeStruct((8, hidden), F32)],
        scratch_shapes=[pltpu.VMEM(half, BF)] * 2
        + [pltpu.VMEM(w.shape, BF) for w in large[1:]]
        + [pltpu.VMEM(both_in.shape, BF)]
        + [pltpu.VMEM((rows, w), BF) for w in widths]
        + [
            pltpu.VMEM((rows, 3 * width), BF),
            pltpu.VMEM((2 * clips, HEADS // 2, rows // (2 * clips), rows // clips), BF),
            pltpu.VMEM((rows, width), BF),
            pltpu.SemaphoreType.DMA((6,)),
            pltpu.SemaphoreType.DMA((12,)),
        ],
        input_output_aliases={len(small) + len(large) + i: 1 + i for i in range(len(filled))},
        compiler_params=params(),
        cost_estimate=cost(clips * frames * both * width * width * 40, 8 * clips * MIB),
        name="temporal",
    )(*small, *large, *filled)


def spatial_backward(dmid_ref, done_ref, qkv_ref, low_ref, wo_ref, *rest):
    dqkv_ref, block_ref = rest[-2:]
    _, n, width = block_ref.shape
    d_mid = dmid_ref[:, 0].reshape(n, width)
    block_ref[0] = done_ref[:, 0].reshape(n, width)
    d_out = dot_nt(d_mid, wo_ref[...]).astype(BF)
    scaled = head_masks(1.0 / math.sqrt(width // HEADS))
    plain = head_masks(1.0)
    for pair in range(HEADS // 2):
        lo = pair * 128
        query = qkv_ref[0, :, lo : lo + 128]
        key = qkv_ref[0, :, width + lo : width + lo + 128]
        value = qkv_ref[0, :, 2 * width + lo : 2 * width + lo + 128]
        d_o = d_out[:, lo : lo + 128]
        d_p = dot_nt(d_o, split_heads(value, plain))
        low = low_ref[0, pair]
        ds = []
        for k in range(2):
            cols = slice(k * n, (k + 1) * n)
            p = low[:, cols].astype(F32)
            pd = p * d_p[:, cols]
            ds.append((pd - p * jnp.sum(pd, axis=-1, keepdims=True)).astype(BF))
        d_s = jnp.concatenate(ds, axis=1)
        dqkv_ref[0, :, lo : lo + 128] = dot(d_s, split_heads(key, scaled)).astype(BF)
        d_k = small_tn(query, d_s) * (1.0 / math.sqrt(width // HEADS))
        dqkv_ref[0, :, width + lo : width + lo + 128] = d_k.astype(BF)
        dqkv_ref[0, :, 2 * width + lo : 2 * width + lo + 128] = small_tn(d_o, low).astype(BF)


def spatial_input(offset, actions_ref, tok_ref, dmid_ref, dqkv_ref, table_ref, gain_ref, wqkv_ref, *rest):
    gin_ref, small_ref, gtable_ref = rest[-3:]
    step = pl.program_id(0)
    action = actions_ref[offset + step]
    x = embed(tok_ref, table_ref, action)
    n, width = x.shape
    d_mid = dmid_ref[:, 0].reshape(n, width)
    d_act = dot_nt(dqkv_ref[0], wqkv_ref[...])
    unit, rstd = norm_parts(x)

    @pl.when(step == 0)
    def _():
        small_ref[...] = jnp.zeros_like(small_ref)
        gtable_ref[...] = jnp.zeros_like(gtable_ref)

    small_ref[0] += fold_rows(d_act * unit)
    small_ref[1] += fold_rows(d_act)
    g = d_mid.astype(F32) + norm_back(unit, rstd, gain_ref[0:1], d_act)
    gin_ref[0] = g
    total = jnp.sum(g, axis=0, keepdims=True)
    rows = lax.broadcasted_iota(jnp.int32, gtable_ref.shape, 0)
    gtable_ref[...] += jnp.where(rows == action, total, 0.0)


def run_spatial_input(offset, actions, tok, both, d_qkv, table, gain, w_qkv, filled):
    total, patch, width = tok.shape
    frames, clips, part, _ = both.shape
    clips //= 2
    later = lambda c: (c + offset, 0, 0)
    inputs = (actions, tok, both, d_qkv, table, gain, w_qkv)
    return pl.pallas_call(
        functools.partial(spatial_input, offset),
        grid=(clips,),
        in_specs=[
            pl.BlockSpec(memory_space=SMEM),
            pl.BlockSpec((1, patch, width), later),
            pl.BlockSpec((frames, 1, part, width), lambda c: (0, c, 0, 0)),
            pl.BlockSpec((1, patch, 3 * width), later),
            resident(table.shape), resident(gain.shape), resident(w_qkv.shape),
        ]
        + [pl.BlockSpec(memory_space=pl.ANY)] * len(filled),
        out_specs=[pl.BlockSpec((1, patch, width), later), resident((2, 8, width)), resident(table.shape)],
        out_shape=[
            jax.ShapeDtypeStruct((total, patch, width), F32),
            jax.ShapeDtypeStruct((2, 8, width), F32),
            jax.ShapeDtypeStruct(table.shape, F32),
        ],
        input_output_aliases={len(inputs) + i: i for i in range(len(filled))},
        compiler_params=params(),
        cost_estimate=cost(clips * patch * width * width * 6, 4 * clips * MIB),
        name="spatial_input",
    )(*inputs, *filled)


def run_spatial_backward(offset, total, both, qkv, low, w_o, filled):
    clips, patch, width = qkv.shape
    width //= 3
    frames, _, part, _ = both.shape
    row = lambda c: (c, 0, 0)
    later = lambda c: (c + offset, 0, 0)
    inputs = (both, both, qkv, low, w_o)
    return pl.pallas_call(
        spatial_backward,
        grid=(clips,),
        in_specs=[
            pl.BlockSpec((frames, 1, part, width), lambda c: (0, c, 0, 0)),
            pl.BlockSpec((frames, 1, part, width), lambda c: (0, c + clips, 0, 0)),
            pl.BlockSpec((1, patch, 3 * width), row),
            pl.BlockSpec((1, HEADS // 2, patch, 2 * patch), lambda c: (c, 0, 0, 0)),
            resident(w_o.shape),
        ]
        + [pl.BlockSpec(memory_space=pl.ANY)] * len(filled),
        out_specs=[pl.BlockSpec((1, patch, 3 * width), later), pl.BlockSpec((1, patch, width), later)],
        out_shape=[
            jax.ShapeDtypeStruct((total, patch, 3 * width), BF),
            jax.ShapeDtypeStruct((total, patch, width), BF),
        ],
        input_output_aliases={len(inputs) + i: i for i in range(len(filled))},
        compiler_params=params(),
        cost_estimate=cost(clips * patch * width * width * 8, 5 * clips * MIB),
        name="spatial_backward",
    )(*inputs, *filled)


def choose(core, first, second, keep_ref, send_ref, at):
    for k in range(first.shape[1] // 128):
        cols = slice(k * 128, (k + 1) * 128)
        keep_ref[at, k] = jnp.where(core == 0, first[:, cols], second[:, cols]).astype(BF)
        send_ref[at, k] = jnp.where(core == 0, second[:, cols], first[:, cols]).astype(BF)


def ffn_grads(core_ref, a_ref, b_ref, c_ref, d_ref, keep_ref, send_ref):
    choose(
        core_ref[0], dot_tn(a_ref[...], b_ref[...]), dot_tn(c_ref[...], d_ref[...]), keep_ref, send_ref, 0
    )


def run_ffn_grads(core, act3, d_pre, hid, d_down):
    total, width = act3.shape
    count = d_pre.shape[1] // width
    wide = pl.BlockSpec((total, width), lambda j: (0, j))
    out = pl.BlockSpec((1, width // 128, width, 128), lambda j: (j, 0, 0, 0))
    return pl.pallas_call(
        ffn_grads,
        grid=(count,),
        in_specs=[pl.BlockSpec(memory_space=SMEM), resident(act3.shape), wide, wide, resident(d_down.shape)],
        out_specs=[out, out],
        out_shape=[jax.ShapeDtypeStruct((count, width // 128, width, 128), BF)] * 2,
        compiler_params=params(),
        cost_estimate=cost(4 * total * width * width * count, 16 * MIB),
        name="ffn_grads",
    )(core, act3, d_pre, hid, d_down)


def columns(v):
    return jnp.stack([v[:, k * 128 : (k + 1) * 128] for k in range(v.shape[1] // 128)])


def temporal_grads(act_ref, dqkv_ref, out_ref, dproj_ref, grad_ref):
    width = act_ref.shape[1]
    for j in range(3):
        grad_ref[j] = columns(dot_tn(act_ref[...], dqkv_ref[:, j * width : (j + 1) * width]).astype(BF))
    grad_ref[3] = columns(dot_tn(out_ref[...], dproj_ref[...]).astype(BF))


def run_temporal_grads(act, d_qkv, out, d_proj):
    total, width = act.shape
    return pl.pallas_call(
        temporal_grads,
        out_shape=jax.ShapeDtypeStruct((4, width // 128, width, 128), BF),
        compiler_params=params(),
        cost_estimate=cost(8 * total * width * width, 8 * MIB),
        name="temporal_grads",
    )(act, d_qkv, out, d_proj)


def spatial_grads(core_ref, act0_ref, act1_ref, dqkv_ref, other_ref, out0_hbm, out1_hbm, both0_hbm, both1_hbm,
                  keep_ref, send_ref, out_s, mid_s, sems):
    step = pl.program_id(0)
    core = core_ref[0]
    half, n, width = act0_ref.shape
    total = 2 * half * n
    pairs = [
        (out0_hbm, out_s.at[0]), (out1_hbm, out_s.at[1]),
        (both0_hbm.at[:, :half], mid_s.at[0]), (both1_hbm.at[:, :half], mid_s.at[1]),
    ]
    loads = [pltpu.make_async_copy(*p, sems.at[i]) for i, p in enumerate(pairs)]

    def emit(grad):
        grad = columns(grad.astype(BF))
        keep_ref[0] = jnp.where(core == 0, other_ref[0], grad)
        send_ref[0] = jnp.where(core == 0, grad, other_ref[0])

    @pl.when(step == 0)
    def _():
        for load in loads:
            load.start()

    @pl.when(step < 3)
    def _():
        act = jnp.concatenate([act0_ref[...].reshape(-1, width), act1_ref[...].reshape(-1, width)], axis=0)
        emit(dot_tn(act, dqkv_ref[...].reshape(total, width)))

    @pl.when(step == 3)
    def _():
        for load in loads:
            load.wait()
        d_mid = jnp.concatenate([mid_s[i, :, c].reshape(n, width) for i in range(2) for c in range(half)], axis=0)
        emit(dot_tn(out_s[...].reshape(total, width), d_mid))


def run_spatial_grads(core, act0, act1, d_qkv, out0, out1, both0, both1, other):
    half, n, width = act0.shape
    frames, _, part, _ = both0.shape
    block = pl.BlockSpec((1, *other.shape[1:]), lambda j: (j, 0, 0, 0))
    return pl.pallas_call(
        spatial_grads,
        grid=(4,),
        in_specs=[
            pl.BlockSpec(memory_space=SMEM), resident(act0.shape), resident(act1.shape),
            pl.BlockSpec((2 * half, n, width), lambda j: (0, 0, jnp.minimum(j, 2))), block,
        ]
        + [pl.BlockSpec(memory_space=pl.ANY)] * 4,
        out_specs=[block, block],
        out_shape=[jax.ShapeDtypeStruct(other.shape, BF)] * 2,
        scratch_shapes=[
            pltpu.VMEM((2, half, n, width), BF), pltpu.VMEM((2, frames, half, part, width), BF),
            pltpu.SemaphoreType.DMA((4,)),
        ],
        compiler_params=params(),
        cost_estimate=cost(8 * 1024 * width * width, 8 * MIB),
        name="spatial_grads",
    )(core, act0, act1, d_qkv, other, out0, out1, both0, both1)


def pack_small(sb0_ref, sb1_ref, ub0_ref, ub1_ref, sc0_ref, sc1_ref, gt0_ref, gt1_ref, sums_ref):
    width = gt0_ref.shape[1]
    fold = lambda v: jnp.sum(v, axis=-2, keepdims=True)
    sb = fold(sb0_ref[...] + sb1_ref[...])
    sc = fold(sc0_ref[...] + sc1_ref[...])
    ub = fold(ub0_ref[...] + ub1_ref[...])
    table = gt0_ref[...] + gt1_ref[...]
    norms = jnp.concatenate([sc[0], sb[2], sb[0], sc[1], sb[3], sb[1], jnp.zeros((2, width), F32)], axis=0)
    cut = lambda v: [v[:, k * 128 : (k + 1) * 128] for k in range(v.shape[1] // 128)]
    rows = jnp.concatenate(cut(table) + cut(norms) + cut(ub), axis=0)
    sums_ref[...] = rows


def run_pack_small(*arrays):
    return pl.pallas_call(
        pack_small,
        out_shape=jax.ShapeDtypeStruct((80, 128), F32),
        compiler_params=params(),
        cost_estimate=cost(2**33, 64 * MIB),
        name="pack_small",
    )(*arrays)


def unpack(main_ref, up_ref, down_ref, tqkv_ref, to_ref, sqkv_ref, so_ref,
           table_ref, gain_ref, bias_ref, ub_ref):
    step = pl.program_id(0)
    width = to_ref.shape[0]
    group = main_ref.shape[0] // 4
    chips = pl.ds((step % 4) * group, group)
    exps = main_ref[chips, :, 336:352].astype(F32)
    sides = []
    for c in range(2):
        e = jnp.where(step < 4, exps[:, c, 0:1], exps[:, c, 1:2])
        sides.append((main_ref[chips, c, pl.ds((step // 4) * 128, 128)].astype(F32) * jnp.exp2(e)).reshape(-1, 128))

    def put(ref, v):
        for k in range(width // 128):
            ref[:, k * 128 : (k + 1) * 128] = v[k * width : (k + 1) * width]

    @pl.when(step == 0)
    def _():
        every = main_ref[:, :, 336:352].astype(F32)

        def total(start, stop, row):
            terms = main_ref[:, :, start:stop].astype(F32) * jnp.exp2(every[:, :, row : row + 1])
            return jnp.sum(jnp.sum(terms, axis=1), axis=0)

        rows = jnp.concatenate([total(256, 288, 2), total(288, 320, 3), total(320, 336, 4)], axis=0)
        for k in range(width // 128):
            cols = slice(k * 128, (k + 1) * 128)
            table_ref[:, cols] = rows[8 * k : 8 * k + 8]
            gain_ref[:, cols] = rows[32 + 8 * k : 35 + 8 * k]
            bias_ref[:, cols] = rows[35 + 8 * k : 38 + 8 * k]
        for k in range(ub_ref.shape[1] // 128):
            ub_ref[:, k * 128 : (k + 1) * 128] = rows[64 + k : 65 + k]

    @pl.when(step < 4)
    def _():
        put(up_ref, sides[0])
        put(down_ref, sides[1])

    @pl.when((step >= 4) & (step < 7))
    def _():
        put(tqkv_ref, sides[0])
        put(sqkv_ref, sides[1])

    @pl.when(step == 7)
    def _():
        put(to_ref, sides[0])
        put(so_ref, sides[1])


def run_unpack(whole, width):
    up = lambda j: (0, jnp.minimum(j, 3))
    down = lambda j: (jnp.minimum(j, 3), 0)
    third = lambda j: (0, jnp.clip(j - 4, 0, 2))
    square = (width, width)
    outs = [(width, 4 * width), (4 * width, width)] + [(width, 3 * width), square] * 2
    outs += [(8, width), (3, width), (3, width), (1, 4 * width)]
    return pl.pallas_call(
        unpack,
        grid=(8,),
        in_specs=[
            pl.BlockSpec(memory_space=pltpu.VMEM),
        ],
        out_specs=[
            pl.BlockSpec(square, up), pl.BlockSpec(square, down),
            pl.BlockSpec(square, third), resident(square), pl.BlockSpec(square, third), resident(square),
        ]
        + [resident(s) for s in outs[6:]],
        out_shape=[jax.ShapeDtypeStruct(s, F32) for s in outs],
        compiler_params=params(36),
        cost_estimate=cost(MIB, 24 * MIB),
        name="unpack",
    )(whole)


def swap_cores(v):
    return lax.ppermute(v, "c", [(0, 1), (1, 0)])


def after(v, *done):
    return lax.optimization_barrier((v, *done))[0]


def over_frames(v):
    return lax.all_to_all(v, FRAME_AXES, 0, 0)


def over_chips(v):
    return lax.all_to_all(v, CHIP_AXES, 0, 0)


def add_parts(parts):
    return jnp.sum(parts.astype(F32), axis=0)


def add_core(keep, send, *done):
    got = after(swap_cores(send), *done)
    return (keep.astype(F32) + got.astype(F32)).astype(BF)


def exponent(v, axes):
    most = jnp.max(jnp.abs(v), axis=axes, keepdims=True)
    return jnp.clip(jnp.ceil(jnp.log2(jnp.maximum(most, 1e-37))), -120.0, 120.0)


def scaled(v, axes):
    e = exponent(v, axes)
    return (v * jnp.exp2(-e)).astype(F16), jnp.broadcast_to(e, (e.shape[0], 128)).astype(F16)


def shards(
    frame_tokens, actions, frame_counts, action_table, ln_gain, ln_bias, w_sqkv, w_so, w_tqkv, w_to,
    w_up, b_up, w_down, cotangent,
):
    clips, _, patch, width = frame_tokens.shape
    frames = lax.axis_size(FRAME_AXES)
    chips = lax.axis_size(CHIP_AXES)
    core = lax.axis_index("c").astype(jnp.int32).reshape(1)
    tok = frame_tokens[:, 0]
    acts = actions[:, 0]
    half = clips // 2
    forward = [
        run_spatial_forward(
            frames, i * half, half, acts, tok, cotangent[:, 0], action_table, ln_gain, ln_bias, w_sqkv, w_so
        )
        for i in range(2)
    ]
    there0 = over_frames(forward[0][0])
    there1 = over_frames(after(forward[1][0], there0))
    back = (ln_gain, ln_bias, b_up[None], w_tqkv, w_to, w_up, w_down)
    first = run_temporal(0, clips, frame_counts, there0, *back, ())
    second = run_temporal(half, clips, frame_counts, there1, *back, first[1:9])
    both0 = over_frames(after(first[0], there1))
    both1 = over_frames(after(second[0], both0))
    act_two, d_tqkv, t_out, d_tproj, act_three, d_pre, hidden, d_down = second[1:9]
    lines = lambda v: v.reshape(chips, -1, 128)
    keep, send = run_ffn_grads(core, after(act_three, both0), d_pre, hidden, d_down)
    ffn = add_core(keep, after(send, both1))
    temporal_part = run_temporal_grads(act_two, d_tqkv, t_out, d_tproj)
    ffn_part = add_parts(over_chips(after(lines(ffn), both1, temporal_part)))

    d_sqkv, block_out = run_spatial_backward(
        half, clips, both1, forward[1][1], forward[1][2], w_so,
        run_spatial_backward(0, clips, both0, forward[0][1], forward[0][2], w_so, ()),
    )
    keep, send = run_spatial_grads(
        core, forward[0][4], forward[1][4], d_sqkv, forward[0][3], forward[1][3], both0, both1, temporal_part
    )
    ffn_rows, ffn_exp = scaled(ffn_part, (0, 1))
    late_rows, late_exp = scaled(add_parts(over_chips(lines(add_core(keep, send, ffn_rows)))), (0, 1))
    low = (action_table, ln_gain, w_sqkv)
    in0 = run_spatial_input(0, acts, tok, both0, d_sqkv, *low, ())
    in1 = run_spatial_input(half, acts, tok, both1, d_sqkv, *low, in0[:1])
    grad_input = in1[0]
    sums = run_pack_small(first[9], second[9], first[10], second[10], in0[1], in1[1], in0[2], in1[2])
    own = [scaled(v, (0, 1)) for v in (sums[:32], sums[32:64], sums[64:])]
    fill = jnp.zeros((11, 128), F16)
    mine = jnp.concatenate(
        [ffn_rows, late_rows, *(v for v, _ in own), ffn_exp, late_exp, *(e for _, e in own), fill], axis=0
    )
    whole = lax.all_gather(mine, (*CHIP_AXES, "c"), axis=0, tiled=True).reshape(chips, 2, -1, 128)
    (grad_up, grad_down, grad_tqkv, grad_to, grad_sqkv, grad_so, grad_table, grad_gain, grad_bias, up_bias) = (
        run_unpack(whole.astype(BF), width)
    )
    return (
        block_out[:, None],
        grad_input[:, None],
        grad_table,
        grad_gain,
        grad_bias,
        grad_sqkv,
        grad_so,
        grad_tqkv,
        grad_to,
        grad_up,
        up_bias.reshape(-1),
        grad_down,
    )


def solution(mesh):
    fine = Mesh(mesh.devices.reshape(4, 2, 2, 4, 2), ("x", "zh", "zl", "y", "c"))
    clip = ("zl", "y", "c")
    tokens = P(clip, FRAME_AXES, None, None)
    in_specs = (tokens, P(clip, FRAME_AXES), P(clip)) + (P(),) * 10 + (tokens,)
    out_specs = (tokens, tokens) + (P(),) * 10
    return jax.shard_map(shards, mesh=fine, in_specs=in_specs, out_specs=out_specs, check_vma=False)
```
